32 devices in a mesh: dp: 2 (over y), fsdp: 16 (over z, x, core).
Axes of the slice: x: 2, y: 2, z: 4, core: 2. Of those that a mesh axis runs over, the one named last changes fastest.
Arguments:
- video: bfloat16 [32, 512, 3072], P(('dp', 'fsdp'))
- audio: bfloat16 [32, 1024, 128], P(('dp', 'fsdp'))
- word_ids: int32 [32, 3, 32], P(('dp', 'fsdp')), may hold values from 0 to 65535
- word_counts: int32 [32, 3], P(('dp', 'fsdp')), may hold values from 4 to 32
- caption_counts: int32 [32], P(('dp', 'fsdp')), may hold values from 1 to 3, as said below
- caption_clips: int32 [32, 3], P(('dp', 'fsdp')), may hold values from 0 to 31, as said below
- mixing_in: float32 [3, 768, 6144], P(None, 'fsdp')
- mixing_in_first: float32 [3, 768, 6144], P(None, 'fsdp'), may hold values from -5.0755807e-07 to 5.0755807e-07
- mixing_in_second: float32 [3, 768, 6144], P(None, 'fsdp'), may hold values from 7.052482e-14 to 2.7943796e-13
- mixing_out: float32 [3, 3072, 768], P(None, 'fsdp'), may hold values from -0.109375 to 0.109375
- mixing_out_first: float32 [3, 3072, 768], P(None, 'fsdp'), may hold values from -5.0755807e-07 to 5.0755807e-07
- mixing_out_second: float32 [3, 3072, 768], P(None, 'fsdp'), may hold values from 7.052482e-14 to 2.7943796e-13
- norm_params: float32 [3, 6, 768], P(None, None, 'fsdp')
- norm_params_first: float32 [3, 6, 768], P(None, None, 'fsdp'), may hold values from -2.5377904e-06 to 2.5377904e-06
- norm_params_second: float32 [3, 6, 768], P(None, None, 'fsdp'), may hold values from 1.7298541e-12 to 7.052482e-12
- input_embed: float32 [3200, 768], P('fsdp')
- input_embed_first: float32 [3200, 768], P('fsdp'), may hold values from -5.0755807e-07 to 5.0755807e-07
- input_embed_second: float32 [3200, 768], P('fsdp'), may hold values from 7.052482e-14 to 2.7943796e-13
- word_table: float32 [65536, 768], P('fsdp'), may hold values from -1.8 to 1.8
- word_table_first: float32 [65536, 768], P('fsdp'), may hold values from -5.0755807e-07 to 5.0755807e-07
- word_table_second: float32 [65536, 768], P('fsdp'), may hold values from 7.052482e-14 to 2.7943796e-13
- head_proj: float32 [768, 1280], P('fsdp'), may hold values from -0.21875 to 0.21875
- head_proj_first: float32 [768, 1280], P('fsdp'), may hold values from -5.0755807e-07 to 5.0755807e-07
- head_proj_second: float32 [768, 1280], P('fsdp'), may hold values from 7.052482e-14 to 2.7943796e-13
- video_text_proj: float32 [512, 256], P('fsdp'), may hold values from -0.25 to 0.25
- video_text_proj_first: float32 [512, 256], P('fsdp'), may hold values from -5.0755807e-07 to 5.0755807e-07
- video_text_proj_second: float32 [512, 256], P('fsdp'), may hold values from 7.052482e-14 to 2.7943796e-13
Outputs:
- loss: float32 [], replicated
- grad_norm: float32 [], replicated
- mixing_in_new: float32 [3, 768, 6144], P(None, 'fsdp')
- mixing_in_first_new: float32 [3, 768, 6144], P(None, 'fsdp')
- mixing_in_second_new: float32 [3, 768, 6144], P(None, 'fsdp')
- mixing_out_new: float32 [3, 3072, 768], P(None, 'fsdp')
- mixing_out_first_new: float32 [3, 3072, 768], P(None, 'fsdp')
- mixing_out_second_new: float32 [3, 3072, 768], P(None, 'fsdp')
- norm_params_new: float32 [3, 6, 768], P(None, None, 'fsdp')
- norm_params_first_new: float32 [3, 6, 768], P(None, None, 'fsdp')
- norm_params_second_new: float32 [3, 6, 768], P(None, None, 'fsdp')
- input_embed_new: float32 [3200, 768], P('fsdp')
- input_embed_first_new: float32 [3200, 768], P('fsdp')
- input_embed_second_new: float32 [3200, 768], P('fsdp')
- word_table_new: float32 [65536, 768], P('fsdp')
- word_table_grad: float32 [65536, 768], P('fsdp')
- word_table_second_new: float32 [65536, 768], P('fsdp')
- head_proj_new: float32 [768, 1280], P('fsdp')
- head_proj_first_new: float32 [768, 1280], P('fsdp')
- head_proj_second_new: float32 [768, 1280], P('fsdp')
- video_text_proj_new: float32 [512, 256], P('fsdp')
- video_text_proj_first_new: float32 [512, 256], P('fsdp')
- video_text_proj_second_new: float32 [512, 256], P('fsdp')
The draws below stay inside these ranges and needn't reach their ends.
Inputs may be any that keep to these rules, and one draw needn't show every extreme that they name: `caption_clips`: slot 0 of a clip names that clip; every other slot names a clip at most two away from its own, counted cyclically over the 32 clips. `caption_counts`: clip c has (c * 3) // 32 plus one or two live slots, at most 3.
All inputs are finite; a program needn't handle non-finite values.
Results may differ from the reference program's by a relative error of at most 0.015.
The reference program's roundings to bfloat16 on the way count: a program that leaves them out, or rounds other values in their place, can miss the bound.
Values may be sent and summed in bfloat16 or wider, within the bound.
A program may use at most 384 MiB of HBM per device.

```python
import math
import jax
import jax.numpy as jnp
import numpy as np
from jax import lax

HEAD = 64
D = 768
FF = 3072
VA = 512
VT = 256
PATCH = 3072
WAVE = 128
VOCAB = 65536
LV = 512
LA = 1024
WORDS = 32
CAP = 3
ADAM_STEP = 10
CLIPS = 32
NPARAMS = 75150848


def clip_signal(key, features, row_count):
    first_key, second_key = jax.random.split(key, 2)
    common = jax.random.normal(first_key, (CLIPS, 1, features), jnp.float32)
    noise = jax.random.normal(second_key, (CLIPS, row_count, features), jnp.float32)
    return 0.4 * common + noise


def draw_video(key, part):
    return clip_signal(jax.random.fold_in(key, 101), PATCH, LV).astype(jnp.bfloat16)


def draw_audio(key, part):
    return clip_signal(jax.random.fold_in(key, 202), WAVE, LA).astype(jnp.bfloat16)


def draw_caption_counts(key, part):
    extra = jax.random.randint(jax.random.fold_in(key, 707), (CLIPS,), 1, 3)
    base = jnp.arange(CLIPS) * CAP // CLIPS
    return jnp.clip(base + extra, 1, CAP).astype(jnp.int32)


def draw_caption_clips(key, part):
    offsets = jax.random.randint(jax.random.fold_in(key, 303), (CLIPS, CAP), -2, 3)
    offsets = jnp.where(jnp.arange(CAP)[None, :] == 0, 0, offsets)
    return ((jnp.arange(CLIPS)[:, None] + offsets + CLIPS) % CLIPS).astype(jnp.int32)


def draw_mixing_in(key, part):
    base = jax.random.normal(jax.random.fold_in(key, 404), (3, D, 4 * D + FF), jnp.float32) * D ** (-0.5)
    lengths = jnp.array([LV, LA, WORDS], jnp.float32)[:, None, None] ** 0.25
    column = jnp.arange(4 * D + FF)[None, None, :]
    widened = jnp.where((column >= 3 * D) & (column < 4 * D), lengths, 1.0)
    return base * widened


def draw_norm_params(key, part):
    noise = jax.random.normal(jax.random.fold_in(key, 505), (3, 6, D), jnp.float32)
    kinds = jnp.arange(6)[None, :, None]
    return jnp.where(kinds % 2 == 0, 1.0 + 0.15 * noise, 0.1 * noise)


def draw_input_embed(key, part):
    noise = jax.random.normal(jax.random.fold_in(key, 606), (PATCH + WAVE, D), jnp.float32)
    rows_index = jnp.arange(PATCH + WAVE)[:, None]
    return noise * jnp.where(rows_index < PATCH, PATCH ** (-0.5), WAVE ** (-0.5))


def set_ends(entries, own_key, low, high):
    longest = entries.shape.index(max(entries.shape))
    spots = []
    for shift in (0, 1):
        where = [jax.random.randint(jax.random.fold_in(own_key, axis), (), 0, length) for axis, length in enumerate(entries.shape)]
        where[longest] = (where[longest] + shift) % entries.shape[longest]
        spots.append(tuple(where))
    return entries.at[spots[0]].set(low).at[spots[1]].set(high)


def levels(stream_key, shape, cuts, smallest, largest):
    gain, own = 1.0, jax.random.fold_in(stream_key, 6)
    for axis_at, blocks in cuts:
        steps = jnp.exp(jax.random.uniform(jax.random.fold_in(own, axis_at), (blocks,), jnp.float32, smallest / len(cuts), largest / len(cuts)))
        gain = gain * jnp.repeat(steps, shape[axis_at] // blocks).reshape([-1 if axis == axis_at else 1 for axis in range(len(shape))])
    return gain


def rank_bounds(amount, lean):
    loads = [(1 << 20) // math.isqrt(standing ** lean) + 1 for standing in range(1, amount + 1)]
    width = 1 + sum(loads) // (1 << 30)
    return np.cumsum(np.array([max(1, weight // width) for weight in loads]))


def skewed_ids(key, dims, count, slope):
    grid = rank_bounds(count, slope)
    lot = jax.random.randint(jax.random.fold_in(key, 1), dims, 0, int(grid[count - 1]))
    rank = jnp.searchsorted(jnp.asarray(grid, jnp.int32), lot, side="right")
    return jax.random.permutation(jax.random.fold_in(key, 2), count)[rank].astype(jnp.int32)


def normal_values(own_key, shape, deviation, reach, cuts=(), kind=jnp.bfloat16):
    drawn = deviation * jax.random.normal(own_key, shape, jnp.float32)
    if cuts:
        drawn = drawn * levels(own_key, shape, cuts, -0.22, 0.18)
    return jnp.clip(drawn, -reach, reach).astype(kind)


def setup_inputs(seed: int = 0) -> dict:
    key_of = jax.random.split(jax.random.key(seed), 28)
    return {
        "video": draw_video(jax.random.fold_in(key_of[27], 71), 0),
        "audio": draw_audio(jax.random.fold_in(key_of[27], 71), 0),
        "word_ids": set_ends(skewed_ids(key_of[2], (CLIPS, CAP, WORDS), VOCAB, 2), jax.random.fold_in(key_of[2], 3), 0, VOCAB - 1).astype(jnp.int32),
        "word_counts": set_ends(jax.random.randint(key_of[3], (CLIPS, CAP), 4, WORDS + 1), jax.random.fold_in(key_of[3], 1), 4, WORDS).astype(jnp.int32),
        "caption_counts": draw_caption_counts(jax.random.fold_in(key_of[27], 71), 0),
        "caption_clips": draw_caption_clips(jax.random.fold_in(key_of[27], 71), 0),
        "mixing_in": draw_mixing_in(jax.random.fold_in(key_of[27], 71), 0),
        "mixing_in_first": normal_values(key_of[7], (3, D, 4 * D + FF), (0.0011 / NPARAMS ** 0.5), 5.07558070239611e-07, ((1, 16),), jnp.float32),
        "mixing_in_second": jnp.clip(jnp.exp(math.log(2.794379582327783e-13) - 1.37681563 * jax.random.uniform(key_of[8], (3, D, 4 * D + FF), jnp.float32) ** levels(key_of[8], (3, D, 4 * D + FF), ((1, 16),), -0.2, 0.2)), 7.052481699760388e-14, 2.794379582327783e-13),
        "mixing_out": normal_values(key_of[9], (3, FF, D), FF ** -0.5, 0.109375, ((1, 16),), jnp.float32),
        "mixing_out_first": normal_values(key_of[10], (3, FF, D), (0.0011 / NPARAMS ** 0.5), 5.07558070239611e-07, ((1, 16),), jnp.float32),
        "mixing_out_second": jnp.clip(jnp.exp(math.log(2.794379582327783e-13) - 1.37681563 * jax.random.uniform(key_of[11], (3, FF, D), jnp.float32) ** levels(key_of[11], (3, FF, D), ((1, 16),), -0.2, 0.2)), 7.052481699760388e-14, 2.794379582327783e-13),
        "norm_params": draw_norm_params(jax.random.fold_in(key_of[27], 71), 0),
        "norm_params_first": normal_values(key_of[13], (3, 6, D), (0.0055 / NPARAMS ** 0.5), 2.537790351198055e-06, ((2, 16),), jnp.float32),
        "norm_params_second": jnp.clip(jnp.exp(math.log(7.052481862390714e-12) - 1.4053425 * jax.random.uniform(key_of[14], (3, 6, D), jnp.float32) ** levels(key_of[14], (3, 6, D), ((2, 16),), -0.2, 0.2)), 1.7298541071797402e-12, 7.052481862390714e-12),
        "input_embed": draw_input_embed(jax.random.fold_in(key_of[27], 71), 0),
        "input_embed_first": normal_values(key_of[16], (PATCH + WAVE, D), (0.0011 / NPARAMS ** 0.5), 5.07558070239611e-07, ((0, 16),), jnp.float32),
        "input_embed_second": jnp.clip(jnp.exp(math.log(2.794379582327783e-13) - 1.37681563 * jax.random.uniform(key_of[17], (PATCH + WAVE, D), jnp.float32) ** levels(key_of[17], (PATCH + WAVE, D), ((0, 16),), -0.2, 0.2)), 7.052481699760388e-14, 2.794379582327783e-13),
        "word_table": normal_values(key_of[18], (VOCAB, D), 0.3, 1.8, ((0, 16),), jnp.float32),
        "word_table_first": normal_values(key_of[19], (VOCAB, D), (0.0011 / NPARAMS ** 0.5), 5.07558070239611e-07, ((0, 16),), jnp.float32),
        "word_table_second": jnp.clip(jnp.exp(math.log(2.794379582327783e-13) - 1.37681563 * jax.random.uniform(key_of[20], (VOCAB, D), jnp.float32) ** levels(key_of[20], (VOCAB, D), ((0, 16),), -0.2, 0.2)), 7.052481699760388e-14, 2.794379582327783e-13),
        "head_proj": normal_values(key_of[21], (D, 2 * VA + VT), D ** -0.5, 0.21875, ((0, 16),), jnp.float32),
        "head_proj_first": normal_values(key_of[22], (D, 2 * VA + VT), (0.0011 / NPARAMS ** 0.5), 5.07558070239611e-07, ((0, 16),), jnp.float32),
        "head_proj_second": jnp.clip(jnp.exp(math.log(2.794379582327783e-13) - 1.37681563 * jax.random.uniform(key_of[23], (D, 2 * VA + VT), jnp.float32) ** levels(key_of[23], (D, 2 * VA + VT), ((0, 16),), -0.2, 0.2)), 7.052481699760388e-14, 2.794379582327783e-13),
        "video_text_proj": normal_values(key_of[24], (VA, VT), VA ** -0.5, 0.25, ((0, 16),), jnp.float32),
        "video_text_proj_first": normal_values(key_of[25], (VA, VT), (0.0011 / NPARAMS ** 0.5), 5.07558070239611e-07, ((0, 16),), jnp.float32),
        "video_text_proj_second": jnp.clip(jnp.exp(math.log(2.794379582327783e-13) - 1.37681563 * jax.random.uniform(key_of[26], (VA, VT), jnp.float32) ** levels(key_of[26], (VA, VT), ((0, 16),), -0.2, 0.2)), 7.052481699760388e-14, 2.794379582327783e-13),
    }


@jax.custom_vjp
def low(v):
    return lax.optimization_barrier(v.astype(jnp.bfloat16)).astype(jnp.float32)

@jax.custom_vjp
def low_back(v):
    return v

def low_keep(v):
    return (low(v), None)

def low_pass(kept, grad):
    return (grad,)

def back_keep(v):
    return (v, None)

def back_low(kept, grad):
    return (low(grad),)
low.defvjp(low_keep, low_pass)
low_back.defvjp(back_keep, back_low)
FULL_PRECISION = lax.Precision.HIGHEST
SOFTMAX_WARMTH = 0.03
CLIP_NORM = 0.01
RATES = (0.1, 0.05, 0.3, 0.1, 0.2, 0.1, 0.1)
BETA_ONE = 0.9
BETA_TWO = 0.95
EPSILON = 1e-08
WEIGHT_DECAY = 0.1

def norm_rows(values, gain_row, shift_row):
    centred = values - lax.optimization_barrier(jnp.mean(values, -1, keepdims=True))
    return centred * lax.rsqrt(lax.optimization_barrier(jnp.mean(centred * centred, -1, keepdims=True)) + 1e-06) * gain_row + shift_row

def unit_rows(values):
    return values * lax.rsqrt(lax.optimization_barrier(jnp.sum(values * values, -1, keepdims=True)) + 1e-06)

def log_sum(similarity_scores):
    highest = lax.optimization_barrier(jnp.max(similarity_scores, -1, keepdims=True))
    return highest[..., 0] + jnp.log(lax.optimization_barrier(jnp.sum(jnp.exp(similarity_scores - highest), -1)))

def word_bias(valid):
    captions, slots = valid.shape
    caption_of = jnp.arange(captions * slots) // slots
    allowed = (caption_of[:, None] == caption_of[None, :]) & (valid.reshape(-1)[None, :] > 0.5)
    return jnp.where(allowed, 0.0, -1000000000.0).astype(jnp.float32)

def pool_plain(stream, gain_row, shift_row):
    return norm_rows(lax.optimization_barrier(jnp.mean(stream, 0)), gain_row, shift_row)

def pool_words(stream, valid, gain_row, shift_row):
    captions, slots = valid.shape
    summed = lax.optimization_barrier(jnp.sum(stream.reshape(captions, slots, -1) * valid[:, :, None], 1))
    return norm_rows(summed / lax.optimization_barrier(jnp.sum(valid, 1))[:, None], gain_row, shift_row)

def project(video_pool, audio_pool, text_pool, heads, video_to_text_embed):
    joint = video_to_text_embed.shape[0]
    video_to_audio_embed = jnp.dot(video_pool, heads[:, :joint], precision=FULL_PRECISION)
    return (unit_rows(video_to_audio_embed), unit_rows(jnp.dot(video_to_audio_embed, video_to_text_embed, precision=FULL_PRECISION)), unit_rows(jnp.dot(audio_pool, heads[:, joint:2 * joint], precision=FULL_PRECISION)), unit_rows(jnp.dot(text_pool, heads[:, 2 * joint:], precision=FULL_PRECISION)))

def contrast(video_to_audio_embed, video_to_text_embed, gathered_audio_rows, gathered_text_rows, live, positive, own_clip):
    similarity_scores = jnp.dot(video_to_audio_embed, gathered_audio_rows.T, precision=FULL_PRECISION) / SOFTMAX_WARMTH
    matched = log_sum(similarity_scores) - lax.optimization_barrier(jnp.sum(similarity_scores * own_clip, -1))
    caption_embeddings = jnp.dot(video_to_text_embed, gathered_text_rows.T, precision=FULL_PRECISION) / SOFTMAX_WARMTH
    every_text = log_sum(jnp.where(live[None, :], caption_embeddings, -1e+30))
    chosen_text = log_sum(jnp.where(positive, caption_embeddings, -1e+30))
    weight_rows = lax.optimization_barrier(jnp.sum(positive.astype(jnp.float32), -1))
    live_total = jnp.sum(live.astype(jnp.float32))
    return jnp.sum(matched) / gathered_audio_rows.shape[0] + jnp.sum(weight_rows * (every_text - chosen_text)) / live_total

def adam_update(master, first, second, gradient, rate):
    first_new = BETA_ONE * first + (1.0 - BETA_ONE) * gradient
    second_new = BETA_TWO * second + (1.0 - BETA_TWO) * gradient * gradient
    first_hat = first_new / (1.0 - BETA_ONE ** ADAM_STEP)
    second_hat = second_new / (1.0 - BETA_TWO ** ADAM_STEP)
    master_new = master - rate * (first_hat / (jnp.sqrt(second_hat) + EPSILON) + WEIGHT_DECAY * master)
    return (master_new, first_new, second_new)

def layer(stream, bias, mixing, mixing_back, gains):
    row_count, features = stream.shape
    scaling = HEAD ** (-0.5)
    normed = low(norm_rows(stream, gains[0], gains[1]))
    joined = low_back(low(jnp.dot(normed, mixing[:, :3 * features], precision=FULL_PRECISION))).reshape(row_count, 3, -1, HEAD)
    similarity_scores = low_back(jnp.einsum('qhe,khe->hqk', joined[:, 0], joined[:, 1], precision=FULL_PRECISION) * scaling + bias[None])
    attention = jax.nn.softmax(similarity_scores, axis=-1)
    mixed = jnp.einsum('hqk,khe->qhe', low(attention), joined[:, 2], precision=FULL_PRECISION).reshape(row_count, features)
    mixed = low_back(low(mixed))
    middle = stream + low_back(jnp.dot(mixed, mixing[:, 3 * features:4 * features], precision=FULL_PRECISION))
    normed_two = low(norm_rows(middle, gains[2], gains[3]))
    hidden = low_back(jnp.dot(normed_two, mixing[:, 4 * features:], precision=FULL_PRECISION))
    return middle + low_back(jnp.dot(low(jax.nn.gelu(hidden)), mixing_back, precision=FULL_PRECISION))

def clip_towers(mixing, mixing_back, gains, embed, video_clip, audio_clip, words_clip, valid):
    video_rows = low_back(jnp.dot(video_clip, embed[:PATCH], precision=FULL_PRECISION))
    audio_rows = low_back(jnp.dot(audio_clip, embed[PATCH:], precision=FULL_PRECISION))
    video_out = layer(video_rows, jnp.zeros((LV, LV), jnp.float32), mixing[0], mixing_back[0], gains[0])
    audio_out = layer(audio_rows, jnp.zeros((LA, LA), jnp.float32), mixing[1], mixing_back[1], gains[1])
    text_out = layer(words_clip, word_bias(valid), mixing[2], mixing_back[2], gains[2])
    return (pool_plain(video_out, gains[0, 4], gains[0, 5]), pool_plain(audio_out, gains[1, 4], gains[1, 5]), pool_words(text_out, valid, gains[2, 4], gains[2, 5]))

def total_loss(masters, video, audio, word_ids, valid, live, positive):
    mixing, mixing_back, gains, embed, table, heads, video_to_text_embed = masters
    mixing = low(mixing)
    mixing_back = low(mixing_back)
    gains = low(gains)
    embed = low(embed)
    heads = low(heads)
    video_to_text_embed = low(video_to_text_embed)
    words = low_back(table[word_ids.reshape(word_ids.shape[0], -1)])

    def per_clip(inputs):
        return clip_towers(mixing, mixing_back, gains, embed, inputs[0], inputs[1], inputs[2], inputs[3])
    video_pool, audio_pool, text_pool = lax.map(jax.checkpoint(per_clip), (video, audio, words, valid))
    video_to_audio_embed, video_textual, audio_unit, text_unit = project(video_pool, audio_pool, text_pool, heads, video_to_text_embed)
    own_clip = jnp.eye(video.shape[0], dtype=jnp.float32)
    return contrast(video_to_audio_embed, video_textual, audio_unit, text_unit.reshape(-1, text_unit.shape[-1]), live, positive, own_clip)

def reference(video, audio, word_ids, word_counts, caption_counts, caption_clips, mixing_in, mixing_in_first, mixing_in_second, mixing_out, mixing_out_first, mixing_out_second, norm_params, norm_params_first, norm_params_second, input_embed, input_embed_first, input_embed_second, word_table, word_table_first, word_table_second, head_proj, head_proj_first, head_proj_second, video_text_proj, video_text_proj_first, video_text_proj_second):
    clip_total = video.shape[0]
    captions = word_ids.shape[1]
    valid = (jnp.arange(WORDS)[None, None, :] < word_counts[:, :, None]).astype(jnp.float32)
    live = (jnp.arange(captions)[None, :] < caption_counts[:, None]).reshape(-1)
    positive = live[None, :] & (caption_clips.reshape(-1)[None, :] == jnp.arange(clip_total)[:, None])
    masters = (mixing_in, mixing_out, norm_params, input_embed, word_table, head_proj, video_text_proj)
    firsts = (mixing_in_first, mixing_out_first, norm_params_first, input_embed_first, word_table_first, head_proj_first, video_text_proj_first)
    seconds = (mixing_in_second, mixing_out_second, norm_params_second, input_embed_second, word_table_second, head_proj_second, video_text_proj_second)
    video_f = video.astype(jnp.float32)
    audio_f = audio.astype(jnp.float32)

    def loss_of(*weights):
        return total_loss(weights, video_f, audio_f, word_ids, valid, live, positive)
    loss, pullback = jax.vjp(loss_of, *masters)
    grads = pullback(jnp.float32(1.0))
    square = sum((jnp.sum(g * g) for g in grads))
    grad_norm = jnp.sqrt(square)
    factor = CLIP_NORM / jnp.maximum(grad_norm, CLIP_NORM)
    clipped = [g * factor for g in grads]
    new = [adam_update(masters[i], firsts[i], seconds[i], clipped[i], RATES[i]) for i in range(7)]
    return (loss, grad_norm, new[0][0], new[0][1], new[0][2], new[1][0], new[1][1], new[1][2], new[2][0], new[2][1], new[2][2], new[3][0], new[3][1], new[3][2], new[4][0], clipped[4], new[4][2], new[5][0], new[5][1], new[5][2], new[6][0], new[6][1], new[6][2])
```

```python
import functools

import jax
import jax.numpy as jnp
from jax import lax
from jax.experimental import pallas as pl
from jax.experimental.pallas import tpu as pltpu
from jax.sharding import PartitionSpec as P

ADAM_STEP = 10
FULL_PRECISION = lax.Precision.HIGHEST
SOFTMAX_WARMTH = 0.03
CLIP_NORM = 0.01
RATES = (0.1, 0.05, 0.3, 0.1, 0.2, 0.1, 0.1)
BETA_ONE = 0.9
BETA_TWO = 0.95
EPSILON = 1e-08
WEIGHT_DECAY = 0.1
F32 = jnp.float32
BF16 = jnp.bfloat16
MESH_ID = pl.DeviceIdType.MESH
VMEM_LIMIT = 56 * 1024 * 1024
NT = (((1,), (1,)), ((), ()))


def dot(a, b):
    return jnp.dot(a, b, preferred_element_type=F32)


def dot_nt(a, b):
    return lax.dot_general(a, b, NT, preferred_element_type=F32)


def dot_tn(a, b):
    return lax.dot_general(a, b, (((0,), (0,)), ((), ())), preferred_element_type=F32)


def full(a, b):
    return jnp.dot(a, b, precision=FULL_PRECISION)


def norm_rows(values, gain_row, shift_row):
    centred = values - jnp.mean(values, -1, keepdims=True)
    return (
        centred * lax.rsqrt(jnp.mean(centred * centred, -1, keepdims=True) + 1e-06) * gain_row
        + shift_row
    )


def unit_rows(values):
    return values * lax.rsqrt(jnp.sum(values * values, -1, keepdims=True) + 1e-06)


def log_sum(scores):
    highest = jnp.max(scores, -1, keepdims=True)
    return highest[..., 0] + jnp.log(jnp.sum(jnp.exp(scores - highest), -1))


def adam_update(master, first, second, gradient, rate):
    first_new = BETA_ONE * first + (1.0 - BETA_ONE) * gradient
    second_new = BETA_TWO * second + (1.0 - BETA_TWO) * gradient * gradient
    first_hat = first_new / (1.0 - BETA_ONE**ADAM_STEP)
    second_hat = second_new / (1.0 - BETA_TWO**ADAM_STEP)
    master_new = master - rate * (
        first_hat / (jnp.sqrt(second_hat) + EPSILON) + WEIGHT_DECAY * master
    )
    return (master_new, first_new, second_new)


def everyone_kernel(x_ref, o_ref, send, recv, local):
    group = lax.axis_size("fsdp")
    count = lax.axis_size("dp") * group
    me = lax.axis_index("dp") * group + lax.axis_index("fsdp")
    barrier = pltpu.get_barrier_semaphore()

    def place(step):
        peer = lax.rem(me + step, count)
        return (peer // group, lax.rem(peer, group))

    def greet(step, carry):
        pl.semaphore_signal(barrier, inc=1, device_id=place(step), device_id_type=MESH_ID)
        return carry

    lax.fori_loop(1, count, greet, 0)
    mine = pltpu.make_async_copy(x_ref, o_ref.at[me], local)
    mine.start()
    pl.semaphore_wait(barrier, count - 1)

    def copy(step):
        return pltpu.make_async_remote_copy(
            src_ref=x_ref,
            dst_ref=o_ref.at[me],
            send_sem=send.at[step],
            recv_sem=recv.at[step],
            device_id=place(step),
            device_id_type=MESH_ID,
        )

    def begin(step, carry):
        copy(step).start()
        return carry

    def finish(step, carry):
        copy(step).wait()
        return carry

    lax.fori_loop(1, count, begin, 0)
    mine.wait()
    lax.fori_loop(1, count, finish, 0)


def everyone(x, collective):
    count = lax.axis_size("dp") * lax.axis_size("fsdp")
    return pl.pallas_call(
        everyone_kernel,
        out_shape=jax.ShapeDtypeStruct((count,) + x.shape, x.dtype),
        in_specs=[pl.BlockSpec(memory_space=pltpu.VMEM)],
        out_specs=pl.BlockSpec(memory_space=pltpu.VMEM),
        scratch_shapes=[
            pltpu.SemaphoreType.DMA((count,)),
            pltpu.SemaphoreType.DMA((count,)),
            pltpu.SemaphoreType.DMA,
        ],
        compiler_params=pltpu.CompilerParams(collective_id=collective, has_side_effects=True),
        name=f"everyone_{collective}",
    )(x)


def attend_kernel(rows, block, masked, *refs):
    if masked:
        qkv_ref, bias_ref, o_ref, l_ref = refs
    else:
        qkv_ref, o_ref, l_ref = refs
    lane = lax.broadcasted_iota(jnp.int32, (1, 128), 1)
    low = lane < 64
    keys = qkv_ref[:, 128:256]
    values = qkv_ref[:, 256:384]
    for at in range(0, rows, block):
        queries = qkv_ref[at : at + block, :128]
        outs, totals = [], []
        for head in range(2):
            picked = jnp.where(low if head == 0 else ~low, queries, 0) * jnp.array(0.125, BF16)
            scores = dot_nt(picked, keys)
            if masked:
                scores = scores + bias_ref[at : at + block, :]
            highest = jnp.max(scores, -1, keepdims=True)
            exponent = jnp.exp(scores - highest)
            summed = jnp.sum(exponent, -1, keepdims=True)
            outs.append(dot(exponent.astype(BF16), values) * (1.0 / summed))
            totals.append(highest + jnp.log(summed))
        o_ref[at : at + block, :] = jnp.where(low, outs[0], outs[1]).astype(BF16)
        l_ref[at : at + block, :] = jnp.where(low, totals[0], totals[1])


def attend(qkv, bias, block):
    rows, width = qkv.shape
    pairs = width // 384
    specs = [pl.BlockSpec((rows, 384), lambda j: (0, j))]
    args = [qkv]
    if bias is not None:
        specs.append(pl.BlockSpec(bias.shape, lambda j: (0, 0)))
        args.append(bias)
    return pl.pallas_call(
        functools.partial(attend_kernel, rows, block, bias is not None),
        grid=(pairs,),
        out_shape=(
            jax.ShapeDtypeStruct((rows, pairs * 128), BF16),
            jax.ShapeDtypeStruct((rows, pairs * 128), F32),
        ),
        in_specs=specs,
        out_specs=(
            pl.BlockSpec((rows, 128), lambda j: (0, j)),
            pl.BlockSpec((rows, 128), lambda j: (0, j)),
        ),
        compiler_params=pltpu.CompilerParams(vmem_limit_bytes=VMEM_LIMIT),
        cost_estimate=pl.CostEstimate(
            flops=16 * rows * rows * 256 * pairs,
            bytes_accessed=rows * pairs * 128 * 12,
            transcendentals=2 * pairs * rows * rows,
        ),
        name=f"attend_{rows}",
    )(*args)


def attend_back_kernel(rows, block, masked, *refs):
    if masked:
        qkv_ref, do_ref, o_ref, l_ref, bias_ref, g_ref, dk_ref, dv_ref = refs
    else:
        qkv_ref, do_ref, o_ref, l_ref, g_ref, dk_ref, dv_ref = refs
    lane = lax.broadcasted_iota(jnp.int32, (1, 128), 1)
    low = lane < 64
    keys = qkv_ref[:, 128:256]
    values = qkv_ref[:, 256:384]
    keys_t = keys.astype(F32).T.astype(BF16)
    row = lax.broadcasted_iota(jnp.int32, (128, 1), 0)
    keys_of = [jnp.where(row < 64, keys_t, 0), jnp.where(row < 64, 0, keys_t)]
    eighth = jnp.array(0.125, BF16)
    for at in range(0, rows, block):
        queries = qkv_ref[at : at + block, :128]
        grads = do_ref[at : at + block, :]
        totals_t = l_ref[at : at + block, :].T
        product_t = (grads.astype(F32) * o_ref[at : at + block, :].astype(F32)).T
        grad_q = None
        for head in range(2):
            mask = low if head == 0 else ~low
            picked = jnp.where(mask, queries, 0) * eighth
            picked_grad = jnp.where(mask, grads, 0)
            total = totals_t[64 * head : 64 * head + 1, :]
            delta = jnp.sum(product_t[64 * head : 64 * head + 64, :], 0, keepdims=True)
            scores = dot_nt(keys, picked)
            if masked:
                scores = scores + bias_ref[:, at : at + block]
            weights = jnp.exp(scores - total)
            grad_weights = dot_nt(values, picked_grad)
            grad_scores = (weights * (grad_weights - delta)).astype(BF16)
            part_v = dot(weights.astype(BF16), picked_grad)
            part_k = dot(grad_scores, picked)
            if at == 0 and head == 0:
                dv_ref[...] = part_v
                dk_ref[...] = part_k
            else:
                dv_ref[...] += part_v
                dk_ref[...] += part_k
            part_q = dot(keys_of[head], grad_scores)
            grad_q = part_q if grad_q is None else grad_q + part_q
        g_ref[at : at + block, :128] = (grad_q.T * 0.125).astype(BF16)
    g_ref[:, 128:256] = dk_ref[...].astype(BF16)
    g_ref[:, 256:384] = dv_ref[...].astype(BF16)


def attend_back(qkv, grad_out, out, totals, bias, block):
    rows, width = qkv.shape
    pairs = width // 384
    specs = [
        pl.BlockSpec((rows, 384), lambda j: (0, j)),
        pl.BlockSpec((rows, 128), lambda j: (0, j)),
        pl.BlockSpec((rows, 128), lambda j: (0, j)),
        pl.BlockSpec((rows, 128), lambda j: (0, j)),
    ]
    args = [qkv, grad_out, out, totals]
    if bias is not None:
        specs.append(pl.BlockSpec(bias.shape, lambda j: (0, 0)))
        args.append(bias)
    return pl.pallas_call(
        functools.partial(attend_back_kernel, rows, block, bias is not None),
        grid=(pairs,),
        out_shape=jax.ShapeDtypeStruct(qkv.shape, BF16),
        in_specs=specs,
        out_specs=pl.BlockSpec((rows, 384), lambda j: (0, j)),
        scratch_shapes=[pltpu.VMEM((rows, 128), F32), pltpu.VMEM((rows, 128), F32)],
        compiler_params=pltpu.CompilerParams(vmem_limit_bytes=VMEM_LIMIT),
        cost_estimate=pl.CostEstimate(
            flops=40 * rows * rows * 256 * pairs,
            bytes_accessed=rows * pairs * 128 * 20,
            transcendentals=2 * pairs * rows * rows,
        ),
        name=f"attend_back_{rows}",
    )(*args)


def feed_kernel(with_product, h_ref, w_ref, sel_ref, slope_ref, sums_ref, *rest):
    hidden = dot(h_ref[...], w_ref[...])
    root = 0.7978845608028654
    square = hidden * hidden
    tang = jnp.tanh(root * hidden * (1.0 + 0.044715 * square))
    half = 0.5 * (1.0 + tang)
    active = (hidden * half).astype(BF16)
    slope = half + (0.5 * root) * hidden * (1.0 - tang * tang) * (1.0 + (3 * 0.044715) * square)
    slope = slope.astype(BF16)
    slope_ref[...] = slope
    if with_product:
        sums_ref[...] = jnp.broadcast_to(
            jnp.sum(active.astype(F32), 0, keepdims=True), sums_ref.shape
        )
        rest[0][...] = dot_tn(h_ref[...], slope).astype(BF16)
    else:
        sums_ref[...] = dot(sel_ref[...], active)


def feed(normed, weight, select, column, tile, with_product):
    rows, features = normed.shape
    width = weight.shape[1] - column
    first = column // tile
    shapes = [
        jax.ShapeDtypeStruct((rows, width), BF16),
        jax.ShapeDtypeStruct((8, width), F32),
    ]
    outs = [
        pl.BlockSpec((rows, tile), lambda j: (0, j)),
        pl.BlockSpec((8, tile), lambda j: (0, j)),
    ]
    if with_product:
        shapes.append(jax.ShapeDtypeStruct((features, width), BF16))
        outs.append(pl.BlockSpec((features, tile), lambda j: (0, j)))
    return pl.pallas_call(
        functools.partial(feed_kernel, with_product),
        grid=(width // tile,),
        out_shape=tuple(shapes),
        in_specs=[
            pl.BlockSpec((rows, features), lambda j: (0, 0)),
            pl.BlockSpec((features, tile), lambda j: (0, first + j)),
            pl.BlockSpec(select.shape, lambda j: (0, 0)),
        ],
        out_specs=tuple(outs),
        compiler_params=pltpu.CompilerParams(vmem_limit_bytes=VMEM_LIMIT),
        cost_estimate=pl.CostEstimate(
            flops=4 * rows * features * width,
            bytes_accessed=2 * features * width * 2 + 2 * rows * width,
            transcendentals=rows * width,
        ),
        name=f"feed_{rows}",
    )(normed, weight, select)


def layer_forward(stream, bias, mixing, gains, select, block, with_product):
    features = stream.shape[1]
    normed = norm_rows(stream, gains[0], gains[1]).astype(BF16)
    joined = dot(normed, mixing[:, : 3 * features]).astype(BF16)
    mixed, totals = attend(joined, bias, block)
    middle = stream + dot(mixed, mixing[:, 3 * features : 4 * features])
    normed_two = norm_rows(middle, gains[2], gains[3]).astype(BF16)
    fed = feed(normed_two, mixing, select, 4 * features, 512, with_product)
    return middle, fed, (stream, normed, joined, totals, mixed, middle, normed_two)


def layer_backward(grad_rows, grad_normed_two, saved, bias, mixing, gains, block):
    stream, normed, joined, totals, mixed, middle, normed_two = saved
    features = stream.shape[1]
    grad_middle_norm, grad_gain_three, grad_shift_three = jax.vjp(
        norm_rows, middle, gains[2], gains[3]
    )[1](grad_normed_two)
    grad_middle = grad_rows + grad_middle_norm
    grad_attention = grad_middle.astype(BF16)
    grad_output = dot_tn(mixed, grad_attention)
    grad_mixed = dot_nt(grad_attention, mixing[:, 3 * features : 4 * features]).astype(BF16)
    grad_joined = attend_back(
        joined, grad_mixed, mixed, totals, None if bias is None else bias.T, block
    )
    grad_inward = dot_tn(normed, grad_joined)
    grad_normed = dot_nt(grad_joined, mixing[:, : 3 * features])
    grad_stream_norm, grad_gain_one, grad_shift_one = jax.vjp(
        norm_rows, stream, gains[0], gains[1]
    )[1](grad_normed)
    grad_gains = jnp.stack([grad_gain_one, grad_shift_one, grad_gain_three, grad_shift_three])
    return (grad_middle + grad_stream_norm, grad_inward, grad_output, grad_gains)


def body(
    video,
    audio,
    word_ids,
    word_counts,
    caption_counts,
    caption_clips,
    mixing_in,
    mixing_in_first,
    mixing_in_second,
    mixing_out,
    mixing_out_first,
    mixing_out_second,
    norm_params,
    norm_params_first,
    norm_params_second,
    input_embed,
    input_embed_first,
    input_embed_second,
    word_table,
    word_table_first,
    word_table_second,
    head_proj,
    head_proj_first,
    head_proj_second,
    video_text_proj,
    video_text_proj_first,
    video_text_proj_second,
):
    group = lax.axis_size("fsdp")
    replicas = lax.axis_size("dp")
    clips = group * replicas
    member = lax.axis_index("fsdp")
    replica = lax.axis_index("dp")
    clip = replica * group + member
    captions, slots = word_ids.shape[1:]
    words = captions * slots
    patch = video.shape[2]
    video_count, audio_count = video.shape[1], audio.shape[1]
    features = mixing_in.shape[1] * group
    pairs = features // 128
    shard = mixing_in.shape[1]
    qkv = 3 * features

    gain_part = norm_params.shape[2]
    packed = jnp.concatenate(
        [
            word_ids.reshape(-1).astype(F32),
            word_counts.reshape(-1).astype(F32),
            caption_counts.reshape(-1).astype(F32),
            caption_clips.reshape(-1).astype(F32),
            norm_params.reshape(-1),
        ]
    )
    size = packed.shape[0]
    packed = jnp.pad(packed, (0, -size % 1024)).reshape(-1, 128)
    every = everyone(packed, 0).reshape(clips, -1)
    all_ids = every[:, :words].astype(jnp.int32)
    at = words + captions
    all_caption_counts = every[:, at].astype(jnp.int32)
    all_counts = every[:, words : words + captions]
    all_caption_clips = every[:, at + 1 : at + 1 + captions].astype(jnp.int32)
    at = at + 1 + captions
    gains_all = (
        every[:group, at : at + 18 * gain_part]
        .reshape(group, 3, 6, gain_part)
        .transpose(1, 2, 0, 3)
        .reshape(3, 6, features)
        .astype(BF16)
        .astype(F32)
    )

    def gather(values, axis=0):
        return lax.all_gather(values, "fsdp", axis=axis, tiled=True)

    def regroup(values):
        inward = values[:, :qkv].reshape(shard, 3, pairs, 128).transpose(0, 2, 1, 3)
        return jnp.concatenate([inward.reshape(shard, qkv), values[:, qkv:]], 1)

    embed = gather(input_embed.astype(BF16))
    mixings = [gather(regroup(mixing_in[tower].astype(BF16))) for tower in range(3)]
    backs = gather(mixing_out.astype(BF16), 1)
    heads = gather(head_proj.astype(BF16)).astype(F32)
    video_text = gather(video_text_proj.astype(BF16)).astype(F32)

    table_rows = word_table.shape[0]

    def owned_rows(ids):
        local_ids = ids - member * table_rows
        owned = (local_ids >= 0) & (local_ids < table_rows)
        return jnp.clip(local_ids, 0, table_rows - 1), owned

    group_ids = lax.dynamic_slice_in_dim(all_ids, replica * group, group, 0).reshape(-1)
    local_ids, owned = owned_rows(group_ids)
    words_in = lax.psum_scatter(
        jnp.where(owned[:, None], word_table[local_ids], 0.0).astype(BF16),
        "fsdp",
        scatter_dimension=0,
        tiled=True,
    ).astype(F32)

    valid = jnp.arange(slots)[None, :] < word_counts[0][:, None]
    flat_valid = valid.reshape(-1)
    caption_of = jnp.arange(words) // slots
    allowed = (caption_of[:, None] == caption_of[None, :]) & flat_valid[None, :]
    word_bias = jnp.where(allowed, 0.0, -1000000000.0).astype(F32)
    select = ((jnp.arange(8)[:, None] == caption_of[None, :]) & flat_valid[None, :]).astype(BF16)
    unused = jnp.zeros((8, 128), BF16)

    streams = (
        dot(video[0], embed[:patch]),
        dot(audio[0], embed[patch:]),
        words_in,
    )
    biases = (None, None, word_bias)
    selects = (unused, unused, select)
    forward_block = (512, 512, words)
    backward_block = (512, 256, words)
    caches, slopes, sums, products = [], [], [], []
    tokens = []
    counts = word_counts[0].astype(F32)
    for tower in range(3):
        middle, fed, cache = layer_forward(
            streams[tower],
            biases[tower],
            mixings[tower],
            gains_all[tower],
            selects[tower],
            forward_block[tower],
            tower < 2,
        )
        caches.append(cache)
        slopes.append(fed[0])
        if tower < 2:
            products.append(fed[2])
            summed = fed[1][:1]
            base = jnp.sum(middle, 0, keepdims=True)
            scale = 1.0 / middle.shape[0]
        else:
            summed = fed[1][:captions]
            base = full(select[:captions].astype(F32), middle)
            scale = 1.0 / counts[:, None]
        upper = summed.astype(BF16)
        lower = (summed - upper.astype(F32)).astype(BF16)
        through = dot(upper, backs[tower]) + dot(lower, backs[tower])
        tokens.append((base + through) * scale)
        sums.append(summed)

    token_count = 2 + captions
    mine = jnp.concatenate(tokens, 0)
    pooled = everyone(jnp.pad(mine, ((0, -token_count % 8), (0, 0))), 1)
    pooled_rows = (pooled[:, 0], pooled[:, 1], pooled[:, 2:token_count].reshape(-1, features))
    live = (jnp.arange(captions)[None, :] < all_caption_counts[:, None]).reshape(-1)
    positive = live[None, :] & (all_caption_clips.reshape(-1)[None, :] == jnp.arange(clips)[:, None])
    joint = video_text.shape[0]
    heads_of = (heads[:, :joint], heads[:, joint : 2 * joint], heads[:, 2 * joint :])

    normed_pull = [
        jax.vjp(norm_rows, pooled_rows[t], gains_all[t, 4], gains_all[t, 5]) for t in range(3)
    ]
    z = [entry[0] for entry in normed_pull]
    embed_video = full(z[0], heads_of[0])
    embed_video_text = full(embed_video, video_text)
    embed_audio = full(z[1], heads_of[1])
    embed_text = full(z[2], heads_of[2])

    def contrast(e_video, e_video_text, e_audio, e_text):
        scores = full(unit_rows(e_video), unit_rows(e_audio).T) / SOFTMAX_WARMTH
        own = jnp.eye(clips, dtype=F32)
        matched = log_sum(scores) - jnp.sum(scores * own, -1)
        text_scores = full(unit_rows(e_video_text), unit_rows(e_text).T) / SOFTMAX_WARMTH
        every_text = log_sum(jnp.where(live[None, :], text_scores, -1e30))
        chosen_text = log_sum(jnp.where(positive, text_scores, -1e30))
        weight_rows = jnp.sum(positive.astype(F32), -1)
        live_total = jnp.sum(live.astype(F32))
        return (
            jnp.sum(matched) / clips
            + jnp.sum(weight_rows * (every_text - chosen_text)) / live_total
        )

    loss, pull = jax.vjp(contrast, embed_video, embed_video_text, embed_audio, embed_text)
    d_video, d_video_text, d_audio, d_text = pull(F32(1.0))
    d_video = d_video + full(d_video_text, video_text.T)
    d_heads = (d_video, d_audio, d_text)
    grad_pooled, grad_pool_gains = [], []
    for t in range(3):
        d_rows, d_gain, d_shift = normed_pull[t][1](full(d_heads[t], heads_of[t].T))
        grad_pooled.append(d_rows)
        grad_pool_gains.append(jnp.stack([d_gain, d_shift]))

    def own_columns(values):
        return lax.dynamic_slice_in_dim(values, member * shard, shard, 1)

    heads_grad = jnp.concatenate([full(own_columns(z[t]).T, d_heads[t]) for t in range(3)], 1)
    joint_part = video_text_proj.shape[0]
    video_text_grad = full(
        lax.dynamic_slice_in_dim(embed_video, member * joint_part, joint_part, 1).T, d_video_text
    )
    grad_rows_all = [
        grad_pooled[0] / video_count,
        grad_pooled[1] / audio_count,
        grad_pooled[2] / all_counts.reshape(-1, 1),
    ]
    branch_all = [rows.astype(BF16) for rows in grad_rows_all]

    every_sum = lax.all_gather(jnp.concatenate(sums, 0), ("dp", "fsdp"), axis=0, tiled=False)
    back_part = mixing_out.shape[1]
    own_sums = lax.dynamic_slice_in_dim(every_sum, member * back_part, back_part, 2)
    own_sums = (own_sums[:, 0], own_sums[:, 1], own_sums[:, 2:].reshape(-1, back_part))
    back_grad = jnp.stack([full(own_sums[t].T, branch_all[t].astype(F32)) for t in range(3)])

    def own_rows(values, per_clip):
        return lax.dynamic_slice_in_dim(values, clip * per_clip, per_clip, 0)

    own_grads = [own_rows(grad_rows_all[t], 1 if t < 2 else captions) for t in range(3)]
    own_slopes = [
        dot_nt(own_grads[t].astype(BF16), backs[t]) for t in range(3)
    ]

    def over_replicas(part):
        part = part.astype(BF16)
        if replicas == 2:
            other = lax.ppermute(part, "dp", [(0, 1), (1, 0)])
            return part.astype(F32) + other.astype(F32)
        return lax.psum(part, "dp").astype(F32)

    def scatter(values):
        part = lax.psum_scatter(values.astype(BF16), "fsdp", scatter_dimension=0, tiled=True)
        return over_replicas(part)

    up_grads = scatter(
        jnp.concatenate(
            [(products[t].astype(F32) * own_slopes[t]).astype(BF16) for t in (1, 0)], 1
        )
    )
    hidden = products[0].shape[1]

    grad_inputs, gains_grads, shares = [None] * 3, [None] * 3, [None] * 3
    for tower in (2, 0, 1):
        weights = mixings[tower]
        if tower == 2:
            spread = select[:captions].astype(F32).T
            rows_grad = full(spread, own_grads[tower])
            slope_rows = full(spread, own_slopes[tower])
            grad_hidden = (slopes[tower].astype(F32) * slope_rows).astype(BF16)
            up = dot_tn(caches[tower][6], grad_hidden)
            grad_normed_two = dot_nt(grad_hidden, weights[:, 4 * features :])
        else:
            rows_grad = own_grads[tower]
            scaled = (weights[:, 4 * features :].astype(F32) * own_slopes[tower]).astype(BF16)
            grad_normed_two = dot_nt(slopes[tower], scaled)
        grad_inputs[tower], inward, outward, gains_grads[tower] = layer_backward(
            rows_grad,
            grad_normed_two,
            caches[tower],
            biases[tower],
            weights,
            gains_all[tower],
            backward_block[tower],
        )
        if tower == 2:
            shares[2] = scatter(
                jnp.concatenate([inward.astype(BF16), outward.astype(BF16), up.astype(BF16)], 1)
            )
            every_word = lax.all_gather(
                grad_inputs[2].astype(BF16), ("dp", "fsdp"), axis=0, tiled=True
            )
            local_ids, owned = owned_rows(all_ids.reshape(-1))
            table_grad = jax.ops.segment_sum(
                jnp.where(owned[:, None], every_word.astype(F32), 0.0),
                local_ids,
                num_segments=table_rows,
            )
        elif tower == 0:
            shares[0] = scatter(jnp.concatenate([inward.astype(BF16), outward.astype(BF16)], 1))
        else:
            gain_columns = jnp.concatenate(gains_grads, 0)
            gain_columns = jnp.pad(gain_columns, ((0, 128 - gain_columns.shape[0]), (0, 0))).T
            shares[1] = scatter(
                jnp.concatenate(
                    [inward.astype(BF16), outward.astype(BF16), gain_columns.astype(BF16)], 1
                )
            )
    embed_grad = scatter(
        jnp.concatenate(
            [
                dot_tn(video[0], grad_inputs[0].astype(BF16)).astype(BF16),
                dot_tn(audio[0], grad_inputs[1].astype(BF16)).astype(BF16),
            ],
            0,
        )
    )

    def ungroup(part):
        inward = part[:, :qkv].reshape(shard, pairs, 3, 128).transpose(0, 2, 1, 3)
        return jnp.concatenate([inward.reshape(shard, qkv), part[:, qkv:]], 1)

    mixing_grad = jnp.stack(
        [
            ungroup(jnp.concatenate([shares[0], up_grads[:, hidden:]], 1)),
            ungroup(jnp.concatenate([shares[1][:, : 4 * features], up_grads[:, :hidden]], 1)),
            ungroup(shares[2]),
        ]
    )
    inner_gains = shares[1][:, 4 * features : 4 * features + 12].T.reshape(3, 4, gain_part)
    outer_gains = lax.dynamic_slice_in_dim(
        jnp.stack(grad_pool_gains), member * gain_part, gain_part, 2
    )
    gains_grad = jnp.concatenate([inner_gains, outer_gains], 1)

    grads = (
        mixing_grad,
        back_grad,
        gains_grad,
        embed_grad,
        table_grad,
        heads_grad,
        video_text_grad,
    )
    local_square = sum((jnp.sum(g * g) for g in grads))
    squares = everyone(jnp.full((8, 128), local_square, F32), 2)
    square = jnp.sum(squares[:group, 0, 0])
    grad_norm = jnp.sqrt(square)
    factor = CLIP_NORM / jnp.maximum(grad_norm, CLIP_NORM)
    clipped = [g * factor for g in grads]
    masters = (
        mixing_in,
        mixing_out,
        norm_params,
        input_embed,
        word_table,
        head_proj,
        video_text_proj,
    )
    firsts = (
        mixing_in_first,
        mixing_out_first,
        norm_params_first,
        input_embed_first,
        word_table_first,
        head_proj_first,
        video_text_proj_first,
    )
    seconds = (
        mixing_in_second,
        mixing_out_second,
        norm_params_second,
        input_embed_second,
        word_table_second,
        head_proj_second,
        video_text_proj_second,
    )
    new = [adam_update(masters[i], firsts[i], seconds[i], clipped[i], RATES[i]) for i in range(7)]
    outputs = [loss, grad_norm]
    for i in range(7):
        outputs += [new[i][0], clipped[4] if i == 4 else new[i][1], new[i][2]]
    return tuple(outputs)


def solution(mesh):
    both = ("dp", "fsdp")
    weight_specs = (
        P(None, "fsdp", None),
        P(None, "fsdp", None),
        P(None, None, "fsdp"),
        P("fsdp", None),
        P("fsdp", None),
        P("fsdp", None),
        P("fsdp", None),
    )
    tripled = tuple(spec for spec in weight_specs for _ in range(3))
    return jax.shard_map(
        body,
        mesh=mesh,
        in_specs=(
            P(both, None, None),
            P(both, None, None),
            P(both, None, None),
            P(both, None),
            P(both),
            P(both, None),
        )
        + tripled,
        out_specs=(P(), P()) + tripled,
        check_vma=False,
    )
```

```python
import functools

import jax
import jax.numpy as jnp
from jax import lax
from jax.experimental import pallas as pl
from jax.experimental.pallas import tpu as pltpu
from jax.sharding import PartitionSpec as P

ADAM_STEP = 10
FULL_PRECISION = lax.Precision.HIGHEST
SOFTMAX_WARMTH = 0.03
CLIP_NORM = 0.01
RATES = (0.1, 0.05, 0.3, 0.1, 0.2, 0.1, 0.1)
BETA_ONE = 0.9
BETA_TWO = 0.95
EPSILON = 1e-08
WEIGHT_DECAY = 0.1
F32 = jnp.float32
BF16 = jnp.bfloat16
MESH_ID = pl.DeviceIdType.MESH
VMEM_LIMIT = 56 * 1024 * 1024
NT = (((1,), (1,)), ((), ()))


def dot(a, b):
    return jnp.dot(a, b, preferred_element_type=F32)


def dot_nt(a, b):
    return lax.dot_general(a, b, NT, preferred_element_type=F32)


def dot_tn(a, b):
    return lax.dot_general(a, b, (((0,), (0,)), ((), ())), preferred_element_type=F32)


def full(a, b):
    return jnp.dot(a, b, precision=FULL_PRECISION)


def dot_nt_full(a, b):
    return lax.dot_general(a, b, NT, precision=FULL_PRECISION, preferred_element_type=F32)


def norm_rows(values, gain_row, shift_row):
    centred = values - jnp.mean(values, -1, keepdims=True)
    return (
        centred * lax.rsqrt(jnp.mean(centred * centred, -1, keepdims=True) + 1e-06) * gain_row
        + shift_row
    )


def unit_rows(values):
    return values * lax.rsqrt(jnp.sum(values * values, -1, keepdims=True) + 1e-06)


def log_sum(scores):
    highest = jnp.max(scores, -1, keepdims=True)
    return highest[..., 0] + jnp.log(jnp.sum(jnp.exp(scores - highest), -1))


def adam_update(master, first, second, gradient, rate):
    first_new = BETA_ONE * first + (1.0 - BETA_ONE) * gradient
    second_new = BETA_TWO * second + (1.0 - BETA_TWO) * gradient * gradient
    first_hat = first_new / (1.0 - BETA_ONE**ADAM_STEP)
    second_hat = second_new / (1.0 - BETA_TWO**ADAM_STEP)
    master_new = master - rate * (
        first_hat / (jnp.sqrt(second_hat) + EPSILON) + WEIGHT_DECAY * master
    )
    return (master_new, first_new, second_new)


def exchange_kernel(within, parts, x_ref, o_ref, send, recv, local):
    group = lax.axis_size("fsdp")
    member = lax.axis_index("fsdp")
    replica = lax.axis_index("dp")
    count = group if within else lax.axis_size("dp") * group
    me = member if within else replica * group + member
    barrier = pltpu.get_barrier_semaphore()

    def place(step):
        peer = lax.rem(me + step, count)
        if within:
            return peer, (replica, peer)
        return peer, (peer // group, lax.rem(peer, group))

    def part(peer):
        return x_ref.at[lax.rem(peer, group)] if parts else x_ref

    def greet(step, carry):
        pl.semaphore_signal(barrier, inc=1, device_id=place(step)[1], device_id_type=MESH_ID)
        return carry

    lax.fori_loop(1, count, greet, 0)
    mine = pltpu.make_async_copy(part(me), o_ref.at[me], local)
    mine.start()
    pl.semaphore_wait(barrier, count - 1)

    def copy(step):
        peer, device = place(step)
        return pltpu.make_async_remote_copy(
            src_ref=part(peer),
            dst_ref=o_ref.at[me],
            send_sem=send.at[step],
            recv_sem=recv.at[step],
            device_id=device,
            device_id_type=MESH_ID,
        )

    def begin(step, carry):
        copy(step).start()
        return carry

    def finish(step, carry):
        copy(step).wait()
        return carry

    lax.fori_loop(1, count, begin, 0)
    mine.wait()
    lax.fori_loop(1, count, finish, 0)


def everyone(x, collective, within=False, parts=False):
    group = lax.axis_size("fsdp")
    count = group if within else lax.axis_size("dp") * group
    return pl.pallas_call(
        functools.partial(exchange_kernel, within, parts),
        out_shape=jax.ShapeDtypeStruct((count,) + x.shape[1 if parts else 0 :], x.dtype),
        in_specs=[pl.BlockSpec(memory_space=pltpu.VMEM)],
        out_specs=pl.BlockSpec(memory_space=pltpu.VMEM),
        scratch_shapes=[
            pltpu.SemaphoreType.DMA((count,)),
            pltpu.SemaphoreType.DMA((count,)),
            pltpu.SemaphoreType.DMA,
        ],
        compiler_params=pltpu.CompilerParams(collective_id=collective, has_side_effects=True),
        name=f"everyone_{collective}",
    )(x)


def pack(values):
    rows = values.reshape(values.shape[0], -1)
    return jnp.pad(rows, ((0, 0), (0, -rows.shape[1] % 1024))).reshape(rows.shape[0], -1, 128)


def unpack(values, shape):
    size = 1
    for length in shape:
        size *= length
    return values.reshape(values.shape[0], -1)[:, :size].reshape((values.shape[0],) + shape)


def attend_kernel(rows, block, masked, *refs):
    if masked:
        qkv_ref, bias_ref, o_ref, l_ref = refs
    else:
        qkv_ref, o_ref, l_ref = refs
    lane = lax.broadcasted_iota(jnp.int32, (1, 128), 1)
    low = lane < 64
    keys = qkv_ref[:, 128:256]
    values = qkv_ref[:, 256:384]
    for at in range(0, rows, block):
        queries = qkv_ref[at : at + block, :128]
        outs, totals = [], []
        for head in range(2):
            picked = jnp.where(low if head == 0 else ~low, queries, 0) * jnp.array(0.125, BF16)
            scores = dot_nt(picked, keys)
            if masked:
                scores = scores + bias_ref[at : at + block, :]
            highest = jnp.max(scores, -1, keepdims=True)
            exponent = jnp.exp(scores - highest)
            summed = jnp.sum(exponent, -1, keepdims=True)
            outs.append(dot(exponent.astype(BF16), values) * (1.0 / summed))
            totals.append(highest + jnp.log(summed))
        o_ref[at : at + block, :] = jnp.where(low, outs[0], outs[1]).astype(BF16)
        l_ref[at : at + block, :] = jnp.where(low, totals[0], totals[1])


def attend(qkv, bias, block):
    rows, width = qkv.shape
    pairs = width // 384
    specs = [pl.BlockSpec((rows, 384), lambda j: (0, j))]
    args = [qkv]
    if bias is not None:
        specs.append(pl.BlockSpec(bias.shape, lambda j: (0, 0)))
        args.append(bias)
    return pl.pallas_call(
        functools.partial(attend_kernel, rows, block, bias is not None),
        grid=(pairs,),
        out_shape=(
            jax.ShapeDtypeStruct((rows, pairs * 128), BF16),
            jax.ShapeDtypeStruct((rows, pairs * 128), F32),
        ),
        in_specs=specs,
        out_specs=(
            pl.BlockSpec((rows, 128), lambda j: (0, j)),
            pl.BlockSpec((rows, 128), lambda j: (0, j)),
        ),
        compiler_params=pltpu.CompilerParams(vmem_limit_bytes=VMEM_LIMIT),
        cost_estimate=pl.CostEstimate(
            flops=16 * rows * rows * 256 * pairs,
            bytes_accessed=rows * pairs * 128 * 12,
            transcendentals=2 * pairs * rows * rows,
        ),
        name=f"attend_{rows}",
    )(*args)


def attend_back_kernel(rows, block, masked, *refs):
    if masked:
        qkv_ref, do_ref, o_ref, l_ref, bias_ref, g_ref, dk_ref, dv_ref = refs
    else:
        qkv_ref, do_ref, o_ref, l_ref, g_ref, dk_ref, dv_ref = refs
    lane = lax.broadcasted_iota(jnp.int32, (1, 128), 1)
    low = lane < 64
    keys = qkv_ref[:, 128:256]
    values = qkv_ref[:, 256:384]
    keys_t = keys.astype(F32).T.astype(BF16)
    row = lax.broadcasted_iota(jnp.int32, (128, 1), 0)
    keys_of = [jnp.where(row < 64, keys_t, 0), jnp.where(row < 64, 0, keys_t)]
    eighth = jnp.array(0.125, BF16)
    for at in range(0, rows, block):
        queries = qkv_ref[at : at + block, :128]
        grads = do_ref[at : at + block, :]
        totals_t = l_ref[at : at + block, :].T
        product_t = (grads.astype(F32) * o_ref[at : at + block, :].astype(F32)).T
        grad_q = None
        for head in range(2):
            mask = low if head == 0 else ~low
            picked = jnp.where(mask, queries, 0) * eighth
            picked_grad = jnp.where(mask, grads, 0)
            total = totals_t[64 * head : 64 * head + 1, :]
            delta = jnp.sum(product_t[64 * head : 64 * head + 64, :], 0, keepdims=True)
            scores = dot_nt(keys, picked)
            if masked:
                scores = scores + bias_ref[:, at : at + block]
            weights = jnp.exp(scores - total)
            grad_weights = dot_nt(values, picked_grad)
            grad_scores = (weights * (grad_weights - delta)).astype(BF16)
            part_v = dot(weights.astype(BF16), picked_grad)
            part_k = dot(grad_scores, picked)
            if at == 0 and head == 0:
                dv_ref[...] = part_v
                dk_ref[...] = part_k
            else:
                dv_ref[...] += part_v
                dk_ref[...] += part_k
            part_q = dot(keys_of[head], grad_scores)
            grad_q = part_q if grad_q is None else grad_q + part_q
        g_ref[at : at + block, :128] = (grad_q.T * 0.125).astype(BF16)
    g_ref[:, 128:256] = dk_ref[...].astype(BF16)
    g_ref[:, 256:384] = dv_ref[...].astype(BF16)


def attend_back(qkv, grad_out, out, totals, bias, block):
    rows, width = qkv.shape
    pairs = width // 384
    specs = [
        pl.BlockSpec((rows, 384), lambda j: (0, j)),
        pl.BlockSpec((rows, 128), lambda j: (0, j)),
        pl.BlockSpec((rows, 128), lambda j: (0, j)),
        pl.BlockSpec((rows, 128), lambda j: (0, j)),
    ]
    args = [qkv, grad_out, out, totals]
    if bias is not None:
        specs.append(pl.BlockSpec(bias.shape, lambda j: (0, 0)))
        args.append(bias)
    return pl.pallas_call(
        functools.partial(attend_back_kernel, rows, block, bias is not None),
        grid=(pairs,),
        out_shape=jax.ShapeDtypeStruct(qkv.shape, BF16),
        in_specs=specs,
        out_specs=pl.BlockSpec((rows, 384), lambda j: (0, j)),
        scratch_shapes=[pltpu.VMEM((rows, 128), F32), pltpu.VMEM((rows, 128), F32)],
        compiler_params=pltpu.CompilerParams(vmem_limit_bytes=VMEM_LIMIT),
        cost_estimate=pl.CostEstimate(
            flops=40 * rows * rows * 256 * pairs,
            bytes_accessed=rows * pairs * 128 * 20,
            transcendentals=2 * pairs * rows * rows,
        ),
        name=f"attend_back_{rows}",
    )(*args)


def column_runs(features, width):
    runs = [
        (kind * features + pair * 128, (3 * pair + kind) * 128, 128)
        for pair in range(features // 128)
        for kind in range(3)
    ]
    return runs + [(3 * features, 3 * features, width - 3 * features)]


def gradient_runs(features, width):
    half = features // 2
    upper = width - 4 * features
    runs = column_runs(features, width)[:-1]
    towers = []
    for piece, upper_at in ((2, upper), (3, 0)):
        tower = []
        for begin, at, size in runs:
            side, local = divmod(at, 3 * half)
            spots = [4 * half * (side ^ core) + local for core in range(2)]
            tower.append((piece, *spots, begin, size))
        for side in range(2):
            spots = [4 * half * (side ^ core) + 3 * half for core in range(2)]
            tower.append((piece, *spots, 3 * features + side * half, half))
        tower.append((0, upper_at, upper_at, 4 * features, upper))
        towers.append(tower)
    tower = [(1, at, at, begin, size) for begin, at, size in runs]
    tower.append((1, 3 * features, 3 * features, 3 * features, width - 3 * features))
    return towers + [tower]


def regroup_kernel(runs, w_ref, low_ref):
    for begin, at, size in runs:
        low_ref[0, :, at : at + size] = w_ref[0, :, begin : begin + size].astype(BF16)


def regroup(mixing, features):
    towers, rows, width = mixing.shape
    spec = pl.BlockSpec((1, rows, width), lambda t: (t, 0, 0))
    return pl.pallas_call(
        functools.partial(regroup_kernel, column_runs(features, width)),
        grid=(towers,),
        out_shape=jax.ShapeDtypeStruct((towers, rows, width), BF16),
        in_specs=[spec],
        out_specs=spec,
        compiler_params=pltpu.CompilerParams(vmem_limit_bytes=VMEM_LIMIT),
        name="regroup",
    )(mixing)


def adam_kernel(towers, scal_ref, core_ref, *refs):
    pieces, (w_ref, first_ref, second_ref), outs = refs[:4], refs[4:7], refs[7:]
    factor = scal_ref[0]
    for tower, runs in enumerate(towers):
        for core in range(2):

            @pl.when((pl.program_id(0) == tower) & (core_ref[0] == core))
            def _():
                for run in runs:
                    piece, begin, size = run[0], run[3], run[4]
                    at = run[1 + core]
                    new = adam_update(
                        w_ref[0, :, begin : begin + size],
                        first_ref[0, :, begin : begin + size],
                        second_ref[0, :, begin : begin + size],
                        pieces[piece][:, at : at + size] * factor,
                        RATES[0],
                    )
                    for out, value in zip(outs, new):
                        out[0, :, begin : begin + size] = value


def adam_mixing(factor, core, pieces, master, first, second, features):
    towers, rows, width = master.shape
    spec = pl.BlockSpec((1, rows, width), lambda t: (t, 0, 0))
    scalar = pl.BlockSpec(memory_space=pltpu.SMEM)
    return pl.pallas_call(
        functools.partial(adam_kernel, gradient_runs(features, width)),
        grid=(towers,),
        out_shape=(jax.ShapeDtypeStruct(master.shape, F32),) * 3,
        in_specs=[scalar, scalar]
        + [pl.BlockSpec(piece.shape, lambda t: (0, 0)) for piece in pieces]
        + [spec] * 3,
        out_specs=(spec,) * 3,
        compiler_params=pltpu.CompilerParams(vmem_limit_bytes=VMEM_LIMIT),
        name="adam_mixing",
    )(factor.reshape(1), core.reshape(1).astype(jnp.int32), *pieces, master, first, second)


def scale_kernel(first_ref, second_ref, slopes_ref, out_ref):
    width = first_ref.shape[1]
    for at, ref in enumerate((first_ref, second_ref)):
        part = ref[...].astype(F32) * slopes_ref[at : at + 1, :]
        out_ref[:, at * width : (at + 1) * width] = part.astype(BF16)


def scale_columns(first, second, slopes):
    rows, width = first.shape
    block = rows // 6
    spec = pl.BlockSpec((block, width), lambda j: (j, 0))
    return pl.pallas_call(
        scale_kernel,
        grid=(rows // block,),
        out_shape=jax.ShapeDtypeStruct((rows, 2 * width), BF16),
        in_specs=[spec, spec, pl.BlockSpec(slopes.shape, lambda j: (0, 0))],
        out_specs=pl.BlockSpec((block, 2 * width), lambda j: (j, 0)),
        compiler_params=pltpu.CompilerParams(vmem_limit_bytes=VMEM_LIMIT),
        name="scale_columns",
    )(first, second, slopes)


def patch_kernel(tile, video_ref, entry_ref, out_ref):
    patch = video_ref.shape[2]
    for at in range(0, patch, tile):
        out_ref[at : at + tile, :] = dot_tn(video_ref[0, :, at : at + tile], entry_ref[...]).astype(
            BF16
        )
    out_ref[patch:, :] = jnp.zeros((out_ref.shape[0] - patch, out_ref.shape[1]), BF16)


def patch_grads(video, entry, rows):
    return pl.pallas_call(
        functools.partial(patch_kernel, 512),
        out_shape=jax.ShapeDtypeStruct((rows, entry.shape[1]), BF16),
        in_specs=[pl.BlockSpec(memory_space=pltpu.VMEM)] * 2,
        out_specs=pl.BlockSpec(memory_space=pltpu.VMEM),
        compiler_params=pltpu.CompilerParams(vmem_limit_bytes=VMEM_LIMIT),
        name="patch_grads",
    )(video, entry)


def middle_kernel(
    scales, yv_ref, ya_ref, yt_ref, gains_ref, heads_ref, vt_ref, live_ref, pos_ref, count_ref,
    loss_ref, dv_ref, da_ref, dt_ref, gg_ref, z_ref, zt_ref, de_ref, dt_e_ref, ev_ref, dvt_ref,
):
    clips = yv_ref.shape[0]
    joint = vt_ref.shape[0]

    def times(a, b, dims):
        return lax.dot_general(
            a, b, (dims, ((), ())), precision=FULL_PRECISION, preferred_element_type=F32
        )

    plain, right, left = ((1,), (0,)), ((1,), (1,)), ((0,), (0,))

    def normalise(values):
        centred = values - jnp.mean(values, -1, keepdims=True)
        inverse = lax.rsqrt(jnp.mean(centred * centred, -1, keepdims=True) + 1e-06)
        return centred * inverse, inverse

    def unit(values):
        scale = lax.rsqrt(jnp.sum(values * values, -1, keepdims=True) + 1e-06)
        return values * scale, scale

    def unit_back(values, scale, grads):
        along = jnp.sum(values * grads, -1, keepdims=True)
        return scale * grads - values * (scale * scale * scale * along)

    def soft(scores):
        highest = jnp.max(scores, -1, keepdims=True)
        exponent = jnp.exp(scores - highest)
        total = jnp.sum(exponent, -1, keepdims=True)
        return highest + jnp.log(total), exponent * (1.0 / total)

    hats, z = [], []
    for t, ref in enumerate((yv_ref, ya_ref, yt_ref)):
        hat, inverse = normalise(ref[...])
        hats.append((hat, inverse))
        z.append(hat * gains_ref[2 * t : 2 * t + 1, :] + gains_ref[2 * t + 1 : 2 * t + 2, :])
    heads = heads_ref[...]
    parts = (heads[:, :joint], heads[:, joint : 2 * joint], heads[:, 2 * joint :])
    video_text = vt_ref[...]
    e_video = times(z[0], parts[0], plain)
    e_both = times(e_video, video_text, plain)
    e_audio = times(z[1], parts[1], plain)
    e_text = times(z[2], parts[2], plain)
    (n_video, s_video), (n_both, s_both) = unit(e_video), unit(e_both)
    (n_audio, s_audio), (n_text, s_text) = unit(e_audio), unit(e_text)
    scores = times(n_video, n_audio, right) / SOFTMAX_WARMTH
    own = lax.broadcasted_iota(jnp.int32, scores.shape, 0) == lax.broadcasted_iota(
        jnp.int32, scores.shape, 1
    )
    total, share = soft(scores)
    matched = total - jnp.sum(jnp.where(own, scores, 0.0), -1, keepdims=True)
    d_scores = (share - jnp.where(own, 1.0, 0.0)) * (1.0 / (clips * SOFTMAX_WARMTH))
    live = live_ref[...]
    positive = pos_ref[...]
    text_scores = times(n_both, n_text, right) / SOFTMAX_WARMTH
    every, every_share = soft(jnp.where(live > 0.5, text_scores, -1e30))
    chosen, chosen_share = soft(jnp.where(positive > 0.5, text_scores, -1e30))
    weight = jnp.sum(positive, -1, keepdims=True) / jnp.sum(live)
    loss = jnp.sum(matched) / clips + jnp.sum(weight * (every - chosen))
    loss_ref[...] = jnp.broadcast_to(loss, loss_ref.shape)
    d_text_scores = (every_share * live - chosen_share * positive) * (weight / SOFTMAX_WARMTH)
    d_video = unit_back(e_video, s_video, times(d_scores, n_audio, plain))
    d_audio = unit_back(e_audio, s_audio, times(d_scores, n_video, left))
    d_both = unit_back(e_both, s_both, times(d_text_scores, n_text, plain))
    d_text = unit_back(e_text, s_text, times(d_text_scores, n_both, left))
    d_video = d_video + times(d_both, video_text, right)
    for t, (grad, out) in enumerate(((d_video, dv_ref), (d_audio, da_ref), (d_text, dt_ref))):
        d_z = times(grad, parts[t], right)
        hat, inverse = hats[t]
        gg_ref[2 * t : 2 * t + 1, :] = jnp.sum(d_z * hat, 0, keepdims=True)
        gg_ref[2 * t + 1 : 2 * t + 2, :] = jnp.sum(d_z, 0, keepdims=True)
        d_hat = d_z * gains_ref[2 * t : 2 * t + 1, :]
        inner = d_hat - jnp.mean(d_hat, -1, keepdims=True)
        rows = inverse * (inner - hat * jnp.mean(d_hat * hat, -1, keepdims=True))
        out[...] = rows * scales[t] if t < 2 else rows / count_ref[...]
    z_ref[0] = z[0]
    z_ref[1] = z[1]
    zt_ref[...] = z[2]
    de_ref[0] = d_video
    de_ref[1] = d_audio
    dt_e_ref[...] = d_text
    ev_ref[...] = e_video
    dvt_ref[...] = d_both


def contrast(scales, rows, gains, heads, video_text, live, positive, counts):
    clips, features = rows[0].shape
    texts = rows[2].shape[0]
    joint, width = video_text.shape
    shapes = [
        (8, 128),
        (clips, features),
        (clips, features),
        (texts, features),
        (8, features),
        (2, clips, features),
        (texts, features),
        (2, clips, joint),
        (texts, width),
        (clips, joint),
        (clips, width),
    ]
    return pl.pallas_call(
        functools.partial(middle_kernel, scales),
        out_shape=tuple(jax.ShapeDtypeStruct(shape, F32) for shape in shapes),
        in_specs=[pl.BlockSpec(memory_space=pltpu.VMEM)] * 9,
        out_specs=tuple(pl.BlockSpec(memory_space=pltpu.VMEM) for _ in shapes),
        compiler_params=pltpu.CompilerParams(vmem_limit_bytes=VMEM_LIMIT),
        name="middle",
    )(*rows, gains, heads, video_text, live, positive, counts)


def feed_kernel(with_product, h_ref, w_ref, sel_ref, slope_ref, sums_ref, *rest):
    hidden = dot(h_ref[...], w_ref[...])
    root = 0.7978845608028654
    square = hidden * hidden
    tang = jnp.tanh(root * hidden * (1.0 + 0.044715 * square))
    half = 0.5 * (1.0 + tang)
    active = (hidden * half).astype(BF16)
    slope = half + (0.5 * root) * hidden * (1.0 - tang * tang) * (1.0 + (3 * 0.044715) * square)
    slope = slope.astype(BF16)
    slope_ref[...] = slope
    if with_product:
        sums_ref[...] = jnp.broadcast_to(
            jnp.sum(active.astype(F32), 0, keepdims=True), sums_ref.shape
        )
        rest[0][...] = dot_tn(h_ref[...], slope).astype(BF16)
    else:
        sums_ref[...] = dot(sel_ref[...], active)


def feed(normed, weight, column, select, tile, with_product):
    rows, features = normed.shape
    width = weight.shape[1] - column
    first = column // tile
    shapes = [
        jax.ShapeDtypeStruct((rows, width), BF16),
        jax.ShapeDtypeStruct((8, width), F32),
    ]
    outs = [
        pl.BlockSpec((rows, tile), lambda j: (0, j)),
        pl.BlockSpec((8, tile), lambda j: (0, j)),
    ]
    if with_product:
        shapes.append(jax.ShapeDtypeStruct((features, width), BF16))
        outs.append(pl.BlockSpec((features, tile), lambda j: (0, j)))
    return pl.pallas_call(
        functools.partial(feed_kernel, with_product),
        grid=(width // tile,),
        out_shape=tuple(shapes),
        in_specs=[
            pl.BlockSpec((rows, features), lambda j: (0, 0)),
            pl.BlockSpec((features, tile), lambda j: (0, first + j)),
            pl.BlockSpec(select.shape, lambda j: (0, 0)),
        ],
        out_specs=tuple(outs),
        compiler_params=pltpu.CompilerParams(vmem_limit_bytes=VMEM_LIMIT),
        cost_estimate=pl.CostEstimate(
            flops=4 * rows * features * width,
            bytes_accessed=2 * features * width * 2 + 2 * rows * width,
            transcendentals=rows * width,
        ),
        name=f"feed_{rows}",
    )(normed, weight, select)


def both_columns(own, other, core):
    first = jnp.where(core == 0, own, other)
    second = jnp.where(core == 0, other, own)
    return jnp.concatenate([first, second], -1)


def attention_forward(stream, bias, mixing, gains, block):
    features = stream.shape[1]
    normed = norm_rows(stream, gains[0], gains[1]).astype(BF16)
    joined = dot(normed, mixing[:, : 3 * features]).astype(BF16)
    return normed, joined, attend(joined, bias, block)


def feed_forward(stream, mixed, mixing, gains, select, with_product):
    features = stream.shape[1]
    middle = stream + dot(mixed, mixing[:, 3 * features : 4 * features])
    normed = norm_rows(middle, gains[2], gains[3]).astype(BF16)
    return middle, normed, feed(normed, mixing, 4 * features, select, 512, with_product)


def output_backward(grad_rows, grad_normed, mixed, middle, mixing, gains):
    features = middle.shape[1]
    grad_norm, grad_gain, grad_shift = jax.vjp(norm_rows, middle, gains[2], gains[3])[1](
        grad_normed
    )
    grad_middle = grad_rows + grad_norm
    grad_attention = grad_middle.astype(BF16)
    grad_mixed = dot_nt(grad_attention, mixing[:, 3 * features : 4 * features]).astype(BF16)
    grad_output = dot_tn(mixed, grad_attention).astype(BF16)
    return grad_middle, grad_output, grad_mixed, [grad_gain, grad_shift]


def input_backward(grad_middle, grad_joined, stream, mixing, gains):
    features = stream.shape[1]
    grad_normed = dot_nt(grad_joined, mixing[:, : 3 * features])
    grad_norm, grad_gain, grad_shift = jax.vjp(norm_rows, stream, gains[0], gains[1])[1](
        grad_normed
    )
    return (grad_middle + grad_norm).astype(BF16), [grad_gain, grad_shift]


def both_columns(own, other, core):
    first = jnp.where(core == 0, own, other)
    second = jnp.where(core == 0, other, own)
    return jnp.concatenate([first, second], -1)


class Links:
    def __init__(self):
        self.group = lax.axis_size("fsdp")
        self.replicas = lax.axis_size("dp")
        self.member = lax.axis_index("fsdp")
        self.replica = lax.axis_index("dp")
        self.core = self.member % 2
        self.paired = self.group == 16 and self.replicas == 2

    def swap(self, values, name):
        if name == "y":
            return lax.ppermute(values, "dp", [(0, 1), (1, 0)])
        bit = {"core": 1, "x": 2, "near": 4, "far": 8}[name]
        return lax.ppermute(values, "fsdp", [(f, f ^ bit) for f in range(self.group)])

    def bit(self, name):
        if name == "y":
            return self.replica
        return (self.member // {"core": 1, "x": 2, "near": 4, "far": 8}[name]) % 2

    def merge(self, values, other, names, name, order=("far", "near", "x", "core", "y")):
        names = sorted(names + [name], key=order.index)
        at = names.index(name)
        place = lax.broadcasted_iota(jnp.int32, (2,) + (1,) * (values.ndim - at), 0)
        joined = jnp.where(
            place == self.bit(name), jnp.expand_dims(values, at), jnp.expand_dims(other, at)
        )
        return joined, names

    def sides(self, values, names, name):
        at = names.index(name)
        bit = self.bit(name)
        give = lax.dynamic_index_in_dim(values, 1 - bit, at, keepdims=False)
        keep = lax.dynamic_index_in_dim(values, bit, at, keepdims=False)
        return keep, give, [n for n in names if n != name]

    def gather_clips(self, values):
        if not self.paired:
            return lax.all_gather(values, ("dp", "fsdp"), axis=0, tiled=True)
        names = []
        order = ["y", "far", "near", "x", "core"]
        for name in ("near", "far", "y", "x", "core"):
            other = yield values, name
            values, names = self.merge(values, other, names, name, order)
        return values.reshape(-1, values.shape[-1])

    def sum_replicas(self, part):
        if not self.paired:
            return lax.psum(part, "dp").astype(F32)
        other = yield part, "y"
        return part.astype(F32) + other.astype(F32)

    def gather_rows(self, shard, order):
        rows, width = shard.shape
        half = width // 2
        if not self.paired:
            return lax.all_gather(shard, "fsdp", axis=0, tiled=True)
        values = lax.dynamic_slice_in_dim(shard, self.replica * half, half, 1)
        names = []
        for name in order + ("core",):
            other = yield values, name
            if name == "y":
                values = both_columns(values, other, self.replica)
            else:
                values, names = self.merge(values, other, names, name)
        return values.reshape(self.group * rows, width)

    def reduce_columns(self, own, other, order):
        rows, half = own.shape
        part = rows // self.group
        other = yield other, "core"
        values = add(own, other).reshape(2, 2, 2, 2, 2, part // 2, half)
        names = ["far", "near", "x", "core", "y"]
        for name in order:
            keep, give, names = self.sides(values, names, name)
            other = yield give, name
            values = add(keep, other)
        return values

    def share_columns(self, values):
        mine, give, _ = self.sides(values, ["core"], "core")
        other = yield give, "core"
        values = jnp.concatenate([mine, other], 1)
        other = yield values, "y"
        values, _ = self.merge(values, other, [], "y")
        return values.reshape(2 * values.shape[1], values.shape[2]).astype(F32)

    def scatter_columns(self, own, other, order):
        if not self.paired:
            half = own.shape[1]
            core = self.core
            whole = both_columns(own, other, core)
            whole = lax.psum_scatter(whole, "fsdp", scatter_dimension=0, tiled=True)
            whole = lax.psum(whole, "dp").astype(F32)
            return jnp.concatenate(
                [
                    lax.dynamic_slice_in_dim(whole, core * half, half, 1),
                    lax.dynamic_slice_in_dim(whole, (1 - core) * half, half, 1),
                ],
                1,
            )
        values = yield from self.reduce_columns(own, other, order)
        return (yield from self.share_columns(values))

    def scatter_rows(self, values, order):
        rows, width = values.shape
        part = rows // self.group
        half = width // 2
        if not self.paired:
            part_sum = lax.psum_scatter(values, "fsdp", scatter_dimension=0, tiled=True)
            return lax.psum(part_sum, "dp").astype(F32)
        values = values.reshape(2, 2, 2, 2, part, width)
        names = ["far", "near", "x", "core"]
        for name in ("core",) + order:
            if name == "y":
                last = values.ndim - 1
                give = lax.dynamic_slice_in_dim(values, (1 - self.replica) * half, half, last)
                keep = lax.dynamic_slice_in_dim(values, self.replica * half, half, last)
            else:
                keep, give, names = self.sides(values, names, name)
            other = yield give, name
            values = add(keep, other)
        other = yield values, "y"
        return both_columns(values, other, self.replica).astype(F32)

    def scatter_words(self, values):
        rows, width = values.shape
        if not self.paired:
            return lax.psum_scatter(values, "fsdp", scatter_dimension=0, tiled=True)
        values = values.reshape(2, 2, 2, 2, rows // self.group, width)
        names = ["far", "near", "x", "core"]
        for name in ("core", "x", "far", "near"):
            keep, give, names = self.sides(values, names, name)
            other = yield give, name
            values = add(keep, other)
        return values

    def stage(self, flows, work=None, inputs=()):
        active = [flow for flow in flows if flow.request is not None]
        names = [flow.request[1] for flow in active]
        held, inputs = lax.optimization_barrier(([flow.request[0] for flow in active], inputs))
        sent = [self.swap(values, name) for values, name in zip(held, names)]
        made = work(*inputs) if work is not None else ()
        sent, made = lax.optimization_barrier((sent, made))
        for flow, other in zip(active, sent):
            flow.push(other)
        return made


class Flow:
    def __init__(self, steps):
        self.steps = steps
        self.value = None
        self.push(None)

    def push(self, other):
        try:
            self.request = self.steps.send(other)
        except StopIteration as end:
            self.request, self.value = None, end.value


def add(left, right):
    return (left.astype(F32) + right.astype(F32)).astype(BF16)


def body(
    video,
    audio,
    word_ids,
    word_counts,
    caption_counts,
    caption_clips,
    mixing_in,
    mixing_in_first,
    mixing_in_second,
    mixing_out,
    mixing_out_first,
    mixing_out_second,
    norm_params,
    norm_params_first,
    norm_params_second,
    input_embed,
    input_embed_first,
    input_embed_second,
    word_table,
    word_table_first,
    word_table_second,
    head_proj,
    head_proj_first,
    head_proj_second,
    video_text_proj,
    video_text_proj_first,
    video_text_proj_second,
):
    group = lax.axis_size("fsdp")
    replicas = lax.axis_size("dp")
    clips = group * replicas
    member = lax.axis_index("fsdp")
    replica = lax.axis_index("dp")
    clip = replica * group + member
    captions, slots = word_ids.shape[1:]
    words = captions * slots
    patch = video.shape[2]
    video_count, audio_count = video.shape[1], audio.shape[1]
    features = mixing_in.shape[1] * group
    pairs = features // 128
    shard = mixing_in.shape[1]
    qkv = 3 * features

    links = Links()
    core = links.core
    half = features // 2
    joint_part, text_width = video_text_proj.shape
    table_rows = word_table.shape[0]
    gain_part = norm_params.shape[2]
    wave = audio.shape[2]
    low = regroup(mixing_in, features)

    def gather(values):
        return lax.all_gather(values, "fsdp", axis=0, tiled=True)

    weights = [None] * 3
    weights[1] = gather(low[1])
    embed_flow = Flow(links.gather_rows(input_embed.astype(BF16), ("near", "far", "x", "y")))

    def exchange(*parts):
        packed = jnp.concatenate([part.reshape(-1).astype(F32) for part in parts])
        packed = jnp.pad(packed, (0, -packed.shape[0] % 1024)).reshape(-1, 128)
        return everyone(packed, 0).reshape(clips, -1)

    every = links.stage(
        [embed_flow],
        exchange,
        (word_ids, word_counts, caption_counts, caption_clips, norm_params),
    )
    all_ids = every[:, :words].astype(jnp.int32)
    at = words + captions
    all_caption_counts = every[:, at].astype(jnp.int32)
    all_counts = every[:, words : words + captions]
    all_caption_clips = every[:, at + 1 : at + 1 + captions].astype(jnp.int32)
    at = at + 1 + captions
    gains_all = (
        every[:group, at : at + 18 * gain_part]
        .reshape(group, 3, 6, gain_part)
        .transpose(1, 2, 0, 3)
        .reshape(3, 6, features)
        .astype(BF16)
        .astype(F32)
    )

    def owned_rows(ids):
        local_ids = ids - member * table_rows
        owned = (local_ids >= 0) & (local_ids < table_rows)
        return jnp.clip(local_ids, 0, table_rows - 1), owned

    def pick_words(ids):
        group_ids = lax.dynamic_slice_in_dim(ids, replica * group, group, 0).reshape(-1)
        local_ids, owned = owned_rows(group_ids)
        return jnp.where(owned[:, None], word_table[local_ids], 0.0).astype(BF16)

    picked = links.stage([embed_flow], pick_words, (all_ids,))
    words_flow = Flow(links.scatter_words(picked))

    valid = jnp.arange(slots)[None, :] < word_counts[0][:, None]
    flat_valid = valid.reshape(-1)
    caption_of = jnp.arange(words) // slots
    allowed = (caption_of[:, None] == caption_of[None, :]) & flat_valid[None, :]
    word_bias = jnp.where(allowed, 0.0, -1000000000.0).astype(F32)
    select = ((jnp.arange(8)[:, None] == caption_of[None, :]) & flat_valid[None, :]).astype(BF16)
    unused = jnp.zeros((8, 128), BF16)

    biases = (None, None, word_bias)
    selects = (unused, unused, select)
    forward_block = (512, 512, words)
    backward_block = (512, 256, words)
    counts = word_counts[0].astype(F32)

    normed, joined, attended, fed, streams = ([None] * 3 for _ in range(5))
    for _ in range(3):
        links.stage([embed_flow, words_flow])
    embed = embed_flow.value
    streams[1], streams[0] = links.stage(
        [words_flow],
        lambda rows: (dot(audio[0], rows[patch:]), dot(video[0], rows[:patch])),
        (embed,),
    )
    heads_low = jnp.concatenate(
        [head_proj, jnp.pad(video_text_proj, ((0, shard - joint_part), (0, 0)))], 1
    ).astype(BF16)
    streams[2] = words_flow.value.astype(F32)

    def forward(tower):
        normed[tower], joined[tower], attended[tower] = attention_forward(
            streams[tower],
            biases[tower],
            weights[tower],
            gains_all[tower],
            forward_block[tower],
        )
        fed[tower] = feed_forward(
            streams[tower],
            attended[tower][0],
            weights[tower],
            gains_all[tower],
            selects[tower],
            tower < 2,
        )

    streams, weights[1], low_video, low_text = lax.optimization_barrier(
        (streams, weights[1], low[0], low[2])
    )
    weights[0] = gather(low_video)
    weights[2] = gather(low_text)
    forward(1)
    fed[1], weights[0] = lax.optimization_barrier((fed[1], weights[0]))
    forward(0)
    fed[0], weights[2], heads_low = lax.optimization_barrier((fed[0], weights[2], heads_low))
    heads_all = gather(heads_low)
    forward(2)

    heads = heads_all[:, : head_proj.shape[1]].astype(F32)
    video_text = heads_all[:, head_proj.shape[1] :].reshape(group, shard, text_width)
    video_text = video_text[:, :joint_part].reshape(group * joint_part, text_width).astype(F32)
    slopes, sums, products, bases = [], [], [], []
    for tower in range(3):
        rows, _, parts = fed[tower]
        slopes.append(parts[0])
        if tower < 2:
            products.append(parts[2])
            sums.append(parts[1][:1])
            bases.append(jnp.sum(rows, 0, keepdims=True))
        else:
            sums.append(parts[1][:captions])
            bases.append(full(select[:captions].astype(F32), rows))

    token_count = 2 + captions
    back_part = mixing_out.shape[1]
    backs = mixing_out.astype(BF16).astype(F32)
    hidden = back_part * group
    summed = jnp.concatenate(sums, 0).reshape(token_count, group, back_part).transpose(1, 0, 2)
    every_sum = unpack(everyone(pack(summed), 3, parts=True), (token_count, back_part))

    def own_group(values):
        return lax.dynamic_slice_in_dim(values, replica * group, group, 0)

    def by_tower(values):
        width = values.shape[-1]
        return values[:, 0], values[:, 1], values[:, 2:].reshape(-1, width)

    def by_clip(parts):
        count, width = parts[0].shape
        return jnp.concatenate(
            [parts[0][:, None], parts[1][:, None], parts[2].reshape(count, captions, width)], 1
        )

    group_sums = by_tower(own_group(every_sum))
    partial = by_clip([full(group_sums[t], backs[t]) for t in range(3)])
    through = everyone(pack(partial), 4, within=True, parts=True)
    through = unpack(jnp.sum(through, 0, keepdims=True), (token_count, features))[0]
    scales = jnp.concatenate([jnp.array([video_count, audio_count], F32), counts])
    mine = (jnp.concatenate(bases, 0) + through) / scales[:, None]

    pooled = unpack(everyone(pack(mine[None])[0], 1), (token_count * features,))
    live = (jnp.arange(captions)[None, :] < all_caption_counts[:, None]).reshape(1, -1)
    positive = live & (all_caption_clips.reshape(1, -1) == jnp.arange(clips)[:, None])
    outer_rows = jnp.pad(gains_all[:, 4:].reshape(6, features), ((0, 2), (0, 0)))
    (
        loss,
        *grad_rows_all,
        outer_grads,
        z_pair,
        z_text,
        d_pair,
        d_text,
        embed_video,
        d_video_text,
    ) = contrast(
        (1.0 / video_count, 1.0 / audio_count),
        (
            pooled[:, :features],
            pooled[:, features : 2 * features],
            pooled[:, 2 * features :].reshape(-1, features),
        ),
        outer_rows,
        heads,
        video_text,
        live.astype(F32),
        positive.astype(F32),
        all_counts.reshape(-1, 1),
    )
    loss = loss[0, 0]
    z = (z_pair[0], z_pair[1], z_text)
    d_heads = (d_pair[0], d_pair[1], d_text)

    def own_columns(values):
        return lax.dynamic_slice_in_dim(values, member * shard, shard, 1)

    def head_grads():
        heads_grad = jnp.concatenate([full(own_columns(z[t]).T, d_heads[t]) for t in range(3)], 1)
        own = lax.dynamic_slice_in_dim(embed_video, member * joint_part, joint_part, 1)
        return heads_grad, full(own.T, d_video_text)

    branch_all = [rows.astype(BF16) for rows in grad_rows_all]

    all_sums = by_tower(every_sum)

    def back_grads():
        return jnp.stack([full(all_sums[t].T, branch_all[t].astype(F32)) for t in range(3)])

    group_branch = by_clip(branch_all)
    group_branch = by_tower(own_group(group_branch).astype(F32))
    partial = by_clip([dot_nt_full(group_branch[t], backs[t]) for t in range(3)])
    sloped = unpack(everyone(pack(partial), 5, within=True, parts=True), (token_count, back_part))
    sloped = sloped.transpose(1, 0, 2).reshape(token_count, hidden)
    own_slopes = (sloped[:1], sloped[1:2], sloped[2:])

    def own_rows(values, per_clip):
        return lax.dynamic_slice_in_dim(values, clip * per_clip, per_clip, 0)

    own_grads = [own_rows(grad_rows_all[t], 1 if t < 2 else captions) for t in range(3)]
    ups = scale_columns(products[1], products[0], jnp.concatenate(own_slopes[1::-1], 0))
    ups, own_slopes = lax.optimization_barrier((ups, own_slopes))
    up_part = lax.psum_scatter(ups, "fsdp", scatter_dimension=0, tiled=True)
    first, second = ("y", "x", "far", "near"), ("x", "y", "far", "near")

    def halves(inward, outward):
        return [
            jnp.concatenate(
                [
                    lax.dynamic_slice_in_dim(inward, at * 3 * half, 3 * half, 1),
                    lax.dynamic_slice_in_dim(outward, at * half, half, 1),
                ],
                1,
            )
            for at in (core, 1 - core)
        ]

    def hidden_backward(tower, slope):
        upper = weights[tower][:, 4 * features :]
        if tower == 2:
            spread = select[:captions].astype(F32).T
            grad_hidden = (slopes[2].astype(F32) * full(spread, slope)).astype(BF16)
            up = dot_tn(fed[2][1], grad_hidden).astype(BF16)
            return full(spread, own_grads[2]), dot_nt(grad_hidden, upper), up
        scaled = (upper.astype(F32) * slope).astype(BF16)
        return own_grads[tower], dot_nt(slopes[tower], scaled), None

    def outward_backward(tower, slope):
        rows_grad, grads, up = hidden_backward(tower, slope)
        made = output_backward(
            rows_grad, grads, attended[tower][0], fed[tower][0], weights[tower], gains_all[tower]
        )
        return made, up

    def inner_backward(tower, grad_mixed):
        turned = None if biases[tower] is None else biases[tower].T
        return attend_back(
            joined[tower],
            grad_mixed,
            attended[tower][0],
            attended[tower][1],
            turned,
            backward_block[tower],
        )

    def entry_backward(tower, grad_middle, grad_joined):
        return input_backward(
            grad_middle, grad_joined, streams[tower], weights[tower], gains_all[tower]
        )

    gains_grads = [None] * 3

    def text_backward(slope):
        made, up = outward_backward(2, slope)
        grad_joined = inner_backward(2, made[2])
        inward = dot_tn(normed[2], grad_joined).astype(BF16)
        entry, entry_gains = entry_backward(2, made[0], grad_joined)
        return jnp.concatenate([inward, made[1], up], 1), entry, entry_gains + made[3]

    text_grad, entry, gains_grads[2] = links.stage([], text_backward, (own_slopes[2],))
    word_flow = Flow(links.gather_clips(entry))
    text_part = lax.psum_scatter(text_grad, "fsdp", scatter_dimension=0, tiled=True)
    made_video, _ = links.stage([word_flow], lambda slope: outward_backward(0, slope), (own_slopes[0],))
    embed_rows = input_embed.shape[0] * group

    def video_inner(grad_mixed):
        grad_joined = inner_backward(0, grad_mixed)
        inward = dot_tn(normed[0], grad_joined).astype(BF16)
        entry, entry_gains = entry_backward(0, made_video[0], grad_joined)
        return halves(inward, made_video[1]), entry, entry_gains

    video_parts, entry, entry_gains = links.stage([word_flow], video_inner, (made_video[2],))
    gains_grads[0] = entry_gains + made_video[3]
    video_flow = Flow(links.scatter_columns(*video_parts, first))

    def video_entry(entry, slope):
        made, _ = outward_backward(1, slope)
        return patch_grads(video, entry, embed_rows), made

    grad_embed, made_audio = links.stage([word_flow, video_flow], video_entry, (entry, own_slopes[1]))
    embed_flow = Flow(links.scatter_rows(grad_embed, first))
    rest = [word_flow, video_flow, embed_flow]
    joined_audio = links.stage(rest, lambda part: inner_backward(1, part), (made_audio[2],))

    def audio_inward(grad_joined):
        return halves(dot_tn(normed[1], grad_joined).astype(BF16), made_audio[1])

    audio_parts = links.stage(rest, audio_inward, (joined_audio,))
    cut = features
    if links.paired:
        audio_flows = [
            Flow(links.reduce_columns(*[part[:, :cut] for part in audio_parts], first)),
            Flow(links.reduce_columns(*[part[:, cut:] for part in audio_parts], second)),
        ]
    else:
        audio_flows = [Flow(links.scatter_columns(*audio_parts, first))]
    rest += audio_flows

    def audio_entry(grad_joined):
        entry, entry_gains = entry_backward(1, made_audio[0], grad_joined)
        wave_grad = dot_tn(entry, audio[0]).astype(BF16)
        every_gain = jnp.stack(gains_grads[0] + entry_gains + made_audio[3] + gains_grads[2])
        every_gain = jnp.pad(every_gain, ((0, wave - every_gain.shape[0]), (0, 0)))
        gain_columns = every_gain.T.astype(BF16)
        return (
            jnp.where(core == 0, wave_grad, gain_columns),
            jnp.where(core == 0, gain_columns, wave_grad),
        )

    beside = links.stage(rest, audio_entry, (joined_audio,))
    beside_flow = Flow(
        links.reduce_columns(*beside, second)
        if links.paired
        else links.scatter_columns(*beside, first)
    )
    rest += [beside_flow]

    def scatter_table(every_word):
        local_ids, owned = owned_rows(all_ids.reshape(-1))
        return jax.ops.segment_sum(
            jnp.where(owned[:, None], every_word.astype(F32), 0.0),
            local_ids,
            num_segments=table_rows,
        )

    def squared(*values):
        return sum(jnp.sum(value * value) for value in values)

    table_grad = links.stage(rest, scatter_table, (word_flow.value,))
    back_grad, (heads_grad, video_text_grad), table_square = links.stage(
        rest, lambda table: (back_grads(), head_grads(), squared(table)), (table_grad,)
    )
    up_flow = Flow(links.sum_replicas(up_part))
    rest += [up_flow]
    small_square = links.stage(rest, squared, (back_grad, heads_grad, video_text_grad))
    links.stage(rest)
    text_flow = Flow(links.sum_replicas(text_part))
    if links.paired:
        values = jnp.concatenate([flow.value for flow in audio_flows], 2)
        audio_flows = [Flow(links.share_columns(values))]
    rest += audio_flows + [text_flow]
    for _ in range(4):
        if any(flow.request is not None for flow in rest):
            links.stage(rest)
    pieces = (up_flow.value, text_flow.value, video_flow.value, audio_flows[0].value)
    embed_grad = embed_flow.value

    outer = lax.dynamic_slice_in_dim(outer_grads[:6], member * gain_part, gain_part, 1)
    local_square = table_square + small_square + squared(*pieces, embed_grad, outer)
    piece = beside_flow.value.reshape(-1, wave)
    piece_square = squared(piece.astype(F32))
    marks = jnp.where(jnp.arange(128) < 64, local_square, piece_square)
    mark_rows = []
    for _ in range(3):
        mark_rows.append(marks.astype(BF16))
        marks = marks - mark_rows[-1].astype(F32)
    mark_rows = jnp.pad(jnp.stack(mark_rows), ((0, 16 - 3 + -piece.shape[0] % 16), (0, 0)))
    sent = everyone(jnp.concatenate([piece, mark_rows], 0), 2).astype(F32)
    marks = jnp.sum(sent[:, piece.shape[0] : piece.shape[0] + 3], 1)
    sent = sent[:, : piece.shape[0]]
    if links.paired:
        square = jnp.sum(marks[:group, 0]) + jnp.sum(marks[:, 127])
        placed = sent.reshape(replicas, group // 2, 2, 2, gain_part // 2, wave)
        placed = placed.transpose(2, 1, 3, 0, 4, 5).reshape(2, features, wave)
    else:
        square = jnp.sum(marks[:group, 0]) + jnp.sum(marks[:group, 127])
        placed = sent[:group].reshape(group, gain_part, 2, wave)
        swapped = (jnp.arange(group) % 2 == 1)[:, None, None, None]
        placed = jnp.where(swapped, placed[:, :, ::-1], placed)
        placed = placed.transpose(2, 0, 1, 3).reshape(2, features, wave)
    wave_rows, gain_rows = placed[0].T, placed[1].T
    embed_part = input_embed.shape[0]
    row = member * embed_part + jnp.arange(embed_part) - patch
    chosen = (row[:, None] == jnp.arange(wave)[None, :]).astype(F32)
    inner = lax.dynamic_slice_in_dim(gain_rows[:12], member * gain_part, gain_part, 1)
    gains_grad = jnp.concatenate(
        [inner.reshape(3, 4, gain_part), outer.reshape(3, 2, gain_part)], 1
    )
    grads = (
        None,
        back_grad,
        gains_grad,
        embed_grad + full(chosen, wave_rows),
        table_grad,
        heads_grad,
        video_text_grad,
    )
    grad_norm = jnp.sqrt(square)
    factor = CLIP_NORM / jnp.maximum(grad_norm, CLIP_NORM)
    clipped = [None] + [g * factor for g in grads[1:]]
    masters = (
        mixing_in,
        mixing_out,
        norm_params,
        input_embed,
        word_table,
        head_proj,
        video_text_proj,
    )
    firsts = (
        mixing_in_first,
        mixing_out_first,
        norm_params_first,
        input_embed_first,
        word_table_first,
        head_proj_first,
        video_text_proj_first,
    )
    seconds = (
        mixing_in_second,
        mixing_out_second,
        norm_params_second,
        input_embed_second,
        word_table_second,
        head_proj_second,
        video_text_proj_second,
    )
    new = [
        adam_mixing(
            factor,
            core,
            pieces,
            mixing_in,
            mixing_in_first,
            mixing_in_second,
            features,
        )
    ]
    for i in range(1, 7):
        new.append(adam_update(masters[i], firsts[i], seconds[i], clipped[i], RATES[i]))
    outputs = [loss, grad_norm]
    for i in range(7):
        outputs += [new[i][0], clipped[4] if i == 4 else new[i][1], new[i][2]]
    return tuple(outputs)


def solution(mesh):
    both = ("dp", "fsdp")
    weight_specs = (
        P(None, "fsdp", None),
        P(None, "fsdp", None),
        P(None, None, "fsdp"),
        P("fsdp", None),
        P("fsdp", None),
        P("fsdp", None),
        P("fsdp", None),
    )
    tripled = tuple(spec for spec in weight_specs for _ in range(3))
    return jax.shard_map(
        body,
        mesh=mesh,
        in_specs=(
            P(both, None, None),
            P(both, None, None),
            P(both, None, None),
            P(both, None),
            P(both),
            P(both, None),
        )
        + tripled,
        out_specs=(P(), P()) + tripled,
        check_vma=False,
    )
```

```python
import functools

import jax
import jax.numpy as jnp
from jax import lax
from jax.experimental import pallas as pl
from jax.experimental.pallas import tpu as pltpu
from jax.sharding import PartitionSpec as P

ADAM_STEP = 10
FULL_PRECISION = lax.Precision.HIGHEST
SOFTMAX_WARMTH = 0.03
CLIP_NORM = 0.01
RATES = (0.1, 0.05, 0.3, 0.1, 0.2, 0.1, 0.1)
BETA_ONE = 0.9
BETA_TWO = 0.95
EPSILON = 1e-08
WEIGHT_DECAY = 0.1
F32 = jnp.float32
BF16 = jnp.bfloat16
MESH_ID = pl.DeviceIdType.MESH
VMEM_LIMIT = 56 * 1024 * 1024
NT = (((1,), (1,)), ((), ()))


def dot(a, b):
    return jnp.dot(a, b, preferred_element_type=F32)


def dot_nt(a, b):
    return lax.dot_general(a, b, NT, preferred_element_type=F32)


def dot_tn(a, b):
    return lax.dot_general(a, b, (((0,), (0,)), ((), ())), preferred_element_type=F32)


def full(a, b):
    return jnp.dot(a, b, precision=FULL_PRECISION)


def dot_nt_full(a, b):
    return lax.dot_general(a, b, NT, precision=FULL_PRECISION, preferred_element_type=F32)


def norm_rows(values, gain_row, shift_row):
    centred = values - jnp.mean(values, -1, keepdims=True)
    return (
        centred * lax.rsqrt(jnp.mean(centred * centred, -1, keepdims=True) + 1e-06) * gain_row
        + shift_row
    )


def unit_rows(values):
    return values * lax.rsqrt(jnp.sum(values * values, -1, keepdims=True) + 1e-06)


def log_sum(scores):
    highest = jnp.max(scores, -1, keepdims=True)
    return highest[..., 0] + jnp.log(jnp.sum(jnp.exp(scores - highest), -1))


def adam_update(master, first, second, gradient, rate):
    first_new = BETA_ONE * first + (1.0 - BETA_ONE) * gradient
    second_new = BETA_TWO * second + (1.0 - BETA_TWO) * gradient * gradient
    first_hat = first_new / (1.0 - BETA_ONE**ADAM_STEP)
    second_hat = second_new / (1.0 - BETA_TWO**ADAM_STEP)
    master_new = master - rate * (
        first_hat / (jnp.sqrt(second_hat) + EPSILON) + WEIGHT_DECAY * master
    )
    return (master_new, first_new, second_new)


def exchange_kernel(within, parts, x_ref, o_ref, send, recv, local):
    group = lax.axis_size("fsdp")
    member = lax.axis_index("fsdp")
    replica = lax.axis_index("dp")
    count = group if within else lax.axis_size("dp") * group
    me = member if within else replica * group + member
    barrier = pltpu.get_barrier_semaphore()

    def place(step):
        peer = lax.rem(me + step, count)
        if within:
            return peer, (replica, peer)
        return peer, (peer // group, lax.rem(peer, group))

    def part(peer):
        return x_ref.at[lax.rem(peer, group)] if parts else x_ref

    def greet(step, carry):
        pl.semaphore_signal(barrier, inc=1, device_id=place(step)[1], device_id_type=MESH_ID)
        return carry

    lax.fori_loop(1, count, greet, 0)
    mine = pltpu.make_async_copy(part(me), o_ref.at[me], local)
    mine.start()
    pl.semaphore_wait(barrier, count - 1)

    def copy(step):
        peer, device = place(step)
        return pltpu.make_async_remote_copy(
            src_ref=part(peer),
            dst_ref=o_ref.at[me],
            send_sem=send.at[step],
            recv_sem=recv.at[step],
            device_id=device,
            device_id_type=MESH_ID,
        )

    def begin(step, carry):
        copy(step).start()
        return carry

    def finish(step, carry):
        copy(step).wait()
        return carry

    lax.fori_loop(1, count, begin, 0)
    mine.wait()
    lax.fori_loop(1, count, finish, 0)


def everyone(x, collective, within=False, parts=False):
    group = lax.axis_size("fsdp")
    count = group if within else lax.axis_size("dp") * group
    return pl.pallas_call(
        functools.partial(exchange_kernel, within, parts),
        out_shape=jax.ShapeDtypeStruct((count,) + x.shape[1 if parts else 0 :], x.dtype),
        in_specs=[pl.BlockSpec(memory_space=pltpu.VMEM)],
        out_specs=pl.BlockSpec(memory_space=pltpu.VMEM),
        scratch_shapes=[
            pltpu.SemaphoreType.DMA((count,)),
            pltpu.SemaphoreType.DMA((count,)),
            pltpu.SemaphoreType.DMA,
        ],
        compiler_params=pltpu.CompilerParams(collective_id=collective, has_side_effects=True),
        name=f"everyone_{collective}",
    )(x)


def pack(values):
    rows = values.reshape(values.shape[0], -1)
    return jnp.pad(rows, ((0, 0), (0, -rows.shape[1] % 1024))).reshape(rows.shape[0], -1, 128)


def unpack(values, shape):
    size = 1
    for length in shape:
        size *= length
    return values.reshape(values.shape[0], -1)[:, :size].reshape((values.shape[0],) + shape)


def attend_kernel(rows, block, masked, *refs):
    if masked:
        qkv_ref, bias_ref, o_ref, l_ref = refs
    else:
        qkv_ref, o_ref, l_ref = refs
    lane = lax.broadcasted_iota(jnp.int32, (1, 128), 1)
    low = lane < 64
    keys = qkv_ref[:, 128:256]
    values = qkv_ref[:, 256:384]
    for at in range(0, rows, block):
        queries = qkv_ref[at : at + block, :128]
        outs, totals = [], []
        for head in range(2):
            picked = jnp.where(low if head == 0 else ~low, queries, 0) * jnp.array(0.125, BF16)
            scores = dot_nt(picked, keys)
            if masked:
                scores = scores + bias_ref[at : at + block, :]
            highest = jnp.max(scores, -1, keepdims=True)
            exponent = jnp.exp(scores - highest)
            summed = jnp.sum(exponent, -1, keepdims=True)
            outs.append(dot(exponent.astype(BF16), values) * (1.0 / summed))
            totals.append(highest + jnp.log(summed))
        o_ref[at : at + block, :] = jnp.where(low, outs[0], outs[1]).astype(BF16)
        l_ref[at : at + block, :] = jnp.where(low, totals[0], totals[1])


def attend(qkv, bias, block):
    rows, width = qkv.shape
    pairs = width // 384
    specs = [pl.BlockSpec((rows, 384), lambda j: (0, j))]
    args = [qkv]
    if bias is not None:
        specs.append(pl.BlockSpec(bias.shape, lambda j: (0, 0)))
        args.append(bias)
    return pl.pallas_call(
        functools.partial(attend_kernel, rows, block, bias is not None),
        grid=(pairs,),
        out_shape=(
            jax.ShapeDtypeStruct((rows, pairs * 128), BF16),
            jax.ShapeDtypeStruct((rows, pairs * 128), F32),
        ),
        in_specs=specs,
        out_specs=(
            pl.BlockSpec((rows, 128), lambda j: (0, j)),
            pl.BlockSpec((rows, 128), lambda j: (0, j)),
        ),
        compiler_params=pltpu.CompilerParams(vmem_limit_bytes=VMEM_LIMIT),
        cost_estimate=pl.CostEstimate(
            flops=rows * rows * 128 * pairs,
            bytes_accessed=rows * pairs * 128,
            transcendentals=0,
        ),
        name=f"attend_{rows}",
    )(*args)


def attend_back_kernel(rows, block, masked, *refs):
    if masked:
        qkv_ref, do_ref, o_ref, l_ref, bias_ref, g_ref, dk_ref, dv_ref = refs
    else:
        qkv_ref, do_ref, o_ref, l_ref, g_ref, dk_ref, dv_ref = refs
    lane = lax.broadcasted_iota(jnp.int32, (1, 128), 1)
    low = lane < 64
    keys = qkv_ref[:, 128:256]
    values = qkv_ref[:, 256:384]
    keys_t = keys.astype(F32).T.astype(BF16)
    row = lax.broadcasted_iota(jnp.int32, (128, 1), 0)
    keys_of = [jnp.where(row < 64, keys_t, 0), jnp.where(row < 64, 0, keys_t)]
    eighth = jnp.array(0.125, BF16)
    for at in range(0, rows, block):
        queries = qkv_ref[at : at + block, :128]
        grads = do_ref[at : at + block, :]
        totals_t = l_ref[at : at + block, :].T
        product_t = (grads.astype(F32) * o_ref[at : at + block, :].astype(F32)).T
        grad_q = None
        for head in range(2):
            mask = low if head == 0 else ~low
            picked = jnp.where(mask, queries, 0) * eighth
            picked_grad = jnp.where(mask, grads, 0)
            total = totals_t[64 * head : 64 * head + 1, :]
            delta = jnp.sum(product_t[64 * head : 64 * head + 64, :], 0, keepdims=True)
            scores = dot_nt(keys, picked)
            if masked:
                scores = scores + bias_ref[:, at : at + block]
            weights = jnp.exp(scores - total)
            grad_weights = dot_nt(values, picked_grad)
            grad_scores = (weights * (grad_weights - delta)).astype(BF16)
            part_v = dot(weights.astype(BF16), picked_grad)
            part_k = dot(grad_scores, picked)
            if at == 0 and head == 0:
                dv_ref[...] = part_v
                dk_ref[...] = part_k
            else:
                dv_ref[...] += part_v
                dk_ref[...] += part_k
            part_q = dot(keys_of[head], grad_scores)
            grad_q = part_q if grad_q is None else grad_q + part_q
        g_ref[at : at + block, :128] = (grad_q.T * 0.125).astype(BF16)
    g_ref[:, 128:256] = dk_ref[...].astype(BF16)
    g_ref[:, 256:384] = dv_ref[...].astype(BF16)


def attend_back(qkv, grad_out, out, totals, bias, block):
    rows, width = qkv.shape
    pairs = width // 384
    specs = [
        pl.BlockSpec((rows, 384), lambda j: (0, j)),
        pl.BlockSpec((rows, 128), lambda j: (0, j)),
        pl.BlockSpec((rows, 128), lambda j: (0, j)),
        pl.BlockSpec((rows, 128), lambda j: (0, j)),
    ]
    args = [qkv, grad_out, out, totals]
    if bias is not None:
        specs.append(pl.BlockSpec(bias.shape, lambda j: (0, 0)))
        args.append(bias)
    return pl.pallas_call(
        functools.partial(attend_back_kernel, rows, block, bias is not None),
        grid=(pairs,),
        out_shape=jax.ShapeDtypeStruct(qkv.shape, BF16),
        in_specs=specs,
        out_specs=pl.BlockSpec((rows, 384), lambda j: (0, j)),
        scratch_shapes=[pltpu.VMEM((rows, 128), F32), pltpu.VMEM((rows, 128), F32)],
        compiler_params=pltpu.CompilerParams(vmem_limit_bytes=VMEM_LIMIT),
        cost_estimate=pl.CostEstimate(
            flops=2 * rows * rows * 128 * pairs,
            bytes_accessed=rows * pairs * 128,
            transcendentals=0,
        ),
        name=f"attend_back_{rows}",
    )(*args)


def column_runs(features, width):
    runs = [
        (kind * features + pair * 128, (3 * pair + kind) * 128, 128)
        for pair in range(features // 128)
        for kind in range(3)
    ]
    return runs + [(3 * features, 3 * features, width - 3 * features)]


def gradient_runs(features, width):
    half = features // 2
    upper = width - 4 * features
    runs = column_runs(features, width)[:-1]
    towers = []
    for piece, upper_at in ((2, upper), (3, 0)):
        tower = []
        for begin, at, size in runs:
            side, local = divmod(at, 3 * half)
            spots = [4 * half * (side ^ core) + local for core in range(2)]
            tower.append((piece, *spots, begin, size))
        for side in range(2):
            spots = [4 * half * (side ^ core) + 3 * half for core in range(2)]
            tower.append((piece, *spots, 3 * features + side * half, half))
        tower.append((0, upper_at, upper_at, 4 * features, upper))
        towers.append(tower)
    tower = [(1, at, at, begin, size) for begin, at, size in runs]
    tower.append((1, 3 * features, 3 * features, 3 * features, width - 3 * features))
    return towers + [tower]


def regroup_kernel(runs, w_ref, low_ref):
    for begin, at, size in runs:
        low_ref[0, :, at : at + size] = w_ref[0, :, begin : begin + size].astype(BF16)


def regroup(mixing, features):
    towers, rows, width = mixing.shape
    spec = pl.BlockSpec((1, rows, width), lambda t: (t, 0, 0))
    return pl.pallas_call(
        functools.partial(regroup_kernel, column_runs(features, width)),
        grid=(towers,),
        out_shape=jax.ShapeDtypeStruct((towers, rows, width), BF16),
        in_specs=[spec],
        out_specs=spec,
        compiler_params=pltpu.CompilerParams(vmem_limit_bytes=VMEM_LIMIT),
        name="regroup",
    )(mixing)


def adam_kernel(towers, scal_ref, core_ref, *refs):
    pieces, (w_ref, first_ref, second_ref), outs = refs[:4], refs[4:7], refs[7:]
    factor = scal_ref[0]
    for tower, runs in enumerate(towers):
        for core in range(2):

            @pl.when((pl.program_id(0) == tower) & (core_ref[0] == core))
            def _():
                for run in runs:
                    piece, begin, size = run[0], run[3], run[4]
                    at = run[1 + core]
                    new = adam_update(
                        w_ref[0, :, begin : begin + size],
                        first_ref[0, :, begin : begin + size],
                        second_ref[0, :, begin : begin + size],
                        pieces[piece][:, at : at + size] * factor,
                        RATES[0],
                    )
                    for out, value in zip(outs, new):
                        out[0, :, begin : begin + size] = value


def adam_mixing(factor, core, pieces, master, first, second, features):
    towers, rows, width = master.shape
    spec = pl.BlockSpec((1, rows, width), lambda t: (t, 0, 0))
    scalar = pl.BlockSpec(memory_space=pltpu.SMEM)
    return pl.pallas_call(
        functools.partial(adam_kernel, gradient_runs(features, width)),
        grid=(towers,),
        out_shape=(jax.ShapeDtypeStruct(master.shape, F32),) * 3,
        in_specs=[scalar, scalar]
        + [pl.BlockSpec(piece.shape, lambda t: (0, 0)) for piece in pieces]
        + [spec] * 3,
        out_specs=(spec,) * 3,
        compiler_params=pltpu.CompilerParams(vmem_limit_bytes=VMEM_LIMIT),
        name="adam_mixing",
    )(factor.reshape(1), core.reshape(1).astype(jnp.int32), *pieces, master, first, second)


def scale_kernel(first_ref, second_ref, slopes_ref, out_ref):
    width = first_ref.shape[1]
    for at, ref in enumerate((first_ref, second_ref)):
        part = ref[...].astype(F32) * slopes_ref[at : at + 1, :]
        out_ref[:, at * width : (at + 1) * width] = part.astype(BF16)


def scale_columns(first, second, slopes):
    rows, width = first.shape
    block = rows // 6
    spec = pl.BlockSpec((block, width), lambda j: (j, 0))
    return pl.pallas_call(
        scale_kernel,
        grid=(rows // block,),
        out_shape=jax.ShapeDtypeStruct((rows, 2 * width), BF16),
        in_specs=[spec, spec, pl.BlockSpec(slopes.shape, lambda j: (0, 0))],
        out_specs=pl.BlockSpec((block, 2 * width), lambda j: (j, 0)),
        compiler_params=pltpu.CompilerParams(vmem_limit_bytes=VMEM_LIMIT),
        name="scale_columns",
    )(first, second, slopes)


def patch_kernel(tile, video_ref, entry_ref, out_ref):
    patch = video_ref.shape[2]
    for at in range(0, patch, tile):
        out_ref[at : at + tile, :] = dot_tn(video_ref[0, :, at : at + tile], entry_ref[...]).astype(
            BF16
        )
    out_ref[patch:, :] = jnp.zeros((out_ref.shape[0] - patch, out_ref.shape[1]), BF16)


def patch_grads(video, entry, rows):
    return pl.pallas_call(
        functools.partial(patch_kernel, 512),
        out_shape=jax.ShapeDtypeStruct((rows, entry.shape[1]), BF16),
        in_specs=[pl.BlockSpec(memory_space=pltpu.VMEM)] * 2,
        out_specs=pl.BlockSpec(memory_space=pltpu.VMEM),
        compiler_params=pltpu.CompilerParams(vmem_limit_bytes=VMEM_LIMIT),
        name="patch_grads",
    )(video, entry)


def middle_kernel(
    scales, captions, sum_ref, base_ref, scale_ref, backs_ref, gains_ref, heads_ref, vt_ref,
    live_ref, pos_ref, count_ref,
    loss_ref, dv_ref, da_ref, dt_ref, gg_ref, z_ref, zt_ref, de_ref, dt_e_ref, ev_ref, dvt_ref,
    r1_ref, slope_ref,
    x1_ref, x2_ref, r2_ref, x3_ref, r3_ref, x4_ref, r4_ref, send, recv,
):
    group = lax.axis_size("fsdp")
    clips = lax.axis_size("dp") * group
    member = lax.axis_index("fsdp")
    replica = lax.axis_index("dp")
    me = replica * group + member
    part = backs_ref.shape[1]
    joint = vt_ref.shape[0]
    own_group = pl.ds(pl.multiple_of(replica * group, group), group)
    barrier = pltpu.get_barrier_semaphore()

    def place(step):
        peer = lax.rem(me + step, clips)
        return peer, (peer // group, lax.rem(peer, group))

    def near(step):
        peer = lax.rem(member + step, group)
        return peer, (replica, peer)

    def greet(step, carry):
        pl.semaphore_signal(barrier, inc=1, device_id=place(step)[1], device_id_type=MESH_ID)
        return carry

    def exchange(phase, count, where, source, target):
        def copy(step):
            peer, device = where(step)
            return pltpu.make_async_remote_copy(
                src_ref=source(peer),
                dst_ref=target,
                send_sem=send.at[phase, step],
                recv_sem=recv.at[phase, step],
                device_id=device,
                device_id_type=MESH_ID,
            )

        def begin(step, carry):
            copy(step).start()
            return carry

        def finish(step, carry):
            copy(step).wait()
            return carry

        lax.fori_loop(1, count, begin, 0)
        lax.fori_loop(1, count, finish, 0)

    def times(a, b, dims):
        return lax.dot_general(
            a, b, (dims, ((), ())), precision=FULL_PRECISION, preferred_element_type=F32
        )

    plain, right, left = ((1,), (0,)), ((1,), (1,)), ((0,), (0,))
    lax.fori_loop(1, clips, greet, 0)
    x1_ref[...] = jnp.zeros_like(x1_ref)
    x2_ref[...] = jnp.zeros_like(x2_ref)
    x4_ref[...] = jnp.zeros_like(x4_ref)
    for at in range(group):
        x1_ref[at, :, :part] = sum_ref[:, at * part : (at + 1) * part]
    pl.semaphore_wait(barrier, clips - 1)
    r1_ref[me] = x1_ref[member]
    exchange(0, clips, place, lambda peer: x1_ref.at[lax.rem(peer, group)], r1_ref.at[me])
    for k in range(2 + captions):
        x2_ref[:, k, :] = times(r1_ref[own_group, k, :part], backs_ref[min(k, 2)], plain)
    r2_ref[member] = x2_ref[member]
    exchange(1, group, near, lambda peer: x2_ref.at[peer], r2_ref.at[member])
    x3_ref[...] = (jnp.sum(r2_ref[...], 0) + base_ref[...]) * scale_ref[...]
    r3_ref[me] = x3_ref[...]
    exchange(2, clips, place, lambda peer: x3_ref, r3_ref.at[me])
    texts = jnp.concatenate([r3_ref[:, 2 + k, :] for k in range(captions)], 0)


    def normalise(values):
        centred = values - jnp.mean(values, -1, keepdims=True)
        inverse = lax.rsqrt(jnp.mean(centred * centred, -1, keepdims=True) + 1e-06)
        return centred * inverse, inverse

    def unit(values):
        scale = lax.rsqrt(jnp.sum(values * values, -1, keepdims=True) + 1e-06)
        return values * scale, scale

    def unit_back(values, scale, grads):
        along = jnp.sum(values * grads, -1, keepdims=True)
        return scale * grads - values * (scale * scale * scale * along)

    def soft(scores):
        highest = jnp.max(scores, -1, keepdims=True)
        exponent = jnp.exp(scores - highest)
        total = jnp.sum(exponent, -1, keepdims=True)
        return highest + jnp.log(total), exponent * (1.0 / total)

    hats, z = [], []
    for t, rows in enumerate((r3_ref[:, 0, :], r3_ref[:, 1, :], texts)):
        hat, inverse = normalise(rows)
        hats.append((hat, inverse))
        z.append(hat * gains_ref[2 * t : 2 * t + 1, :] + gains_ref[2 * t + 1 : 2 * t + 2, :])
    heads = heads_ref[...].astype(F32)
    parts = (heads[:, :joint], heads[:, joint : 2 * joint], heads[:, 2 * joint :])
    video_text = vt_ref[...].astype(F32)
    e_video = times(z[0], parts[0], plain)
    e_both = times(e_video, video_text, plain)
    e_audio = times(z[1], parts[1], plain)
    e_text = times(z[2], parts[2], plain)
    (n_video, s_video), (n_both, s_both) = unit(e_video), unit(e_both)
    (n_audio, s_audio), (n_text, s_text) = unit(e_audio), unit(e_text)
    scores = times(n_video, n_audio, right) / SOFTMAX_WARMTH
    own = lax.broadcasted_iota(jnp.int32, scores.shape, 0) == lax.broadcasted_iota(
        jnp.int32, scores.shape, 1
    )
    total, share = soft(scores)
    matched = total - jnp.sum(jnp.where(own, scores, 0.0), -1, keepdims=True)
    d_scores = (share - jnp.where(own, 1.0, 0.0)) * (1.0 / (clips * SOFTMAX_WARMTH))
    live = live_ref[...]
    positive = pos_ref[...]
    text_scores = times(n_both, n_text, right) / SOFTMAX_WARMTH
    every, every_share = soft(jnp.where(live > 0.5, text_scores, -1e30))
    chosen, chosen_share = soft(jnp.where(positive > 0.5, text_scores, -1e30))
    weight = jnp.sum(positive, -1, keepdims=True) / jnp.sum(live)
    loss = jnp.sum(matched) / clips + jnp.sum(weight * (every - chosen))
    loss_ref[...] = jnp.broadcast_to(loss, loss_ref.shape)
    d_text_scores = (every_share * live - chosen_share * positive) * (weight / SOFTMAX_WARMTH)
    d_video = unit_back(e_video, s_video, times(d_scores, n_audio, plain))
    d_audio = unit_back(e_audio, s_audio, times(d_scores, n_video, left))
    d_both = unit_back(e_both, s_both, times(d_text_scores, n_text, plain))
    d_text = unit_back(e_text, s_text, times(d_text_scores, n_both, left))
    d_video = d_video + times(d_both, video_text, right)
    for t, (grad, out) in enumerate(((d_video, dv_ref), (d_audio, da_ref), (d_text, dt_ref))):
        d_z = times(grad, parts[t], right)
        hat, inverse = hats[t]
        gg_ref[2 * t : 2 * t + 1, :] = jnp.sum(d_z * hat, 0, keepdims=True)
        gg_ref[2 * t + 1 : 2 * t + 2, :] = jnp.sum(d_z, 0, keepdims=True)
        d_hat = d_z * gains_ref[2 * t : 2 * t + 1, :]
        inner = d_hat - jnp.mean(d_hat, -1, keepdims=True)
        rows = inverse * (inner - hat * jnp.mean(d_hat * hat, -1, keepdims=True))
        out[...] = rows * scales[t] if t < 2 else rows / count_ref[...]
    z_ref[0] = z[0]
    z_ref[1] = z[1]
    zt_ref[...] = z[2]
    de_ref[0] = d_video
    de_ref[1] = d_audio
    dt_e_ref[...] = d_text
    ev_ref[...] = e_video
    dvt_ref[...] = d_both
    for k in range(2 + captions):
        if k < 2:
            rows = (dv_ref, da_ref)[k][own_group, :]
        else:
            begin = pl.multiple_of((k - 2) * clips + replica * group, group)
            rows = dt_ref[pl.ds(begin, group), :]
        x4_ref[:, k, :part] = times(rows.astype(BF16).astype(F32), backs_ref[min(k, 2)], right)
    r4_ref[member] = x4_ref[member]
    exchange(3, group, near, lambda peer: x4_ref.at[peer], r4_ref.at[member])
    for at in range(group):
        slope_ref[:, at * part : (at + 1) * part] = r4_ref[at, :, :part]


def contrast(scales, captions, sums, bases, token_scales, backs, gains, heads, video_text, *masks):
    group = lax.axis_size("fsdp")
    clips = lax.axis_size("dp") * group
    features = bases.shape[1]
    texts = captions * clips
    joint, width = video_text.shape
    part = backs.shape[1]
    padded = part + -part % 128
    shapes = [
        (8, 128),
        (clips, features),
        (clips, features),
        (texts, features),
        (8, features),
        (2, clips, features),
        (texts, features),
        (2, clips, joint),
        (texts, width),
        (clips, joint),
        (clips, width),
        (clips, 8, padded),
        (8, part * group),
    ]
    return pl.pallas_call(
        functools.partial(middle_kernel, scales, captions),
        out_shape=tuple(jax.ShapeDtypeStruct(shape, F32) for shape in shapes),
        in_specs=[pl.BlockSpec(memory_space=pltpu.VMEM)] * 10,
        out_specs=tuple(pl.BlockSpec(memory_space=pltpu.VMEM) for _ in shapes),
        scratch_shapes=[
            pltpu.VMEM((group, 8, padded), F32),
            pltpu.VMEM((group, 8, features), F32),
            pltpu.VMEM((group, 8, features), F32),
            pltpu.VMEM((8, features), F32),
            pltpu.VMEM((clips, 8, features), F32),
            pltpu.VMEM((group, 8, padded), F32),
            pltpu.VMEM((group, 8, padded), F32),
            pltpu.SemaphoreType.DMA((4, clips)),
            pltpu.SemaphoreType.DMA((4, clips)),
        ],
        compiler_params=pltpu.CompilerParams(
            vmem_limit_bytes=VMEM_LIMIT, collective_id=1, has_side_effects=True
        ),
        name="middle",
    )(sums, bases, token_scales, backs, gains, heads, video_text, *masks)


def feed_kernel(with_product, h_ref, w_ref, sel_ref, slope_ref, sums_ref, *rest):
    hidden = dot(h_ref[...], w_ref[...])
    root = 0.7978845608028654
    square = hidden * hidden
    tang = jnp.tanh(root * hidden * (1.0 + 0.044715 * square))
    half = 0.5 * (1.0 + tang)
    active = (hidden * half).astype(BF16)
    slope = half + (0.5 * root) * hidden * (1.0 - tang * tang) * (1.0 + (3 * 0.044715) * square)
    slope = slope.astype(BF16)
    slope_ref[...] = slope
    if with_product:
        sums_ref[...] = jnp.broadcast_to(
            jnp.sum(active.astype(F32), 0, keepdims=True), sums_ref.shape
        )
        rest[0][...] = dot_tn(h_ref[...], slope).astype(BF16)
    else:
        sums_ref[...] = dot(sel_ref[...], active)


def feed(normed, weight, column, select, tile, with_product):
    rows, features = normed.shape
    width = weight.shape[1] - column
    first = column // tile
    shapes = [
        jax.ShapeDtypeStruct((rows, width), BF16),
        jax.ShapeDtypeStruct((8, width), F32),
    ]
    outs = [
        pl.BlockSpec((rows, tile), lambda j: (0, j)),
        pl.BlockSpec((8, tile), lambda j: (0, j)),
    ]
    if with_product:
        shapes.append(jax.ShapeDtypeStruct((features, width), BF16))
        outs.append(pl.BlockSpec((features, tile), lambda j: (0, j)))
    return pl.pallas_call(
        functools.partial(feed_kernel, with_product),
        grid=(width // tile,),
        out_shape=tuple(shapes),
        in_specs=[
            pl.BlockSpec((rows, features), lambda j: (0, 0)),
            pl.BlockSpec((features, tile), lambda j: (0, first + j)),
            pl.BlockSpec(select.shape, lambda j: (0, 0)),
        ],
        out_specs=tuple(outs),
        compiler_params=pltpu.CompilerParams(vmem_limit_bytes=VMEM_LIMIT),
        cost_estimate=pl.CostEstimate(
            flops=rows * features * width // 8,
            bytes_accessed=rows * width,
            transcendentals=0,
        ),
        name=f"feed_{rows}",
    )(normed, weight, select)


def both_columns(own, other, core):
    first = jnp.where(core == 0, own, other)
    second = jnp.where(core == 0, other, own)
    return jnp.concatenate([first, second], -1)


def attention_forward(stream, bias, mixing, gains, block):
    features = stream.shape[1]
    normed = norm_rows(stream, gains[0], gains[1]).astype(BF16)
    joined = dot(normed, mixing[:, : 3 * features]).astype(BF16)
    return normed, joined, attend(joined, bias, block)


def feed_forward(stream, mixed, mixing, gains, select, with_product):
    features = stream.shape[1]
    middle = stream + dot(mixed, mixing[:, 3 * features : 4 * features])
    normed = norm_rows(middle, gains[2], gains[3]).astype(BF16)
    return middle, normed, feed(normed, mixing, 4 * features, select, 512, with_product)


def output_backward(grad_rows, grad_normed, mixed, middle, mixing, gains):
    features = middle.shape[1]
    grad_norm, grad_gain, grad_shift = jax.vjp(norm_rows, middle, gains[2], gains[3])[1](
        grad_normed
    )
    grad_middle = grad_rows + grad_norm
    grad_attention = grad_middle.astype(BF16)
    grad_mixed = dot_nt(grad_attention, mixing[:, 3 * features : 4 * features]).astype(BF16)
    grad_output = dot_tn(mixed, grad_attention).astype(BF16)
    return grad_middle, grad_output, grad_mixed, [grad_gain, grad_shift]


def input_backward(grad_middle, grad_joined, stream, mixing, gains):
    features = stream.shape[1]
    grad_normed = dot_nt(grad_joined, mixing[:, : 3 * features])
    grad_norm, grad_gain, grad_shift = jax.vjp(norm_rows, stream, gains[0], gains[1])[1](
        grad_normed
    )
    return (grad_middle + grad_norm).astype(BF16), [grad_gain, grad_shift]


def both_columns(own, other, core):
    first = jnp.where(core == 0, own, other)
    second = jnp.where(core == 0, other, own)
    return jnp.concatenate([first, second], -1)


class Links:
    def __init__(self):
        self.group = lax.axis_size("fsdp")
        self.replicas = lax.axis_size("dp")
        self.member = lax.axis_index("fsdp")
        self.replica = lax.axis_index("dp")
        self.core = self.member % 2
        self.paired = self.group == 16 and self.replicas == 2

    def swap(self, values, name):
        if name == "y":
            return lax.ppermute(values, "dp", [(0, 1), (1, 0)])
        bit = {"core": 1, "x": 2, "near": 4, "far": 8, "across": 12}[name]
        return lax.ppermute(values, "fsdp", [(f, f ^ bit) for f in range(self.group)])

    def bit(self, name):
        if name == "y":
            return self.replica
        return (self.member // {"core": 1, "x": 2, "near": 4, "far": 8}[name]) % 2

    def merge(self, values, other, names, name, order=("far", "near", "x", "core", "y")):
        names = sorted(names + [name], key=order.index)
        at = names.index(name)
        place = lax.broadcasted_iota(jnp.int32, (2,) + (1,) * (values.ndim - at), 0)
        joined = jnp.where(
            place == self.bit(name), jnp.expand_dims(values, at), jnp.expand_dims(other, at)
        )
        return joined, names

    def sides(self, values, names, name):
        at = names.index(name)
        bit = self.bit(name)
        give = lax.dynamic_index_in_dim(values, 1 - bit, at, keepdims=False)
        keep = lax.dynamic_index_in_dim(values, bit, at, keepdims=False)
        return keep, give, [n for n in names if n != name]

    def spread(self, values):
        for name in ("core", "x", "near", "far"):
            other = yield values, name
            values = jnp.where(self.bit(name) == 1, values, other)
        return values

    def gather_clips(self, values):
        if not self.paired:
            return lax.all_gather(values, ("dp", "fsdp"), axis=0, tiled=True)
        names = []
        order = ["y", "far", "near", "x", "core"]
        one, two, three = yield [(values, "near"), (values, "far"), (values, "across")]
        values, _ = self.merge(values, one, [], "near", order)
        others, names = self.merge(two, three, [], "near", order)
        values, names = self.merge(values, others, names, "far", order)
        for name in ("y", "x", "core"):
            other = yield values, name
            values, names = self.merge(values, other, names, name, order)
        return values.reshape(-1, values.shape[-1])

    def sum_replicas(self, part):
        if not self.paired:
            return lax.psum(part, "dp").astype(F32)
        other = yield part, "y"
        return part.astype(F32) + other.astype(F32)

    def gather_rows(self, shard, order):
        rows, width = shard.shape
        half = width // 2
        if not self.paired:
            return lax.all_gather(shard, "fsdp", axis=0, tiled=True)
        values = lax.dynamic_slice_in_dim(shard, self.replica * half, half, 1)
        names = []
        for name in order + ("core",):
            other = yield values, name
            if name == "y":
                values = both_columns(values, other, self.replica)
            else:
                values, names = self.merge(values, other, names, name)
        return values.reshape(self.group * rows, width)

    def reduce_columns(self, own, other, order):
        rows, half = own.shape
        part = rows // self.group
        other = yield other, "core"
        values = add(own, other).reshape(2, 2, 2, 2, 2, part // 2, half)
        names = ["far", "near", "x", "core", "y"]
        for name in order:
            keep, give, names = self.sides(values, names, name)
            other = yield give, name
            values = add(keep, other)
        return values

    def share_columns(self, values):
        mine, give, _ = self.sides(values, ["core"], "core")
        other = yield give, "core"
        values = jnp.concatenate([mine, other], 1)
        other = yield values, "y"
        values, _ = self.merge(values, other, [], "y")
        return values.reshape(2 * values.shape[1], values.shape[2]).astype(F32)

    def scatter_columns(self, own, other, order):
        if not self.paired:
            half = own.shape[1]
            core = self.core
            whole = both_columns(own, other, core)
            whole = lax.psum_scatter(whole, "fsdp", scatter_dimension=0, tiled=True)
            whole = lax.psum(whole, "dp").astype(F32)
            return jnp.concatenate(
                [
                    lax.dynamic_slice_in_dim(whole, core * half, half, 1),
                    lax.dynamic_slice_in_dim(whole, (1 - core) * half, half, 1),
                ],
                1,
            )
        values = yield from self.reduce_columns(own, other, order)
        return (yield from self.share_columns(values))

    def scatter_rows(self, values, order):
        rows, width = values.shape
        part = rows // self.group
        half = width // 2
        if not self.paired:
            part_sum = lax.psum_scatter(values, "fsdp", scatter_dimension=0, tiled=True)
            return lax.psum(part_sum, "dp").astype(F32)
        values = values.reshape(2, 2, 2, 2, part, width)
        names = ["far", "near", "x", "core"]
        for name in ("core",) + order:
            if name == "y":
                last = values.ndim - 1
                give = lax.dynamic_slice_in_dim(values, (1 - self.replica) * half, half, last)
                keep = lax.dynamic_slice_in_dim(values, self.replica * half, half, last)
            else:
                keep, give, names = self.sides(values, names, name)
            other = yield give, name
            values = add(keep, other)
        other = yield values, "y"
        return both_columns(values, other, self.replica).astype(F32)

    def scatter_words(self, values):
        rows, width = values.shape
        if not self.paired:
            return lax.psum_scatter(values, "fsdp", scatter_dimension=0, tiled=True)
        values = values.reshape(2, 2, 2, 2, rows // self.group, width)
        names = ["far", "near", "x", "core"]
        for name in ("core", "x", "far", "near"):
            keep, give, names = self.sides(values, names, name)
            other = yield give, name
            values = add(keep, other)
        return values

    def stage(self, flows, work=None, inputs=()):
        active = [flow for flow in flows if flow.request is not None]
        asked = [flow.request if isinstance(flow.request, list) else [flow.request] for flow in active]
        held = [[values for values, _ in asks] for asks in asked]
        held, inputs = lax.optimization_barrier((held, inputs))
        sent = [
            [self.swap(values, name) for values, (_, name) in zip(group, asks)]
            for group, asks in zip(held, asked)
        ]
        made = work(*inputs) if work is not None else ()
        sent, made = lax.optimization_barrier((sent, made))
        for flow, others in zip(active, sent):
            flow.push(others if isinstance(flow.request, list) else others[0])
        return made


class Flow:
    def __init__(self, steps):
        self.steps = steps
        self.value = None
        self.push(None)

    def push(self, other):
        try:
            self.request = self.steps.send(other)
        except StopIteration as end:
            self.request, self.value = None, end.value


def add(left, right):
    return (left.astype(F32) + right.astype(F32)).astype(BF16)


def body(
    video,
    audio,
    word_ids,
    word_counts,
    caption_counts,
    caption_clips,
    mixing_in,
    mixing_in_first,
    mixing_in_second,
    mixing_out,
    mixing_out_first,
    mixing_out_second,
    norm_params,
    norm_params_first,
    norm_params_second,
    input_embed,
    input_embed_first,
    input_embed_second,
    word_table,
    word_table_first,
    word_table_second,
    head_proj,
    head_proj_first,
    head_proj_second,
    video_text_proj,
    video_text_proj_first,
    video_text_proj_second,
):
    group = lax.axis_size("fsdp")
    replicas = lax.axis_size("dp")
    clips = group * replicas
    member = lax.axis_index("fsdp")
    replica = lax.axis_index("dp")
    clip = replica * group + member
    captions, slots = word_ids.shape[1:]
    words = captions * slots
    patch = video.shape[2]
    video_count, audio_count = video.shape[1], audio.shape[1]
    features = mixing_in.shape[1] * group
    pairs = features // 128
    shard = mixing_in.shape[1]
    qkv = 3 * features

    links = Links()
    core = links.core
    half = features // 2
    joint_part, text_width = video_text_proj.shape
    table_rows = word_table.shape[0]
    gain_part = norm_params.shape[2]
    wave = audio.shape[2]
    low = regroup(mixing_in, features)

    def gather(values):
        return lax.all_gather(values, "fsdp", axis=0, tiled=True)

    weights = [None] * 3
    weights[1] = gather(low[1])
    def exchange(*parts):
        packed = jnp.concatenate([part.reshape(-1).astype(F32) for part in parts])
        packed = jnp.pad(packed, (0, -packed.shape[0] % 1024)).reshape(-1, 128)
        return everyone(packed, 0).reshape(clips, -1)

    embed_low = input_embed.astype(BF16)
    embed_flow = Flow(links.gather_rows(embed_low, ("near", "far", "y", "x")))
    wave_flow = Flow(links.spread(embed_low[-wave:])) if links.paired else embed_flow
    every = links.stage(
        [embed_flow, wave_flow],
        exchange,
        (word_ids, word_counts, caption_counts, caption_clips, norm_params),
    )

    def owned_rows(ids):
        local_ids = ids - member * table_rows
        owned = (local_ids >= 0) & (local_ids < table_rows)
        return jnp.clip(local_ids, 0, table_rows - 1), owned

    def pick_words(every):
        ids = every[:, :words].astype(jnp.int32)
        group_ids = lax.dynamic_slice_in_dim(ids, replica * group, group, 0).reshape(-1)
        local_ids, owned = owned_rows(group_ids)
        return jnp.where(owned[:, None], word_table[local_ids], 0.0).astype(BF16)

    picked = links.stage([embed_flow, wave_flow], pick_words, (every,))
    words_flow = Flow(links.scatter_words(picked))

    def prepare(every):
        local_ids = owned_rows(every[:, :words].astype(jnp.int32).reshape(-1))
        at = words + captions
        live = jnp.arange(captions)[:, None] < every[:, at].astype(jnp.int32)[None, :]
        live = live.reshape(1, -1)
        counts = every[:, words : words + captions].T.reshape(-1, 1)
        owners = every[:, at + 1 : at + 1 + captions].astype(jnp.int32).T.reshape(1, -1)
        positive = live & (owners == jnp.arange(clips)[:, None])
        at = at + 1 + captions
        gains_all = (
            every[:group, at : at + 18 * gain_part]
            .reshape(group, 3, 6, gain_part)
            .transpose(1, 2, 0, 3)
            .reshape(3, 6, features)
            .astype(BF16)
            .astype(F32)
        )
        outer_rows = jnp.pad(gains_all[:, 4:].reshape(6, features), ((0, 2), (0, 0)))
        masks = (live.astype(F32), positive.astype(F32), counts)
        valid = (jnp.arange(slots)[None, :] < word_counts[0][:, None]).reshape(-1)
        caption_of = jnp.arange(words) // slots
        allowed = (caption_of[:, None] == caption_of[None, :]) & valid[None, :]
        word_bias = jnp.where(allowed, 0.0, -1000000000.0).astype(F32)
        select = ((jnp.arange(8)[:, None] == caption_of[None, :]) & valid[None, :]).astype(BF16)
        own_counts = word_counts[0].astype(F32)
        sizes = jnp.array([video_count, audio_count], F32)
        scales = 1.0 / jnp.concatenate([sizes, own_counts, jnp.ones(6 - captions, F32)])
        heads_low = jnp.concatenate(
            [head_proj, jnp.pad(video_text_proj, ((0, shard - joint_part), (0, 0)))], 1
        ).astype(BF16)
        backs = mixing_out.astype(BF16).astype(F32)
        return (
            gains_all,
            outer_rows,
            masks,
            (word_bias, word_bias.T, select),
            scales[:, None],
            heads_low,
            backs,
            local_ids,
        )

    (
        gains_all,
        outer_rows,
        masks,
        (word_bias, turned_bias, select),
        token_scales,
        heads_low,
        backs,
        (local_ids, owned),
    ) = links.stage([embed_flow, wave_flow, words_flow], prepare, (every,))
    unused = jnp.zeros((8, 128), BF16)
    biases = (None, None, word_bias)
    turned_biases = (None, None, turned_bias)
    selects = (unused, unused, select)
    forward_block = (512, 512, words)
    backward_block = (512, 256, words)
    normed, joined, attended, fed, streams = ([None] * 3 for _ in range(5))
    links.stage([wave_flow, words_flow])
    wave_rows = wave_flow.value
    if not links.paired:
        wave_rows = wave_rows[patch:]
    streams[1] = links.stage(
        [words_flow], lambda rows: dot(audio[0], rows), (wave_rows,)
    )

    def attention(tower, stream, mixing):
        return attention_forward(
            stream, biases[tower], mixing, gains_all[tower], forward_block[tower]
        )

    def feeding(tower, stream, mixed, mixing):
        return feed_forward(
            stream, mixed, mixing, gains_all[tower], selects[tower], tower < 2
        )

    streams, weights[1], low_video, low_text = lax.optimization_barrier(
        (streams, weights[1], low[0], low[2])
    )
    weights[0] = gather(low_video)
    weights[2] = gather(low_text)
    normed[1], joined[1], attended[1] = links.stage(
        [embed_flow, words_flow],
        lambda stream, mixing: attention(1, stream, mixing),
        (streams[1], weights[1]),
    )
    streams[2] = words_flow.value.astype(F32)
    fed[1] = links.stage(
        [embed_flow],
        lambda mixed: feeding(1, streams[1], mixed, weights[1]),
        (attended[1][0],),
    )
    embed = embed_flow.value
    fed[1], weights[0], embed = lax.optimization_barrier((fed[1], weights[0], embed))
    streams[0] = dot(video[0], embed[:patch])
    normed[0], joined[0], attended[0] = attention(0, streams[0], weights[0])
    fed[0] = feeding(0, streams[0], attended[0][0], weights[0])
    fed[0], weights[2], heads_low = lax.optimization_barrier((fed[0], weights[2], heads_low))
    heads_all = gather(heads_low)
    normed[2], joined[2], attended[2] = attention(2, streams[2], weights[2])
    fed[2] = feeding(2, streams[2], attended[2][0], weights[2])

    heads = heads_all[:, : head_proj.shape[1]]
    video_text = heads_all[:, head_proj.shape[1] :].reshape(group, shard, text_width)
    video_text = video_text[:, :joint_part].reshape(group * joint_part, text_width)
    slopes = [fed[t][2][0] for t in range(3)]
    products = [fed[t][2][2] for t in range(2)]
    row_sums = [fed[t][2][1] for t in range(3)]
    token_count = 2 + captions
    summed = jnp.concatenate(
        [row_sums[0][:1], row_sums[1][:1], row_sums[2][: 8 - 2]], 0
    )
    bases = jnp.concatenate(
        [
            jnp.sum(fed[0][0], 0, keepdims=True),
            jnp.sum(fed[1][0], 0, keepdims=True),
            full(select[: 8 - 2].astype(F32), fed[2][0]),
        ],
        0,
    )
    (
        loss,
        *grad_rows_all,
        outer_grads,
        z_pair,
        z_text,
        d_pair,
        d_text,
        embed_video,
        d_video_text,
        every_sum,
        sloped,
    ) = contrast(
        (1.0 / video_count, 1.0 / audio_count),
        captions,
        summed,
        bases,
        token_scales,
        backs,
        outer_rows,
        heads,
        video_text,
        *masks,
    )
    loss = loss[0, 0]
    z = (z_pair[0], z_pair[1], z_text)
    d_heads = (d_pair[0], d_pair[1], d_text)

    def own_columns(values):
        return lax.dynamic_slice_in_dim(values, member * shard, shard, 1)

    def head_grads():
        heads_grad = jnp.concatenate([full(own_columns(z[t]).T, d_heads[t]) for t in range(3)], 1)
        own = lax.dynamic_slice_in_dim(embed_video, member * joint_part, joint_part, 1)
        return heads_grad, full(own.T, d_video_text)

    branch_all = [rows.astype(BF16) for rows in grad_rows_all]

    back_part = mixing_out.shape[1]

    def back_grads():
        own = every_sum[:, :, :back_part].transpose(1, 0, 2)
        own = (own[0], own[1], own[2:token_count].reshape(-1, back_part))
        return jnp.stack([full(own[t].T, branch_all[t].astype(F32)) for t in range(3)])

    own_grads = [
        lax.dynamic_slice_in_dim(grad_rows_all[0], clip, 1, 0),
        lax.dynamic_slice_in_dim(grad_rows_all[1], clip, 1, 0),
        lax.dynamic_slice_in_dim(
            grad_rows_all[2].reshape(captions, clips, features), clip, 1, 1
        ).reshape(captions, features),
    ]
    own_slopes = (sloped[:1], sloped[1:2], sloped[2:token_count])
    ups = scale_columns(products[1], products[0], jnp.concatenate(own_slopes[1::-1], 0))
    ups, own_slopes = lax.optimization_barrier((ups, own_slopes))
    up_part = lax.psum_scatter(ups, "fsdp", scatter_dimension=0, tiled=True)
    first, second = ("y", "x", "far", "near"), ("x", "y", "far", "near")

    def halves(inward, outward):
        return [
            jnp.concatenate(
                [
                    lax.dynamic_slice_in_dim(inward, at * 3 * half, 3 * half, 1),
                    lax.dynamic_slice_in_dim(outward, at * half, half, 1),
                ],
                1,
            )
            for at in (core, 1 - core)
        ]

    def hidden_backward(tower, slope):
        upper = weights[tower][:, 4 * features :]
        if tower == 2:
            spread = select[:captions].astype(F32).T
            grad_hidden = (slopes[2].astype(F32) * full(spread, slope)).astype(BF16)
            up = dot_tn(fed[2][1], grad_hidden).astype(BF16)
            return full(spread, own_grads[2]), dot_nt(grad_hidden, upper), up
        scaled = (upper.astype(F32) * slope).astype(BF16)
        return own_grads[tower], dot_nt(slopes[tower], scaled), None

    def outward_backward(tower, slope):
        rows_grad, grads, up = hidden_backward(tower, slope)
        made = output_backward(
            rows_grad, grads, attended[tower][0], fed[tower][0], weights[tower], gains_all[tower]
        )
        return made, up

    def inner_backward(tower, grad_mixed):
        return attend_back(
            joined[tower],
            grad_mixed,
            attended[tower][0],
            attended[tower][1],
            turned_biases[tower],
            backward_block[tower],
        )

    def entry_backward(tower, grad_middle, grad_joined):
        return input_backward(
            grad_middle, grad_joined, streams[tower], weights[tower], gains_all[tower]
        )

    gains_grads = [None] * 3

    def text_backward(slope):
        made, up = outward_backward(2, slope)
        grad_joined = inner_backward(2, made[2])
        inward = dot_tn(normed[2], grad_joined).astype(BF16)
        entry, entry_gains = entry_backward(2, made[0], grad_joined)
        return jnp.concatenate([inward, made[1], up], 1), entry, entry_gains + made[3]

    text_grad, entry, gains_grads[2] = links.stage([], text_backward, (own_slopes[2],))
    word_flow = Flow(links.gather_clips(entry))
    text_part = lax.psum_scatter(text_grad, "fsdp", scatter_dimension=0, tiled=True)
    made_video, _ = links.stage([word_flow], lambda slope: outward_backward(0, slope), (own_slopes[0],))
    embed_rows = input_embed.shape[0] * group

    def video_inner(grad_mixed):
        grad_joined = inner_backward(0, grad_mixed)
        inward = dot_tn(normed[0], grad_joined).astype(BF16)
        entry, entry_gains = entry_backward(0, made_video[0], grad_joined)
        return halves(inward, made_video[1]), entry, entry_gains

    video_parts, entry, entry_gains = links.stage([word_flow], video_inner, (made_video[2],))
    gains_grads[0] = entry_gains + made_video[3]
    video_flow = Flow(links.scatter_columns(*video_parts, first))

    def video_entry(entry, slope):
        made, _ = outward_backward(1, slope)
        return patch_grads(video, entry, embed_rows), made

    grad_embed, made_audio = links.stage([word_flow, video_flow], video_entry, (entry, own_slopes[1]))
    embed_flow = Flow(links.scatter_rows(grad_embed, first))
    rest = [word_flow, video_flow, embed_flow]
    joined_audio = links.stage(rest, lambda part: inner_backward(1, part), (made_audio[2],))

    def scatter_table(every_word):
        return jax.ops.segment_sum(
            jnp.where(owned[:, None], every_word.astype(F32), 0.0),
            local_ids,
            num_segments=table_rows,
        )

    def audio_inward(grad_joined, every_word):
        inward = dot_tn(normed[1], grad_joined).astype(BF16)
        return halves(inward, made_audio[1]), scatter_table(every_word)

    audio_parts, table_grad = links.stage(rest, audio_inward, (joined_audio, word_flow.value))
    cut = features
    if links.paired:
        audio_flows = [
            Flow(links.reduce_columns(*[part[:, :cut] for part in audio_parts], first)),
            Flow(links.reduce_columns(*[part[:, cut:] for part in audio_parts], second)),
        ]
    else:
        audio_flows = [Flow(links.scatter_columns(*audio_parts, first))]
    rest += audio_flows

    def audio_entry(grad_joined):
        entry, entry_gains = entry_backward(1, made_audio[0], grad_joined)
        wave_grad = dot_tn(entry, audio[0]).astype(BF16)
        every_gain = jnp.stack(gains_grads[0] + entry_gains + made_audio[3] + gains_grads[2])
        every_gain = jnp.pad(every_gain, ((0, wave - every_gain.shape[0]), (0, 0)))
        gain_columns = every_gain.T.astype(BF16)
        return (
            jnp.where(core == 0, wave_grad, gain_columns),
            jnp.where(core == 0, gain_columns, wave_grad),
        )

    beside = links.stage(rest, audio_entry, (joined_audio,))
    beside_flow = Flow(
        links.reduce_columns(*beside, second)
        if links.paired
        else links.scatter_columns(*beside, first)
    )
    rest += [beside_flow]

    def squared(*values):
        return sum(jnp.sum(value * value) for value in values)

    links.stage(rest)
    back_grad, (heads_grad, video_text_grad), table_square = links.stage(
        rest, lambda table: (back_grads(), head_grads(), squared(table)), (table_grad,)
    )
    up_flow = Flow(links.sum_replicas(up_part))
    rest += [up_flow]
    small_square = links.stage(rest, squared, (back_grad, heads_grad, video_text_grad))
    links.stage(rest)
    text_flow = Flow(links.sum_replicas(text_part))
    if links.paired:
        values = jnp.concatenate([flow.value for flow in audio_flows], 2)
        audio_flows = [Flow(links.share_columns(values))]
    rest += audio_flows + [text_flow]
    for _ in range(4):
        if any(flow.request is not None for flow in rest):
            links.stage(rest)
    pieces = (up_flow.value, text_flow.value, video_flow.value, audio_flows[0].value)
    embed_grad = embed_flow.value

    outer = lax.dynamic_slice_in_dim(outer_grads[:6], member * gain_part, gain_part, 1)
    local_square = table_square + small_square + squared(*pieces, embed_grad, outer)
    piece = beside_flow.value.reshape(-1, wave)
    piece_square = squared(piece.astype(F32))
    marks = jnp.where(jnp.arange(128) < 64, local_square, piece_square)
    mark_rows = []
    for _ in range(3):
        mark_rows.append(marks.astype(BF16))
        marks = marks - mark_rows[-1].astype(F32)
    mark_rows = jnp.pad(jnp.stack(mark_rows), ((0, 16 - 3 + -piece.shape[0] % 16), (0, 0)))
    sent = everyone(jnp.concatenate([piece, mark_rows], 0), 2).astype(F32)
    marks = jnp.sum(sent[:, piece.shape[0] : piece.shape[0] + 3], 1)
    sent = sent[:, : piece.shape[0]]
    if links.paired:
        square = jnp.sum(marks[:group, 0]) + jnp.sum(marks[:, 127])
        placed = sent.reshape(replicas, group // 2, 2, 2, gain_part // 2, wave)
        placed = placed.transpose(2, 1, 3, 0, 4, 5).reshape(2, features, wave)
    else:
        square = jnp.sum(marks[:group, 0]) + jnp.sum(marks[:group, 127])
        placed = sent[:group].reshape(group, gain_part, 2, wave)
        swapped = (jnp.arange(group) % 2 == 1)[:, None, None, None]
        placed = jnp.where(swapped, placed[:, :, ::-1], placed)
        placed = placed.transpose(2, 0, 1, 3).reshape(2, features, wave)
    wave_rows, gain_rows = placed[0].T, placed[1].T
    embed_part = input_embed.shape[0]
    row = member * embed_part + jnp.arange(embed_part) - patch
    chosen = (row[:, None] == jnp.arange(wave)[None, :]).astype(F32)
    inner = lax.dynamic_slice_in_dim(gain_rows[:12], member * gain_part, gain_part, 1)
    gains_grad = jnp.concatenate(
        [inner.reshape(3, 4, gain_part), outer.reshape(3, 2, gain_part)], 1
    )
    grads = (
        None,
        back_grad,
        gains_grad,
        embed_grad + full(chosen, wave_rows),
        table_grad,
        heads_grad,
        video_text_grad,
    )
    grad_norm = jnp.sqrt(square)
    factor = CLIP_NORM / jnp.maximum(grad_norm, CLIP_NORM)
    clipped = [None] + [g * factor for g in grads[1:]]
    masters = (
        mixing_in,
        mixing_out,
        norm_params,
        input_embed,
        word_table,
        head_proj,
        video_text_proj,
    )
    firsts = (
        mixing_in_first,
        mixing_out_first,
        norm_params_first,
        input_embed_first,
        word_table_first,
        head_proj_first,
        video_text_proj_first,
    )
    seconds = (
        mixing_in_second,
        mixing_out_second,
        norm_params_second,
        input_embed_second,
        word_table_second,
        head_proj_second,
        video_text_proj_second,
    )
    new = [
        adam_mixing(
            factor,
            core,
            pieces,
            mixing_in,
            mixing_in_first,
            mixing_in_second,
            features,
        )
    ]
    for i in range(1, 7):
        new.append(adam_update(masters[i], firsts[i], seconds[i], clipped[i], RATES[i]))
    outputs = [loss, grad_norm]
    for i in range(7):
        outputs += [new[i][0], clipped[4] if i == 4 else new[i][1], new[i][2]]
    return tuple(outputs)


def solution(mesh):
    both = ("dp", "fsdp")
    weight_specs = (
        P(None, "fsdp", None),
        P(None, "fsdp", None),
        P(None, None, "fsdp"),
        P("fsdp", None),
        P("fsdp", None),
        P("fsdp", None),
        P("fsdp", None),
    )
    tripled = tuple(spec for spec in weight_specs for _ in range(3))
    return jax.shard_map(
        body,
        mesh=mesh,
        in_specs=(
            P(both, None, None),
            P(both, None, None),
            P(both, None, None),
            P(both, None),
            P(both),
            P(both, None),
        )
        + tripled,
        out_specs=(P(), P()) + tripled,
        check_vma=False,
    )
```

```python
import functools

import jax
import jax.numpy as jnp
from jax import lax
from jax.experimental import pallas as pl
from jax.experimental.pallas import tpu as pltpu
from jax.sharding import PartitionSpec as P

ADAM_STEP = 10
FULL_PRECISION = lax.Precision.HIGHEST
SOFTMAX_WARMTH = 0.03
CLIP_NORM = 0.01
RATES = (0.1, 0.05, 0.3, 0.1, 0.2, 0.1, 0.1)
BETA_ONE = 0.9
BETA_TWO = 0.95
EPSILON = 1e-08
WEIGHT_DECAY = 0.1
F32 = jnp.float32
BF16 = jnp.bfloat16
MESH_ID = pl.DeviceIdType.MESH
VMEM_LIMIT = 56 * 1024 * 1024
NT = (((1,), (1,)), ((), ()))


def dot(a, b):
    return jnp.dot(a, b, preferred_element_type=F32)


def dot_nt(a, b):
    return lax.dot_general(a, b, NT, preferred_element_type=F32)


def dot_tn(a, b):
    return lax.dot_general(a, b, (((0,), (0,)), ((), ())), preferred_element_type=F32)


def full(a, b):
    return jnp.dot(a, b, precision=FULL_PRECISION)


def dot_nt_full(a, b):
    return lax.dot_general(a, b, NT, precision=FULL_PRECISION, preferred_element_type=F32)


def norm_rows(values, gain_row, shift_row):
    centred = values - jnp.mean(values, -1, keepdims=True)
    return (
        centred * lax.rsqrt(jnp.mean(centred * centred, -1, keepdims=True) + 1e-06) * gain_row
        + shift_row
    )


def unit_rows(values):
    return values * lax.rsqrt(jnp.sum(values * values, -1, keepdims=True) + 1e-06)


def log_sum(scores):
    highest = jnp.max(scores, -1, keepdims=True)
    return highest[..., 0] + jnp.log(jnp.sum(jnp.exp(scores - highest), -1))


def adam_update(master, first, second, gradient, rate):
    first_new = BETA_ONE * first + (1.0 - BETA_ONE) * gradient
    second_new = BETA_TWO * second + (1.0 - BETA_TWO) * gradient * gradient
    first_hat = first_new / (1.0 - BETA_ONE**ADAM_STEP)
    second_hat = second_new / (1.0 - BETA_TWO**ADAM_STEP)
    master_new = master - rate * (
        first_hat / (jnp.sqrt(second_hat) + EPSILON) + WEIGHT_DECAY * master
    )
    return (master_new, first_new, second_new)


def exchange_kernel(within, parts, x_ref, o_ref, send, recv, local):
    group = lax.axis_size("fsdp")
    member = lax.axis_index("fsdp")
    replica = lax.axis_index("dp")
    count = group if within else lax.axis_size("dp") * group
    me = member if within else replica * group + member
    barrier = pltpu.get_barrier_semaphore()

    def place(step):
        peer = lax.rem(me + step, count)
        if within:
            return peer, (replica, peer)
        return peer, (peer // group, lax.rem(peer, group))

    def part(peer):
        return x_ref.at[lax.rem(peer, group)] if parts else x_ref

    def greet(step, carry):
        pl.semaphore_signal(barrier, inc=1, device_id=place(step)[1], device_id_type=MESH_ID)
        return carry

    lax.fori_loop(1, count, greet, 0)
    mine = pltpu.make_async_copy(part(me), o_ref.at[me], local)
    mine.start()
    pl.semaphore_wait(barrier, count - 1)

    def copy(step):
        peer, device = place(step)
        return pltpu.make_async_remote_copy(
            src_ref=part(peer),
            dst_ref=o_ref.at[me],
            send_sem=send.at[step],
            recv_sem=recv.at[step],
            device_id=device,
            device_id_type=MESH_ID,
        )

    def begin(step, carry):
        copy(step).start()
        return carry

    def finish(step, carry):
        copy(step).wait()
        return carry

    lax.fori_loop(1, count, begin, 0)
    mine.wait()
    lax.fori_loop(1, count, finish, 0)


def everyone(x, collective, within=False, parts=False):
    group = lax.axis_size("fsdp")
    count = group if within else lax.axis_size("dp") * group
    return pl.pallas_call(
        functools.partial(exchange_kernel, within, parts),
        out_shape=jax.ShapeDtypeStruct((count,) + x.shape[1 if parts else 0 :], x.dtype),
        in_specs=[pl.BlockSpec(memory_space=pltpu.VMEM)],
        out_specs=pl.BlockSpec(memory_space=pltpu.VMEM),
        scratch_shapes=[
            pltpu.SemaphoreType.DMA((count,)),
            pltpu.SemaphoreType.DMA((count,)),
            pltpu.SemaphoreType.DMA,
        ],
        compiler_params=pltpu.CompilerParams(collective_id=collective, has_side_effects=True),
        name=f"everyone_{collective}",
    )(x)


def pack(values):
    rows = values.reshape(values.shape[0], -1)
    return jnp.pad(rows, ((0, 0), (0, -rows.shape[1] % 1024))).reshape(rows.shape[0], -1, 128)


def unpack(values, shape):
    size = 1
    for length in shape:
        size *= length
    return values.reshape(values.shape[0], -1)[:, :size].reshape((values.shape[0],) + shape)


def attend_kernel(rows, block, masked, *refs):
    if masked:
        qkv_ref, bias_ref, o_ref, l_ref = refs
    else:
        qkv_ref, o_ref, l_ref = refs
    lane = lax.broadcasted_iota(jnp.int32, (1, 128), 1)
    low = lane < 64
    keys = qkv_ref[:, 128:256]
    values = qkv_ref[:, 256:384]
    for at in range(0, rows, block):
        queries = qkv_ref[at : at + block, :128]
        outs, totals = [], []
        for head in range(2):
            picked = jnp.where(low if head == 0 else ~low, queries, 0) * jnp.array(0.125, BF16)
            scores = dot_nt(picked, keys)
            if masked:
                scores = scores + bias_ref[at : at + block, :]
            highest = jnp.max(scores, -1, keepdims=True)
            exponent = jnp.exp(scores - highest)
            summed = jnp.sum(exponent, -1, keepdims=True)
            outs.append(dot(exponent.astype(BF16), values) * (1.0 / summed))
            totals.append(highest + jnp.log(summed))
        o_ref[at : at + block, :] = jnp.where(low, outs[0], outs[1]).astype(BF16)
        l_ref[at : at + block, :] = jnp.where(low, totals[0], totals[1])


def attend(qkv, bias, block):
    rows, width = qkv.shape
    pairs = width // 384
    specs = [pl.BlockSpec((rows, 384), lambda j: (0, j))]
    args = [qkv]
    if bias is not None:
        specs.append(pl.BlockSpec(bias.shape, lambda j: (0, 0)))
        args.append(bias)
    return pl.pallas_call(
        functools.partial(attend_kernel, rows, block, bias is not None),
        grid=(pairs,),
        out_shape=(
            jax.ShapeDtypeStruct((rows, pairs * 128), BF16),
            jax.ShapeDtypeStruct((rows, pairs * 128), F32),
        ),
        in_specs=specs,
        out_specs=(
            pl.BlockSpec((rows, 128), lambda j: (0, j)),
            pl.BlockSpec((rows, 128), lambda j: (0, j)),
        ),
        compiler_params=pltpu.CompilerParams(vmem_limit_bytes=VMEM_LIMIT),
        cost_estimate=pl.CostEstimate(
            flops=rows * rows * 128 * pairs,
            bytes_accessed=rows * pairs * 128,
            transcendentals=0,
        ),
        name=f"attend_{rows}",
    )(*args)


def attend_back_kernel(rows, block, masked, *refs):
    if masked:
        qkv_ref, do_ref, o_ref, l_ref, bias_ref, g_ref, dk_ref, dv_ref = refs
    else:
        qkv_ref, do_ref, o_ref, l_ref, g_ref, dk_ref, dv_ref = refs
    lane = lax.broadcasted_iota(jnp.int32, (1, 128), 1)
    low = lane < 64
    keys = qkv_ref[:, 128:256]
    values = qkv_ref[:, 256:384]
    keys_t = keys.astype(F32).T.astype(BF16)
    row = lax.broadcasted_iota(jnp.int32, (128, 1), 0)
    keys_of = [jnp.where(row < 64, keys_t, 0), jnp.where(row < 64, 0, keys_t)]
    eighth = jnp.array(0.125, BF16)
    for at in range(0, rows, block):
        queries = qkv_ref[at : at + block, :128]
        grads = do_ref[at : at + block, :]
        totals_t = l_ref[at : at + block, :].T
        product_t = (grads.astype(F32) * o_ref[at : at + block, :].astype(F32)).T
        grad_q = None
        for head in range(2):
            mask = low if head == 0 else ~low
            picked = jnp.where(mask, queries, 0) * eighth
            picked_grad = jnp.where(mask, grads, 0)
            total = totals_t[64 * head : 64 * head + 1, :]
            delta = jnp.sum(product_t[64 * head : 64 * head + 64, :], 0, keepdims=True)
            scores = dot_nt(keys, picked)
            if masked:
                scores = scores + bias_ref[:, at : at + block]
            weights = jnp.exp(scores - total)
            grad_weights = dot_nt(values, picked_grad)
            grad_scores = (weights * (grad_weights - delta)).astype(BF16)
            part_v = dot(weights.astype(BF16), picked_grad)
            part_k = dot(grad_scores, picked)
            if at == 0 and head == 0:
                dv_ref[...] = part_v
                dk_ref[...] = part_k
            else:
                dv_ref[...] += part_v
                dk_ref[...] += part_k
            part_q = dot(keys_of[head], grad_scores)
            grad_q = part_q if grad_q is None else grad_q + part_q
        g_ref[at : at + block, :128] = (grad_q.T * 0.125).astype(BF16)
    g_ref[:, 128:256] = dk_ref[...].astype(BF16)
    g_ref[:, 256:384] = dv_ref[...].astype(BF16)


def attend_back(qkv, grad_out, out, totals, bias, block, begin=0, end=None, buffer=None):
    rows, width = qkv.shape
    pairs = (width // 384 if end is None else end) - begin
    specs = [
        pl.BlockSpec((rows, 384), lambda j: (0, begin + j)),
        pl.BlockSpec((rows, 128), lambda j: (0, begin + j)),
        pl.BlockSpec((rows, 128), lambda j: (0, begin + j)),
        pl.BlockSpec((rows, 128), lambda j: (0, begin + j)),
    ]
    args = [qkv, grad_out, out, totals]
    if bias is not None:
        specs.append(pl.BlockSpec(bias.shape, lambda j: (0, 0)))
        args.append(bias)
    kernel = functools.partial(attend_back_kernel, rows, block, bias is not None)
    aliases = {}
    if buffer is not None:
        aliases = {len(args): 0}
        specs.append(pl.BlockSpec(memory_space=pl.ANY))
        at = len(args)
        args.append(buffer)
        inner = kernel

        def kernel(*refs):
            return inner(*refs[:at], *refs[at + 1 :])

    return pl.pallas_call(
        kernel,
        grid=(pairs,),
        out_shape=jax.ShapeDtypeStruct(qkv.shape, BF16),
        in_specs=specs,
        out_specs=pl.BlockSpec((rows, 384), lambda j: (0, begin + j)),
        scratch_shapes=[pltpu.VMEM((rows, 128), F32), pltpu.VMEM((rows, 128), F32)],
        compiler_params=pltpu.CompilerParams(vmem_limit_bytes=VMEM_LIMIT),
        cost_estimate=pl.CostEstimate(
            flops=2 * rows * rows * 128 * pairs,
            bytes_accessed=rows * pairs * 128,
            transcendentals=0,
        ),
        input_output_aliases=aliases,
        name=f"attend_back_{rows}_{begin}",
    )(*args)


def column_runs(features, width):
    runs = [
        (kind * features + pair * 128, (3 * pair + kind) * 128, 128)
        for pair in range(features // 128)
        for kind in range(3)
    ]
    return runs + [(3 * features, 3 * features, width - 3 * features)]


def gradient_runs(features, width):
    upper = width - 4 * features
    runs = column_runs(features, width)[:-1]
    towers = []
    half = features // 2
    tower = [(1, width + at, begin, size) for begin, at, size in runs]
    tower.append((1, width + 3 * features, 3 * features, features))
    tower.append((0, upper, 4 * features, upper))
    towers.append(tower)
    tower = [(2, at + at // (3 * half) * half, begin, size) for begin, at, size in runs]
    for side in range(2):
        spot = (4 * side + 3) * half
        tower.append((2, spot, 3 * features + side * half, half))
    tower.append((0, 0, 4 * features, upper))
    towers.append(tower)
    tower = [(1, at, begin, size) for begin, at, size in runs]
    tower.append((1, 3 * features, 3 * features, width - 3 * features))
    return towers + [tower]


def regroup_kernel(runs, w_ref, low_ref):
    for begin, at, size in runs:
        low_ref[0, :, at : at + size] = w_ref[0, :, begin : begin + size].astype(BF16)


def regroup(mixing, features):
    towers, rows, width = mixing.shape
    spec = pl.BlockSpec((1, rows, width), lambda t: (t, 0, 0))
    return pl.pallas_call(
        functools.partial(regroup_kernel, column_runs(features, width)),
        grid=(towers,),
        out_shape=jax.ShapeDtypeStruct((towers, rows, width), BF16),
        in_specs=[spec],
        out_specs=spec,
        compiler_params=pltpu.CompilerParams(vmem_limit_bytes=VMEM_LIMIT),
        name="regroup",
    )(mixing)


def adam_kernel(towers, scal_ref, *refs):
    pieces, (w_ref, first_ref, second_ref), outs = refs[:3], refs[3:6], refs[6:]
    factor = scal_ref[0]
    for tower, runs in enumerate(towers):

        @pl.when(pl.program_id(1) == tower)
        def _():
            for piece, at, begin, size in runs:
                new = adam_update(
                    w_ref[0, :, begin : begin + size],
                    first_ref[0, :, begin : begin + size],
                    second_ref[0, :, begin : begin + size],
                    pieces[piece][:, at : at + size] * factor,
                    RATES[0],
                )
                for out, value in zip(outs, new):
                    out[0, :, begin : begin + size] = value


def adam_mixing(factor, pieces, master, first, second, features):
    towers, rows, width = master.shape
    block = rows // 3 if rows % 24 == 0 else rows
    spec = pl.BlockSpec((1, block, width), lambda r, t: (t, r, 0))
    return pl.pallas_call(
        functools.partial(adam_kernel, gradient_runs(features, width)),
        grid=(rows // block, towers),
        out_shape=(jax.ShapeDtypeStruct(master.shape, F32),) * 3,
        in_specs=[pl.BlockSpec(memory_space=pltpu.SMEM)]
        + [pl.BlockSpec((block, piece.shape[1]), lambda r, t: (r, 0)) for piece in pieces]
        + [spec] * 3,
        out_specs=(spec,) * 3,
        compiler_params=pltpu.CompilerParams(vmem_limit_bytes=VMEM_LIMIT),
        name="adam_mixing",
    )(factor.reshape(1), *pieces, master, first, second)


def scale_kernel(first_ref, second_ref, slopes_ref, out_ref):
    width = first_ref.shape[1]
    for at, ref in enumerate((first_ref, second_ref)):
        part = ref[...].astype(F32) * slopes_ref[at : at + 1, :]
        out_ref[:, at * width : (at + 1) * width] = part.astype(BF16)


def scale_columns(first, second, slopes):
    rows, width = first.shape
    block = rows // 6
    spec = pl.BlockSpec((block, width), lambda j: (j, 0))
    return pl.pallas_call(
        scale_kernel,
        grid=(rows // block,),
        out_shape=jax.ShapeDtypeStruct((rows, 2 * width), BF16),
        in_specs=[spec, spec, pl.BlockSpec(slopes.shape, lambda j: (0, 0))],
        out_specs=pl.BlockSpec((block, 2 * width), lambda j: (j, 0)),
        compiler_params=pltpu.CompilerParams(vmem_limit_bytes=VMEM_LIMIT),
        name="scale_columns",
    )(first, second, slopes)


def patch_kernel(tile, video_ref, entry_ref, out_ref):
    patch = video_ref.shape[2]
    for at in range(0, patch, tile):
        out_ref[at : at + tile, :] = dot_tn(video_ref[0, :, at : at + tile], entry_ref[...]).astype(
            BF16
        )
    out_ref[patch:, :] = jnp.zeros((out_ref.shape[0] - patch, out_ref.shape[1]), BF16)


def patch_grads(video, entry, rows):
    return pl.pallas_call(
        functools.partial(patch_kernel, 512),
        out_shape=jax.ShapeDtypeStruct((rows, entry.shape[1]), BF16),
        in_specs=[pl.BlockSpec(memory_space=pltpu.VMEM)] * 2,
        out_specs=pl.BlockSpec(memory_space=pltpu.VMEM),
        compiler_params=pltpu.CompilerParams(vmem_limit_bytes=VMEM_LIMIT),
        name="patch_grads",
    )(video, entry)


def middle_kernel(
    scales, captions, sum_ref, base_ref, scale_ref, backs_ref, gains_ref, heads_ref, vt_ref,
    live_ref, pos_ref, count_ref,
    loss_ref, dv_ref, da_ref, dt_ref, gg_ref, z_ref, zt_ref, de_ref, dt_e_ref, ev_ref, dvt_ref,
    r1_ref, slope_ref,
    x1_ref, x2_ref, r2_ref, x3_ref, r3_ref, x4_ref, r4_ref, send, recv,
):
    group = lax.axis_size("fsdp")
    clips = lax.axis_size("dp") * group
    member = lax.axis_index("fsdp")
    replica = lax.axis_index("dp")
    me = replica * group + member
    part = backs_ref.shape[1]
    joint = vt_ref.shape[0]
    own_group = pl.ds(pl.multiple_of(replica * group, group), group)
    barrier = pltpu.get_barrier_semaphore()

    def place(step):
        peer = lax.rem(me + step, clips)
        return peer, (peer // group, lax.rem(peer, group))

    def near(step):
        peer = lax.rem(member + step, group)
        return peer, (replica, peer)

    def greet(step, carry):
        pl.semaphore_signal(barrier, inc=1, device_id=place(step)[1], device_id_type=MESH_ID)
        return carry

    def exchange(phase, count, where, source, target):
        def copy(step):
            peer, device = where(step)
            return pltpu.make_async_remote_copy(
                src_ref=source(peer),
                dst_ref=target,
                send_sem=send.at[phase, step],
                recv_sem=recv.at[phase, step],
                device_id=device,
                device_id_type=MESH_ID,
            )

        def begin(step, carry):
            copy(step).start()
            return carry

        def finish(step, carry):
            copy(step).wait()
            return carry

        lax.fori_loop(1, count, begin, 0)
        lax.fori_loop(1, count, finish, 0)

    def times(a, b, dims):
        return lax.dot_general(
            a, b, (dims, ((), ())), precision=FULL_PRECISION, preferred_element_type=F32
        )

    plain, right, left = ((1,), (0,)), ((1,), (1,)), ((0,), (0,))
    lax.fori_loop(1, clips, greet, 0)
    x1_ref[...] = jnp.zeros_like(x1_ref)
    x2_ref[...] = jnp.zeros_like(x2_ref)
    x4_ref[...] = jnp.zeros_like(x4_ref)
    for at in range(group):
        x1_ref[at, :, :part] = sum_ref[:, at * part : (at + 1) * part]
    pl.semaphore_wait(barrier, clips - 1)
    r1_ref[me] = x1_ref[member]
    exchange(0, clips, place, lambda peer: x1_ref.at[lax.rem(peer, group)], r1_ref.at[me])
    for k in range(2 + captions):
        x2_ref[:, k, :] = times(r1_ref[own_group, k, :part], backs_ref[min(k, 2)], plain)
    r2_ref[member] = x2_ref[member]
    exchange(1, group, near, lambda peer: x2_ref.at[peer], r2_ref.at[member])
    x3_ref[...] = (jnp.sum(r2_ref[...], 0) + base_ref[...]) * scale_ref[...]
    r3_ref[me] = x3_ref[...]
    exchange(2, clips, place, lambda peer: x3_ref, r3_ref.at[me])
    texts = jnp.concatenate([r3_ref[:, 2 + k, :] for k in range(captions)], 0)


    def normalise(values):
        centred = values - jnp.mean(values, -1, keepdims=True)
        inverse = lax.rsqrt(jnp.mean(centred * centred, -1, keepdims=True) + 1e-06)
        return centred * inverse, inverse

    def unit(values):
        scale = lax.rsqrt(jnp.sum(values * values, -1, keepdims=True) + 1e-06)
        return values * scale, scale

    def unit_back(values, scale, grads):
        along = jnp.sum(values * grads, -1, keepdims=True)
        return scale * grads - values * (scale * scale * scale * along)

    def soft(scores):
        highest = jnp.max(scores, -1, keepdims=True)
        exponent = jnp.exp(scores - highest)
        total = jnp.sum(exponent, -1, keepdims=True)
        return highest + jnp.log(total), exponent * (1.0 / total)

    hats, z = [], []
    for t, rows in enumerate((r3_ref[:, 0, :], r3_ref[:, 1, :], texts)):
        hat, inverse = normalise(rows)
        hats.append((hat, inverse))
        z.append(hat * gains_ref[2 * t : 2 * t + 1, :] + gains_ref[2 * t + 1 : 2 * t + 2, :])
    heads = heads_ref[...].astype(F32)
    parts = (heads[:, :joint], heads[:, joint : 2 * joint], heads[:, 2 * joint :])
    video_text = vt_ref[...].astype(F32)
    e_video = times(z[0], parts[0], plain)
    e_both = times(e_video, video_text, plain)
    e_audio = times(z[1], parts[1], plain)
    e_text = times(z[2], parts[2], plain)
    (n_video, s_video), (n_both, s_both) = unit(e_video), unit(e_both)
    (n_audio, s_audio), (n_text, s_text) = unit(e_audio), unit(e_text)
    scores = times(n_video, n_audio, right) / SOFTMAX_WARMTH
    own = lax.broadcasted_iota(jnp.int32, scores.shape, 0) == lax.broadcasted_iota(
        jnp.int32, scores.shape, 1
    )
    total, share = soft(scores)
    matched = total - jnp.sum(jnp.where(own, scores, 0.0), -1, keepdims=True)
    d_scores = (share - jnp.where(own, 1.0, 0.0)) * (1.0 / (clips * SOFTMAX_WARMTH))
    live = live_ref[...]
    positive = pos_ref[...]
    text_scores = times(n_both, n_text, right) / SOFTMAX_WARMTH
    every, every_share = soft(jnp.where(live > 0.5, text_scores, -1e30))
    chosen, chosen_share = soft(jnp.where(positive > 0.5, text_scores, -1e30))
    weight = jnp.sum(positive, -1, keepdims=True) / jnp.sum(live)
    loss = jnp.sum(matched) / clips + jnp.sum(weight * (every - chosen))
    loss_ref[...] = jnp.broadcast_to(loss, loss_ref.shape)
    d_text_scores = (every_share * live - chosen_share * positive) * (weight / SOFTMAX_WARMTH)
    d_video = unit_back(e_video, s_video, times(d_scores, n_audio, plain))
    d_audio = unit_back(e_audio, s_audio, times(d_scores, n_video, left))
    d_both = unit_back(e_both, s_both, times(d_text_scores, n_text, plain))
    d_text = unit_back(e_text, s_text, times(d_text_scores, n_both, left))
    d_video = d_video + times(d_both, video_text, right)
    for t, (grad, out) in enumerate(((d_video, dv_ref), (d_audio, da_ref), (d_text, dt_ref))):
        d_z = times(grad, parts[t], right)
        hat, inverse = hats[t]
        gg_ref[2 * t : 2 * t + 1, :] = jnp.sum(d_z * hat, 0, keepdims=True)
        gg_ref[2 * t + 1 : 2 * t + 2, :] = jnp.sum(d_z, 0, keepdims=True)
        d_hat = d_z * gains_ref[2 * t : 2 * t + 1, :]
        inner = d_hat - jnp.mean(d_hat, -1, keepdims=True)
        rows = inverse * (inner - hat * jnp.mean(d_hat * hat, -1, keepdims=True))
        out[...] = rows * scales[t] if t < 2 else rows / count_ref[...]
    z_ref[0] = z[0]
    z_ref[1] = z[1]
    zt_ref[...] = z[2]
    de_ref[0] = d_video
    de_ref[1] = d_audio
    dt_e_ref[...] = d_text
    ev_ref[...] = e_video
    dvt_ref[...] = d_both
    for k in range(2 + captions):
        if k < 2:
            rows = (dv_ref, da_ref)[k][own_group, :]
        else:
            begin = pl.multiple_of((k - 2) * clips + replica * group, group)
            rows = dt_ref[pl.ds(begin, group), :]
        x4_ref[:, k, :part] = times(rows.astype(BF16).astype(F32), backs_ref[min(k, 2)], right)
    r4_ref[member] = x4_ref[member]
    exchange(3, group, near, lambda peer: x4_ref.at[peer], r4_ref.at[member])
    for at in range(group):
        slope_ref[:, at * part : (at + 1) * part] = r4_ref[at, :, :part]


def contrast(scales, captions, sums, bases, token_scales, backs, gains, heads, video_text, *masks):
    group = lax.axis_size("fsdp")
    clips = lax.axis_size("dp") * group
    features = bases.shape[1]
    texts = captions * clips
    joint, width = video_text.shape
    part = backs.shape[1]
    padded = part + -part % 128
    shapes = [
        (8, 128),
        (clips, features),
        (clips, features),
        (texts, features),
        (8, features),
        (2, clips, features),
        (texts, features),
        (2, clips, joint),
        (texts, width),
        (clips, joint),
        (clips, width),
        (clips, 8, padded),
        (8, part * group),
    ]
    return pl.pallas_call(
        functools.partial(middle_kernel, scales, captions),
        out_shape=tuple(jax.ShapeDtypeStruct(shape, F32) for shape in shapes),
        in_specs=[pl.BlockSpec(memory_space=pltpu.VMEM)] * 10,
        out_specs=tuple(pl.BlockSpec(memory_space=pltpu.VMEM) for _ in shapes),
        scratch_shapes=[
            pltpu.VMEM((group, 8, padded), F32),
            pltpu.VMEM((group, 8, features), F32),
            pltpu.VMEM((group, 8, features), F32),
            pltpu.VMEM((8, features), F32),
            pltpu.VMEM((clips, 8, features), F32),
            pltpu.VMEM((group, 8, padded), F32),
            pltpu.VMEM((group, 8, padded), F32),
            pltpu.SemaphoreType.DMA((4, clips)),
            pltpu.SemaphoreType.DMA((4, clips)),
        ],
        compiler_params=pltpu.CompilerParams(
            vmem_limit_bytes=VMEM_LIMIT, collective_id=1, has_side_effects=True
        ),
        name="middle",
    )(sums, bases, token_scales, backs, gains, heads, video_text, *masks)


def feed_kernel(with_product, h_ref, w_ref, sel_ref, slope_ref, sums_ref, *rest):
    hidden = dot(h_ref[...], w_ref[...])
    root = 0.7978845608028654
    square = hidden * hidden
    tang = jnp.tanh(root * hidden * (1.0 + 0.044715 * square))
    half = 0.5 * (1.0 + tang)
    active = (hidden * half).astype(BF16)
    slope = half + (0.5 * root) * hidden * (1.0 - tang * tang) * (1.0 + (3 * 0.044715) * square)
    slope = slope.astype(BF16)
    slope_ref[...] = slope
    if with_product:
        sums_ref[...] = jnp.broadcast_to(
            jnp.sum(active.astype(F32), 0, keepdims=True), sums_ref.shape
        )
        rest[0][...] = dot_tn(h_ref[...], slope).astype(BF16)
    else:
        sums_ref[...] = dot(sel_ref[...], active)


def feed(normed, weight, column, select, tile, with_product):
    rows, features = normed.shape
    width = weight.shape[1] - column
    first = column // tile
    shapes = [
        jax.ShapeDtypeStruct((rows, width), BF16),
        jax.ShapeDtypeStruct((8, width), F32),
    ]
    outs = [
        pl.BlockSpec((rows, tile), lambda j: (0, j)),
        pl.BlockSpec((8, tile), lambda j: (0, j)),
    ]
    if with_product:
        shapes.append(jax.ShapeDtypeStruct((features, width), BF16))
        outs.append(pl.BlockSpec((features, tile), lambda j: (0, j)))
    return pl.pallas_call(
        functools.partial(feed_kernel, with_product),
        grid=(width // tile,),
        out_shape=tuple(shapes),
        in_specs=[
            pl.BlockSpec((rows, features), lambda j: (0, 0)),
            pl.BlockSpec((features, tile), lambda j: (0, first + j)),
            pl.BlockSpec(select.shape, lambda j: (0, 0)),
        ],
        out_specs=tuple(outs),
        compiler_params=pltpu.CompilerParams(vmem_limit_bytes=VMEM_LIMIT),
        cost_estimate=pl.CostEstimate(
            flops=rows * features * width // 8,
            bytes_accessed=rows * width,
            transcendentals=0,
        ),
        name=f"feed_{rows}",
    )(normed, weight, select)


def both_columns(own, other, core):
    first = jnp.where(core == 0, own, other)
    second = jnp.where(core == 0, other, own)
    return jnp.concatenate([first, second], -1)


def attention_forward(stream, bias, mixing, gains, block):
    features = stream.shape[1]
    normed = norm_rows(stream, gains[0], gains[1]).astype(BF16)
    joined = dot(normed, mixing[:, : 3 * features]).astype(BF16)
    return normed, joined, attend(joined, bias, block)


def feed_forward(stream, mixed, mixing, upper, column, gains, select, with_product):
    features = stream.shape[1]
    middle = stream + dot(mixed, mixing[:, 3 * features : 4 * features])
    normed = norm_rows(middle, gains[2], gains[3]).astype(BF16)
    return middle, normed, feed(normed, upper, column, select, 512, with_product)


def output_backward(grad_rows, grad_normed, mixed, middle, mixing, gains):
    features = middle.shape[1]
    grad_norm, grad_gain, grad_shift = jax.vjp(norm_rows, middle, gains[2], gains[3])[1](
        grad_normed
    )
    grad_middle = grad_rows + grad_norm
    grad_attention = grad_middle.astype(BF16)
    grad_mixed = dot_nt(grad_attention, mixing[:, 3 * features : 4 * features]).astype(BF16)
    grad_output = dot_tn(mixed, grad_attention).astype(BF16)
    return grad_middle, grad_output, grad_mixed, [grad_gain, grad_shift]


def input_backward(grad_middle, grad_joined, stream, mixing, gains):
    features = stream.shape[1]
    grad_normed = dot_nt(grad_joined, mixing[:, : 3 * features])
    grad_norm, grad_gain, grad_shift = jax.vjp(norm_rows, stream, gains[0], gains[1])[1](
        grad_normed
    )
    return (grad_middle + grad_norm).astype(BF16), [grad_gain, grad_shift]


def both_columns(own, other, core):
    first = jnp.where(core == 0, own, other)
    second = jnp.where(core == 0, other, own)
    return jnp.concatenate([first, second], -1)


class Links:
    def __init__(self):
        self.group = lax.axis_size("fsdp")
        self.replicas = lax.axis_size("dp")
        self.member = lax.axis_index("fsdp")
        self.replica = lax.axis_index("dp")
        self.core = self.member % 2
        self.paired = self.group == 16 and self.replicas == 2
        self.carried = []

    def swap(self, values, name):
        if name == "y":
            return lax.ppermute(values, "dp", [(0, 1), (1, 0)])
        if name == "corner":
            count = 2 * self.group
            pairs = [(f, (f + self.group) % count ^ 1) for f in range(count)]
            return lax.ppermute(values, ("dp", "fsdp"), pairs)
        bit = {"core": 1, "x": 2, "near": 4, "far": 8, "across": 12}[name]
        return lax.ppermute(values, "fsdp", [(f, f ^ bit) for f in range(self.group)])

    def bit(self, name):
        if name == "y":
            return self.replica
        return (self.member // {"core": 1, "x": 2, "near": 4, "far": 8}[name]) % 2

    def merge(self, values, other, names, name, order=("far", "near", "x", "core", "y")):
        names = sorted(names + [name], key=order.index)
        at = names.index(name)
        place = lax.broadcasted_iota(jnp.int32, (2,) + (1,) * (values.ndim - at), 0)
        joined = jnp.where(
            place == self.bit(name), jnp.expand_dims(values, at), jnp.expand_dims(other, at)
        )
        return joined, names

    def sides(self, values, names, name):
        at = names.index(name)
        bit = self.bit(name)
        give = lax.dynamic_index_in_dim(values, 1 - bit, at, keepdims=False)
        keep = lax.dynamic_index_in_dim(values, bit, at, keepdims=False)
        return keep, give, [n for n in names if n != name]

    def spread(self, values):
        for name in ("core", "x", "near", "far"):
            other = yield values, name
            values = jnp.where(self.bit(name) == 1, values, other)
        return values

    def gather_clips(self, values):
        if not self.paired:
            return lax.all_gather(values, ("dp", "fsdp"), axis=0, tiled=True)
        names = []
        order = ["y", "far", "near", "x", "core"]
        one, two, three = yield [(values, "near"), (values, "far"), (values, "across")]
        values, _ = self.merge(values, one, [], "near", order)
        others, names = self.merge(two, three, [], "near", order)
        values, names = self.merge(values, others, names, "far", order)
        for name in ("y", "x", "core"):
            other = yield values, name
            values, names = self.merge(values, other, names, name, order)
        return values.reshape(-1, values.shape[-1])

    def sum_replicas(self, part):
        if not self.paired:
            return lax.psum(part, "dp").astype(F32)
        other = yield part, "y"
        return part.astype(F32) + other.astype(F32)

    def gather_rows(self, shard, order):
        rows, width = shard.shape
        half = width // 2
        if not self.paired:
            return lax.all_gather(shard, "fsdp", axis=0, tiled=True)
        values = lax.dynamic_slice_in_dim(shard, self.replica * half, half, 1)
        names = []
        for name in order + ("core",):
            other = yield values, name
            if name == "y":
                values = both_columns(values, other, self.replica)
            else:
                values, names = self.merge(values, other, names, name)
        return values.reshape(self.group * rows, width)

    def reduce_line(self, values):
        far, near = self.bit("far"), self.bit("near")

        def part(at_far, at_near):
            begin = (at_far, at_near) + (0,) * (values.ndim - 2)
            return lax.dynamic_slice(values, begin, (1, 1) + values.shape[2:])[0, 0]

        others = yield [
            (part(far, 1 - near), "near"),
            (part(1 - far, near), "far"),
            (part(1 - far, 1 - near), "across"),
        ]
        total = part(far, near).astype(F32)
        for other in others:
            total = total + other.astype(F32)
        return total.astype(BF16)

    def reduce_columns(self, own, other, order):
        rows, half = own.shape
        part = rows // self.group
        if not self.paired:
            whole = both_columns(own, other, self.core)
            whole = lax.psum_scatter(whole, "fsdp", scatter_dimension=0, tiled=True)
            return lax.psum(whole, "dp")
        other = yield other, "core"
        values = add(own, other).reshape(2, 2, 2, 2, 2, part // 2, half)
        names = ["far", "near", "x", "core", "y"]
        for name in order:
            keep, give, names = self.sides(values, names, name)
            other = yield give, name
            values = add(keep, other)
        return (yield from self.reduce_line(values))

    def scatter_columns(self, own, other, order):
        values = yield from self.reduce_columns(own, other, order)
        if not self.paired:
            return values.astype(F32)
        mine, give, _ = self.sides(values, ["core"], "core")
        beside, across, corner = yield [(give, "core"), (mine, "y"), (give, "corner")]
        near = both_columns(mine, beside, self.core)
        far = both_columns(across, corner, self.core)
        values, _ = self.merge(near, far, [], "y")
        return values.reshape(2 * values.shape[1], values.shape[2]).astype(F32)

    def scatter_rows(self, values, order):
        rows, width = values.shape
        part = rows // self.group
        half = width // 2
        if not self.paired:
            part_sum = lax.psum_scatter(values, "fsdp", scatter_dimension=0, tiled=True)
            return lax.psum(part_sum, "dp").astype(F32)
        values = values.reshape(2, 2, 2, 2, part, width)
        names = ["far", "near", "x", "core"]
        for name in ("core",) + order:
            if name == "y":
                last = values.ndim - 1
                give = lax.dynamic_slice_in_dim(values, (1 - self.replica) * half, half, last)
                keep = lax.dynamic_slice_in_dim(values, self.replica * half, half, last)
            else:
                keep, give, names = self.sides(values, names, name)
            other = yield give, name
            values = add(keep, other)
        values = yield from self.reduce_line(values)
        other = yield values, "y"
        return both_columns(values, other, self.replica).astype(F32)

    def scatter_words(self, values):
        rows, width = values.shape
        if not self.paired:
            return lax.psum_scatter(values, "fsdp", scatter_dimension=0, tiled=True)
        values = values.reshape(2, 2, 2, 2, rows // self.group, width)
        names = ["far", "near", "x", "core"]
        for name in ("core", "x", "far", "near"):
            keep, give, names = self.sides(values, names, name)
            other = yield give, name
            values = add(keep, other)
        return values

    def stage(self, flows, work=None, inputs=(), slow=()):
        slow = [flow for flow in slow if flow.request is not None]
        active = [flow for flow in flows if flow.request is not None]
        every = active + slow
        asked = [flow.request if isinstance(flow.request, list) else [flow.request] for flow in every]
        held = [[values for values, _ in asks] for asks in asked]
        held, inputs = lax.optimization_barrier((held, inputs))
        sent = [
            [self.swap(values, name) for values, (_, name) in zip(group, asks)]
            for group, asks in zip(held, asked)
        ]
        ending = list(zip(active, sent)) + self.carried
        self.carried = list(zip(slow, sent[len(active) :]))
        made = work(*inputs) if work is not None else ()
        received, made = lax.optimization_barrier(([others for _, others in ending], made))
        for (flow, _), others in zip(ending, received):
            flow.push(others if isinstance(flow.request, list) else others[0])
        return made


class Flow:
    def __init__(self, steps):
        self.steps = steps
        self.value = None
        self.push(None)

    def push(self, other):
        try:
            self.request = self.steps.send(other)
        except StopIteration as end:
            self.request, self.value = None, end.value


def add(left, right):
    return (left.astype(F32) + right.astype(F32)).astype(BF16)


def body(
    video,
    audio,
    word_ids,
    word_counts,
    caption_counts,
    caption_clips,
    mixing_in,
    mixing_in_first,
    mixing_in_second,
    mixing_out,
    mixing_out_first,
    mixing_out_second,
    norm_params,
    norm_params_first,
    norm_params_second,
    input_embed,
    input_embed_first,
    input_embed_second,
    word_table,
    word_table_first,
    word_table_second,
    head_proj,
    head_proj_first,
    head_proj_second,
    video_text_proj,
    video_text_proj_first,
    video_text_proj_second,
):
    group = lax.axis_size("fsdp")
    replicas = lax.axis_size("dp")
    clips = group * replicas
    member = lax.axis_index("fsdp")
    replica = lax.axis_index("dp")
    clip = replica * group + member
    captions, slots = word_ids.shape[1:]
    words = captions * slots
    patch = video.shape[2]
    video_count, audio_count = video.shape[1], audio.shape[1]
    features = mixing_in.shape[1] * group
    pairs = features // 128
    shard = mixing_in.shape[1]
    qkv = 3 * features

    links = Links()
    core = links.core
    half = features // 2
    joint_part, text_width = video_text_proj.shape
    table_rows = word_table.shape[0]
    gain_part = norm_params.shape[2]
    wave = audio.shape[2]
    low = regroup(mixing_in, features)

    def gather(values):
        return lax.all_gather(values, "fsdp", axis=0, tiled=True)

    weights = [None] * 3
    weights[1] = gather(low[1])
    def exchange(*parts):
        packed = jnp.concatenate([part.reshape(-1).astype(F32) for part in parts])
        packed = jnp.pad(packed, (0, -packed.shape[0] % 1024)).reshape(-1, 128)
        return everyone(packed, 0).reshape(clips, -1)

    embed_low = input_embed.astype(BF16)
    embed_flow = Flow(links.gather_rows(embed_low, ("near", "far", "x", "y")))
    wave_flow = Flow(links.spread(embed_low[-wave:])) if links.paired else embed_flow
    every = links.stage(
        [embed_flow, wave_flow],
        exchange,
        (word_ids, word_counts, caption_counts, caption_clips, norm_params),
    )

    def owned_rows(ids):
        local_ids = ids - member * table_rows
        owned = (local_ids >= 0) & (local_ids < table_rows)
        return jnp.clip(local_ids, 0, table_rows - 1), owned

    def pick_words(every):
        ids = every[:, :words].astype(jnp.int32)
        group_ids = lax.dynamic_slice_in_dim(ids, replica * group, group, 0).reshape(-1)
        local_ids, owned = owned_rows(group_ids)
        return jnp.where(owned[:, None], word_table[local_ids], 0.0).astype(BF16)

    picked = links.stage([embed_flow, wave_flow], pick_words, (every,))
    words_flow = Flow(links.scatter_words(picked))

    def prepare(every):
        local_ids = owned_rows(every[:, :words].astype(jnp.int32).reshape(-1))
        at = words + captions
        live = jnp.arange(captions)[:, None] < every[:, at].astype(jnp.int32)[None, :]
        live = live.reshape(1, -1)
        counts = every[:, words : words + captions].T.reshape(-1, 1)
        owners = every[:, at + 1 : at + 1 + captions].astype(jnp.int32).T.reshape(1, -1)
        positive = live & (owners == jnp.arange(clips)[:, None])
        at = at + 1 + captions
        gains_all = (
            every[:group, at : at + 18 * gain_part]
            .reshape(group, 3, 6, gain_part)
            .transpose(1, 2, 0, 3)
            .reshape(3, 6, features)
            .astype(BF16)
            .astype(F32)
        )
        outer_rows = jnp.pad(gains_all[:, 4:].reshape(6, features), ((0, 2), (0, 0)))
        masks = (live.astype(F32), positive.astype(F32), counts)
        valid = (jnp.arange(slots)[None, :] < word_counts[0][:, None]).reshape(-1)
        caption_of = jnp.arange(words) // slots
        allowed = (caption_of[:, None] == caption_of[None, :]) & valid[None, :]
        word_bias = jnp.where(allowed, 0.0, -1000000000.0).astype(F32)
        select = ((jnp.arange(8)[:, None] == caption_of[None, :]) & valid[None, :]).astype(BF16)
        own_counts = word_counts[0].astype(F32)
        sizes = jnp.array([video_count, audio_count], F32)
        scales = 1.0 / jnp.concatenate([sizes, own_counts, jnp.ones(6 - captions, F32)])
        heads_low = jnp.concatenate(
            [head_proj, jnp.pad(video_text_proj, ((0, shard - joint_part), (0, 0)))], 1
        ).astype(BF16)
        backs = mixing_out.astype(BF16).astype(F32)
        return (
            gains_all,
            outer_rows,
            masks,
            (word_bias, word_bias.T, select),
            scales[:, None],
            heads_low,
            backs,
            local_ids,
        )

    (
        gains_all,
        outer_rows,
        masks,
        (word_bias, turned_bias, select),
        token_scales,
        heads_low,
        backs,
        (local_ids, owned),
    ) = links.stage([embed_flow, wave_flow], prepare, (every,))
    unused = jnp.zeros((8, 128), BF16)
    biases = (None, None, word_bias)
    turned_biases = (None, None, turned_bias)
    selects = (unused, unused, select)
    forward_block = (512, 512, words)
    backward_block = (512, 256, words)
    normed, joined, attended, fed, streams = ([None] * 3 for _ in range(5))
    links.stage([wave_flow])
    wave_rows = wave_flow.value
    if not links.paired:
        wave_rows = wave_rows[patch:]
    streams[1] = dot(audio[0], wave_rows)

    def attention(tower, stream, mixing):
        return attention_forward(
            stream, biases[tower], mixing, gains_all[tower], forward_block[tower]
        )

    def feeding(tower, stream, mixed, mixing, upper, column):
        return feed_forward(
            stream, mixed, mixing, upper, column, gains_all[tower], selects[tower], tower < 2
        )

    streams, weights[1], low_video, low_text = lax.optimization_barrier(
        (streams, weights[1], low[0], low[2, :, : 4 * features])
    )
    weights[0] = gather(low_video)
    weights[2] = gather(low_text)
    upper_flow = Flow(links.gather_rows(low[2, :, 4 * features :], ("near", "far", "x", "y")))
    normed[1], joined[1], attended[1] = links.stage(
        [embed_flow, words_flow, upper_flow],
        lambda stream, mixing: attention(1, stream, mixing),
        (streams[1], weights[1]),
    )
    fed[1] = links.stage(
        [embed_flow, words_flow, upper_flow],
        lambda mixed: feeding(1, streams[1], mixed, weights[1], weights[1], 4 * features),
        (attended[1][0],),
    )
    embed = embed_flow.value
    fed[1], weights[0], embed = lax.optimization_barrier((fed[1], weights[0], embed))

    def video_attention(rows, mixing):
        stream = dot(video[0], rows)
        return stream, attention(0, stream, mixing)

    streams[0], (normed[0], joined[0], attended[0]) = links.stage(
        [words_flow, upper_flow], video_attention, (embed[:patch], weights[0])
    )
    fed[0] = links.stage(
        [words_flow, upper_flow],
        lambda mixed: feeding(0, streams[0], mixed, weights[0], weights[0], 4 * features),
        (attended[0][0],),
    )
    links.stage([upper_flow])
    streams[2] = words_flow.value.astype(F32)
    text_upper = upper_flow.value
    text_upper, weights[2], heads_low = lax.optimization_barrier(
        (text_upper, weights[2], heads_low)
    )
    heads_all = gather(heads_low)
    normed[2], joined[2], attended[2] = attention(2, streams[2], weights[2])
    fed[2] = feeding(2, streams[2], attended[2][0], weights[2], text_upper, 0)
    uppers = (weights[0][:, 4 * features :], weights[1][:, 4 * features :], text_upper)

    heads = heads_all[:, : head_proj.shape[1]]
    video_text = heads_all[:, head_proj.shape[1] :].reshape(group, shard, text_width)
    video_text = video_text[:, :joint_part].reshape(group * joint_part, text_width)
    slopes = [fed[t][2][0] for t in range(3)]
    products = [fed[t][2][2] for t in range(2)]
    row_sums = [fed[t][2][1] for t in range(3)]
    token_count = 2 + captions
    summed = jnp.concatenate(
        [row_sums[0][:1], row_sums[1][:1], row_sums[2][: 8 - 2]], 0
    )
    bases = jnp.concatenate(
        [
            jnp.sum(fed[0][0], 0, keepdims=True),
            jnp.sum(fed[1][0], 0, keepdims=True),
            full(select[: 8 - 2].astype(F32), fed[2][0]),
        ],
        0,
    )
    (
        loss,
        *grad_rows_all,
        outer_grads,
        z_pair,
        z_text,
        d_pair,
        d_text,
        embed_video,
        d_video_text,
        every_sum,
        sloped,
    ) = contrast(
        (1.0 / video_count, 1.0 / audio_count),
        captions,
        summed,
        bases,
        token_scales,
        backs,
        outer_rows,
        heads,
        video_text,
        *masks,
    )
    loss = loss[0, 0]
    z = (z_pair[0], z_pair[1], z_text)
    d_heads = (d_pair[0], d_pair[1], d_text)

    def own_columns(values):
        return lax.dynamic_slice_in_dim(values, member * shard, shard, 1)

    def head_grads():
        heads_grad = jnp.concatenate([full(own_columns(z[t]).T, d_heads[t]) for t in range(3)], 1)
        own = lax.dynamic_slice_in_dim(embed_video, member * joint_part, joint_part, 1)
        return heads_grad, full(own.T, d_video_text)

    branch_all = [rows.astype(BF16) for rows in grad_rows_all]

    back_part = mixing_out.shape[1]

    def back_grads():
        own = every_sum[:, :, :back_part].transpose(1, 0, 2)
        own = (own[0], own[1], own[2:token_count].reshape(-1, back_part))
        return jnp.stack([full(own[t].T, branch_all[t].astype(F32)) for t in range(3)])

    own_grads = [
        lax.dynamic_slice_in_dim(grad_rows_all[0], clip, 1, 0),
        lax.dynamic_slice_in_dim(grad_rows_all[1], clip, 1, 0),
        lax.dynamic_slice_in_dim(
            grad_rows_all[2].reshape(captions, clips, features), clip, 1, 1
        ).reshape(captions, features),
    ]
    own_slopes = (sloped[:1], sloped[1:2], sloped[2:token_count])
    ups = scale_columns(products[1], products[0], jnp.concatenate(own_slopes[1::-1], 0))
    ups, own_slopes = lax.optimization_barrier((ups, own_slopes))
    up_part = lax.psum_scatter(ups, "fsdp", scatter_dimension=0, tiled=True)
    first, second = ("y", "x"), ("x", "y")

    def hidden_backward(tower, slope):
        upper = uppers[tower]
        if tower == 2:
            spread = select[:captions].astype(F32).T
            grad_hidden = (slopes[2].astype(F32) * full(spread, slope)).astype(BF16)
            up = dot_tn(fed[2][1], grad_hidden).astype(BF16)
            return full(spread, own_grads[2]), dot_nt(grad_hidden, upper), up
        scaled = (upper.astype(F32) * slope).astype(BF16)
        return own_grads[tower], dot_nt(slopes[tower], scaled), None

    def outward_backward(tower, slope):
        rows_grad, grads, up = hidden_backward(tower, slope)
        made = output_backward(
            rows_grad, grads, attended[tower][0], fed[tower][0], weights[tower], gains_all[tower]
        )
        return made, up

    def inner_backward(tower, grad_mixed):
        return attend_back(
            joined[tower],
            grad_mixed,
            attended[tower][0],
            attended[tower][1],
            turned_biases[tower],
            backward_block[tower],
        )

    def entry_backward(tower, grad_middle, grad_joined):
        return input_backward(
            grad_middle, grad_joined, streams[tower], weights[tower], gains_all[tower]
        )

    gains_grads = [None] * 3

    def text_backward(slope):
        made, up = outward_backward(2, slope)
        grad_joined = inner_backward(2, made[2])
        inward = dot_tn(normed[2], grad_joined).astype(BF16)
        entry, entry_gains = entry_backward(2, made[0], grad_joined)
        return (inward, made[1], up), entry, entry_gains + made[3]

    text_grad, entry, gains_grads[2] = links.stage([], text_backward, (own_slopes[2],))
    word_flow = Flow(links.gather_clips(entry))
    made_video, _ = links.stage(
        [word_flow], lambda slope: outward_backward(0, slope), (own_slopes[0],)
    )
    embed_rows = input_embed.shape[0] * group

    def video_inner(grad_mixed):
        grad_joined = inner_backward(0, grad_mixed)
        inward = dot_tn(normed[0], grad_joined).astype(BF16)
        entry, entry_gains = entry_backward(0, made_video[0], grad_joined)
        return jnp.concatenate([*text_grad, inward, made_video[1]], 1), entry, entry_gains

    pair_grad, entry, entry_gains = links.stage([word_flow], video_inner, (made_video[2],))
    gains_grads[0] = entry_gains + made_video[3]
    pair_part = lax.psum_scatter(pair_grad, "fsdp", scatter_dimension=0, tiled=True)

    def video_entry(entry, slope):
        made, _ = outward_backward(1, slope)
        return patch_grads(video, entry, embed_rows), made

    grad_embed, made_audio = links.stage([word_flow], video_entry, (entry, own_slopes[1]))
    embed_flow = Flow(links.scatter_rows(grad_embed, ("y", "x")))

    def audio_pairs(grad_mixed, *bounds):
        return attend_back(
            joined[1],
            grad_mixed,
            attended[1][0],
            attended[1][1],
            None,
            backward_block[1],
            *bounds,
        )

    first_pairs = links.stage(
        [word_flow, embed_flow], lambda part: audio_pairs(part, 0, pairs // 2), (made_audio[2],)
    )

    def audio_inner(grad_mixed, first_pairs):
        grad_joined = audio_pairs(grad_mixed, pairs // 2, pairs, first_pairs)
        inward = dot_tn(normed[1], grad_joined).astype(BF16)
        sides = [
            jnp.concatenate(
                [
                    lax.dynamic_slice_in_dim(inward, at * 3 * half, 3 * half, 1),
                    lax.dynamic_slice_in_dim(made_audio[1], at * half, half, 1),
                ],
                1,
            )
            for at in (core, 1 - core)
        ]
        return grad_joined, sides

    joined_audio, audio_sides = links.stage(
        [embed_flow], audio_inner, (made_audio[2], first_pairs)
    )
    audio_flow = Flow(links.scatter_columns(*audio_sides, ("y", "x")))

    def scatter_table(every_word):
        return jax.ops.segment_sum(
            jnp.where(owned[:, None], every_word.astype(F32), 0.0),
            local_ids,
            num_segments=table_rows,
        )

    def squared(*values):
        return sum(jnp.sum(value * value) for value in values)

    def audio_entry(grad_joined):
        entry, entry_gains = entry_backward(1, made_audio[0], grad_joined)
        wave_grad = dot_tn(entry, audio[0]).astype(BF16)
        every_gain = jnp.stack(gains_grads[0] + entry_gains + made_audio[3] + gains_grads[2])
        every_gain = jnp.pad(every_gain, ((0, wave - every_gain.shape[0]), (0, 0)))
        gain_columns = every_gain.T.astype(BF16)
        return (
            jnp.where(core == 0, wave_grad, gain_columns),
            jnp.where(core == 0, gain_columns, wave_grad),
        )

    up_flow = Flow(links.sum_replicas(up_part))
    beside = links.stage([audio_flow, up_flow], audio_entry, (joined_audio,), [embed_flow])
    beside_flow = Flow(links.reduce_columns(*beside, ("y", "x")))
    rest = [audio_flow, beside_flow]
    table_grad = links.stage(rest, scatter_table, (word_flow.value,))
    back_grad, (heads_grad, video_text_grad), table_square = links.stage(
        rest,
        lambda table, up: (back_grads(), head_grads(), squared(table, up)),
        (table_grad, up_flow.value),
        [embed_flow],
    )
    pair_flow = Flow(links.sum_replicas(pair_part))
    small_square = links.stage(
        rest + [pair_flow], squared, (back_grad, heads_grad, video_text_grad)
    )
    small_square = small_square + links.stage(rest + [embed_flow], squared, (pair_flow.value,))
    pieces = (up_flow.value, pair_flow.value, audio_flow.value)
    embed_grad = embed_flow.value

    outer = lax.dynamic_slice_in_dim(outer_grads[:6], member * gain_part, gain_part, 1)
    local_square = table_square + small_square + squared(pieces[2], embed_grad, outer)
    piece = beside_flow.value.reshape(-1, wave)
    piece_square = squared(piece.astype(F32))
    marks = jnp.where(jnp.arange(128) < 64, local_square, piece_square)
    mark_rows = []
    for _ in range(3):
        mark_rows.append(marks.astype(BF16))
        marks = marks - mark_rows[-1].astype(F32)
    mark_rows = jnp.pad(jnp.stack(mark_rows), ((0, 16 - 3 + -piece.shape[0] % 16), (0, 0)))
    sent = everyone(jnp.concatenate([piece, mark_rows], 0), 2).astype(F32)
    marks = jnp.sum(sent[:, piece.shape[0] : piece.shape[0] + 3], 1)
    sent = sent[:, : piece.shape[0]]
    if links.paired:
        square = jnp.sum(marks[:group, 0]) + jnp.sum(marks[:, 127])
        placed = sent.reshape(replicas, group // 2, 2, 2, gain_part // 2, wave)
        placed = placed.transpose(2, 1, 3, 0, 4, 5).reshape(2, features, wave)
    else:
        square = jnp.sum(marks[:group, 0]) + jnp.sum(marks[:group, 127])
        placed = sent[:group].reshape(group, gain_part, 2, wave)
        placed = placed.transpose(2, 0, 1, 3).reshape(2, features, wave)
    wave_rows, gain_rows = placed[0].T, placed[1].T
    embed_part = input_embed.shape[0]
    row = member * embed_part + jnp.arange(embed_part) - patch
    chosen = (row[:, None] == jnp.arange(wave)[None, :]).astype(F32)
    inner = lax.dynamic_slice_in_dim(gain_rows[:12], member * gain_part, gain_part, 1)
    gains_grad = jnp.concatenate(
        [inner.reshape(3, 4, gain_part), outer.reshape(3, 2, gain_part)], 1
    )
    grads = (
        None,
        back_grad,
        gains_grad,
        embed_grad + full(chosen, wave_rows),
        table_grad,
        heads_grad,
        video_text_grad,
    )
    grad_norm = jnp.sqrt(square)
    factor = CLIP_NORM / jnp.maximum(grad_norm, CLIP_NORM)
    clipped = [None] + [g * factor for g in grads[1:]]
    masters = (
        mixing_in,
        mixing_out,
        norm_params,
        input_embed,
        word_table,
        head_proj,
        video_text_proj,
    )
    firsts = (
        mixing_in_first,
        mixing_out_first,
        norm_params_first,
        input_embed_first,
        word_table_first,
        head_proj_first,
        video_text_proj_first,
    )
    seconds = (
        mixing_in_second,
        mixing_out_second,
        norm_params_second,
        input_embed_second,
        word_table_second,
        head_proj_second,
        video_text_proj_second,
    )
    new = [
        adam_mixing(
            factor,
            pieces,
            mixing_in,
            mixing_in_first,
            mixing_in_second,
            features,
        )
    ]
    for i in range(1, 7):
        new.append(adam_update(masters[i], firsts[i], seconds[i], clipped[i], RATES[i]))
    outputs = [loss, grad_norm]
    for i in range(7):
        outputs += [new[i][0], clipped[4] if i == 4 else new[i][1], new[i][2]]
    return tuple(outputs)


def solution(mesh):
    both = ("dp", "fsdp")
    weight_specs = (
        P(None, "fsdp", None),
        P(None, "fsdp", None),
        P(None, None, "fsdp"),
        P("fsdp", None),
        P("fsdp", None),
        P("fsdp", None),
        P("fsdp", None),
    )
    tripled = tuple(spec for spec in weight_specs for _ in range(3))
    return jax.shard_map(
        body,
        mesh=mesh,
        in_specs=(
            P(both, None, None),
            P(both, None, None),
            P(both, None, None),
            P(both, None),
            P(both),
            P(both, None),
        )
        + tripled,
        out_specs=(P(), P()) + tripled,
        check_vma=False,
    )
```

```python
import functools

import jax
import jax.numpy as jnp
from jax import lax
from jax.experimental import pallas as pl
from jax.experimental.pallas import tpu as pltpu
from jax.sharding import PartitionSpec as P

ADAM_STEP = 10
FULL_PRECISION = lax.Precision.HIGHEST
SOFTMAX_WARMTH = 0.03
CLIP_NORM = 0.01
RATES = (0.1, 0.05, 0.3, 0.1, 0.2, 0.1, 0.1)
BETA_ONE = 0.9
BETA_TWO = 0.95
EPSILON = 1e-08
WEIGHT_DECAY = 0.1
F32 = jnp.float32
BF16 = jnp.bfloat16
MESH_ID = pl.DeviceIdType.MESH
VMEM_LIMIT = 56 * 1024 * 1024
NT = (((1,), (1,)), ((), ()))


def dot(a, b):
    return jnp.dot(a, b, preferred_element_type=F32)


def dot_nt(a, b):
    return lax.dot_general(a, b, NT, preferred_element_type=F32)


def dot_tn(a, b):
    return lax.dot_general(a, b, (((0,), (0,)), ((), ())), preferred_element_type=F32)


def full(a, b):
    return jnp.dot(a, b, precision=FULL_PRECISION)


def dot_nt_full(a, b):
    return lax.dot_general(a, b, NT, precision=FULL_PRECISION, preferred_element_type=F32)


def norm_rows(values, gain_row, shift_row):
    centred = values - jnp.mean(values, -1, keepdims=True)
    return (
        centred * lax.rsqrt(jnp.mean(centred * centred, -1, keepdims=True) + 1e-06) * gain_row
        + shift_row
    )


def unit_rows(values):
    return values * lax.rsqrt(jnp.sum(values * values, -1, keepdims=True) + 1e-06)


def log_sum(scores):
    highest = jnp.max(scores, -1, keepdims=True)
    return highest[..., 0] + jnp.log(jnp.sum(jnp.exp(scores - highest), -1))


def adam_update(master, first, second, gradient, rate):
    first_new = BETA_ONE * first + (1.0 - BETA_ONE) * gradient
    second_new = BETA_TWO * second + (1.0 - BETA_TWO) * gradient * gradient
    first_hat = first_new / (1.0 - BETA_ONE**ADAM_STEP)
    second_hat = second_new / (1.0 - BETA_TWO**ADAM_STEP)
    master_new = master - rate * (
        first_hat / (jnp.sqrt(second_hat) + EPSILON) + WEIGHT_DECAY * master
    )
    return (master_new, first_new, second_new)


def exchange_kernel(within, parts, x_ref, o_ref, send, recv, local):
    group = lax.axis_size("fsdp")
    member = lax.axis_index("fsdp")
    replica = lax.axis_index("dp")
    count = group if within else lax.axis_size("dp") * group
    me = member if within else replica * group + member
    barrier = pltpu.get_barrier_semaphore()

    def place(step):
        peer = lax.rem(me + step, count)
        if within:
            return peer, (replica, peer)
        return peer, (peer // group, lax.rem(peer, group))

    def part(peer):
        return x_ref.at[lax.rem(peer, group)] if parts else x_ref

    def greet(step, carry):
        pl.semaphore_signal(barrier, inc=1, device_id=place(step)[1], device_id_type=MESH_ID)
        return carry

    lax.fori_loop(1, count, greet, 0)
    mine = pltpu.make_async_copy(part(me), o_ref.at[me], local)
    mine.start()
    pl.semaphore_wait(barrier, count - 1)

    def copy(step):
        peer, device = place(step)
        return pltpu.make_async_remote_copy(
            src_ref=part(peer),
            dst_ref=o_ref.at[me],
            send_sem=send.at[step],
            recv_sem=recv.at[step],
            device_id=device,
            device_id_type=MESH_ID,
        )

    def begin(step, carry):
        copy(step).start()
        return carry

    def finish(step, carry):
        copy(step).wait()
        return carry

    lax.fori_loop(1, count, begin, 0)
    mine.wait()
    lax.fori_loop(1, count, finish, 0)


def everyone(x, collective, within=False, parts=False):
    group = lax.axis_size("fsdp")
    count = group if within else lax.axis_size("dp") * group
    return pl.pallas_call(
        functools.partial(exchange_kernel, within, parts),
        out_shape=jax.ShapeDtypeStruct((count,) + x.shape[1 if parts else 0 :], x.dtype),
        in_specs=[pl.BlockSpec(memory_space=pltpu.VMEM)],
        out_specs=pl.BlockSpec(memory_space=pltpu.VMEM),
        scratch_shapes=[
            pltpu.SemaphoreType.DMA((count,)),
            pltpu.SemaphoreType.DMA((count,)),
            pltpu.SemaphoreType.DMA,
        ],
        compiler_params=pltpu.CompilerParams(collective_id=collective, has_side_effects=True),
        name=f"everyone_{collective}",
    )(x)


def pack(values):
    rows = values.reshape(values.shape[0], -1)
    return jnp.pad(rows, ((0, 0), (0, -rows.shape[1] % 1024))).reshape(rows.shape[0], -1, 128)


def unpack(values, shape):
    size = 1
    for length in shape:
        size *= length
    return values.reshape(values.shape[0], -1)[:, :size].reshape((values.shape[0],) + shape)


def attend_kernel(rows, block, masked, *refs):
    if masked:
        qkv_ref, bias_ref, o_ref, l_ref = refs
    else:
        qkv_ref, o_ref, l_ref = refs
    lane = lax.broadcasted_iota(jnp.int32, (1, 128), 1)
    low = lane < 64
    keys = qkv_ref[:, 128:256]
    values = qkv_ref[:, 256:384]
    for at in range(0, rows, block):
        queries = qkv_ref[at : at + block, :128]
        outs, totals = [], []
        for head in range(2):
            picked = jnp.where(low if head == 0 else ~low, queries, 0) * jnp.array(0.125, BF16)
            scores = dot_nt(picked, keys)
            if masked:
                scores = scores + bias_ref[at : at + block, :]
            highest = jnp.max(scores, -1, keepdims=True)
            exponent = jnp.exp(scores - highest)
            summed = jnp.sum(exponent, -1, keepdims=True)
            outs.append(dot(exponent.astype(BF16), values) * (1.0 / summed))
            totals.append(highest + jnp.log(summed))
        o_ref[at : at + block, :] = jnp.where(low, outs[0], outs[1]).astype(BF16)
        l_ref[at : at + block, :] = jnp.where(low, totals[0], totals[1])


def attend(qkv, bias, block):
    rows, width = qkv.shape
    pairs = width // 384
    specs = [pl.BlockSpec((rows, 384), lambda j: (0, j))]
    args = [qkv]
    if bias is not None:
        specs.append(pl.BlockSpec(bias.shape, lambda j: (0, 0)))
        args.append(bias)
    return pl.pallas_call(
        functools.partial(attend_kernel, rows, block, bias is not None),
        grid=(pairs,),
        out_shape=(
            jax.ShapeDtypeStruct((rows, pairs * 128), BF16),
            jax.ShapeDtypeStruct((rows, pairs * 128), F32),
        ),
        in_specs=specs,
        out_specs=(
            pl.BlockSpec((rows, 128), lambda j: (0, j)),
            pl.BlockSpec((rows, 128), lambda j: (0, j)),
        ),
        compiler_params=pltpu.CompilerParams(vmem_limit_bytes=VMEM_LIMIT),
        cost_estimate=pl.CostEstimate(
            flops=rows * rows * 128 * pairs,
            bytes_accessed=rows * pairs * 128,
            transcendentals=0,
        ),
        name=f"attend_{rows}",
    )(*args)


def attend_back_kernel(rows, block, masked, *refs):
    if masked:
        qkv_ref, do_ref, o_ref, l_ref, bias_ref, g_ref, dk_ref, dv_ref = refs
    else:
        qkv_ref, do_ref, o_ref, l_ref, g_ref, dk_ref, dv_ref = refs
    lane = lax.broadcasted_iota(jnp.int32, (1, 128), 1)
    low = lane < 64
    keys = qkv_ref[:, 128:256]
    values = qkv_ref[:, 256:384]
    keys_t = keys.astype(F32).T.astype(BF16)
    row = lax.broadcasted_iota(jnp.int32, (128, 1), 0)
    keys_of = [jnp.where(row < 64, keys_t, 0), jnp.where(row < 64, 0, keys_t)]
    eighth = jnp.array(0.125, BF16)
    for at in range(0, rows, block):
        queries = qkv_ref[at : at + block, :128]
        grads = do_ref[at : at + block, :]
        totals_t = l_ref[at : at + block, :].T
        product_t = (grads.astype(F32) * o_ref[at : at + block, :].astype(F32)).T
        grad_q = None
        for head in range(2):
            mask = low if head == 0 else ~low
            picked = jnp.where(mask, queries, 0) * eighth
            picked_grad = jnp.where(mask, grads, 0)
            total = totals_t[64 * head : 64 * head + 1, :]
            delta = jnp.sum(product_t[64 * head : 64 * head + 64, :], 0, keepdims=True)
            scores = dot_nt(keys, picked)
            if masked:
                scores = scores + bias_ref[:, at : at + block]
            weights = jnp.exp(scores - total)
            grad_weights = dot_nt(values, picked_grad)
            grad_scores = (weights * (grad_weights - delta)).astype(BF16)
            part_v = dot(weights.astype(BF16), picked_grad)
            part_k = dot(grad_scores, picked)
            if at == 0 and head == 0:
                dv_ref[...] = part_v
                dk_ref[...] = part_k
            else:
                dv_ref[...] += part_v
                dk_ref[...] += part_k
            part_q = dot(keys_of[head], grad_scores)
            grad_q = part_q if grad_q is None else grad_q + part_q
        g_ref[at : at + block, :128] = (grad_q.T * 0.125).astype(BF16)
    g_ref[:, 128:256] = dk_ref[...].astype(BF16)
    g_ref[:, 256:384] = dv_ref[...].astype(BF16)


def attend_back(qkv, grad_out, out, totals, bias, block, begin=0, end=None, buffer=None):
    rows, width = qkv.shape
    pairs = (width // 384 if end is None else end) - begin
    specs = [
        pl.BlockSpec((rows, 384), lambda j: (0, begin + j)),
        pl.BlockSpec((rows, 128), lambda j: (0, begin + j)),
        pl.BlockSpec((rows, 128), lambda j: (0, begin + j)),
        pl.BlockSpec((rows, 128), lambda j: (0, begin + j)),
    ]
    args = [qkv, grad_out, out, totals]
    if bias is not None:
        specs.append(pl.BlockSpec(bias.shape, lambda j: (0, 0)))
        args.append(bias)
    kernel = functools.partial(attend_back_kernel, rows, block, bias is not None)
    aliases = {}
    if buffer is not None:
        aliases = {len(args): 0}
        specs.append(pl.BlockSpec(memory_space=pl.ANY))
        at = len(args)
        args.append(buffer)
        inner = kernel

        def kernel(*refs):
            return inner(*refs[:at], *refs[at + 1 :])

    return pl.pallas_call(
        kernel,
        grid=(pairs,),
        out_shape=jax.ShapeDtypeStruct(qkv.shape, BF16),
        in_specs=specs,
        out_specs=pl.BlockSpec((rows, 384), lambda j: (0, begin + j)),
        scratch_shapes=[pltpu.VMEM((rows, 128), F32), pltpu.VMEM((rows, 128), F32)],
        compiler_params=pltpu.CompilerParams(vmem_limit_bytes=VMEM_LIMIT),
        cost_estimate=pl.CostEstimate(
            flops=2 * rows * rows * 128 * pairs,
            bytes_accessed=rows * pairs * 128,
            transcendentals=0,
        ),
        input_output_aliases=aliases,
        name=f"attend_back_{rows}_{begin}",
    )(*args)


def column_runs(features, width):
    runs = [
        (kind * features + pair * 128, (3 * pair + kind) * 128, 128)
        for pair in range(features // 128)
        for kind in range(3)
    ]
    return runs + [(3 * features, 3 * features, width - 3 * features)]


def gradient_runs(features, width):
    upper = width - 4 * features
    runs = column_runs(features, width)[:-1]
    towers = []
    half = features // 2
    tower = [(1, width + at, begin, size) for begin, at, size in runs]
    tower.append((1, width + 3 * features, 3 * features, features))
    tower.append((0, upper, 4 * features, upper))
    towers.append(tower)
    tower = [(2, at + at // (3 * half) * half, begin, size) for begin, at, size in runs]
    for side in range(2):
        spot = (4 * side + 3) * half
        tower.append((2, spot, 3 * features + side * half, half))
    tower.append((0, 0, 4 * features, upper))
    towers.append(tower)
    tower = [(1, at, begin, size) for begin, at, size in runs]
    tower.append((1, 3 * features, 3 * features, width - 3 * features))
    return towers + [tower]


def regroup_kernel(runs, w_ref, low_ref):
    for begin, at, size in runs:
        low_ref[0, :, at : at + size] = w_ref[0, :, begin : begin + size].astype(BF16)


def regroup(mixing, features):
    towers, rows, width = mixing.shape
    spec = pl.BlockSpec((1, rows, width), lambda t: (t, 0, 0))
    return pl.pallas_call(
        functools.partial(regroup_kernel, column_runs(features, width)),
        grid=(towers,),
        out_shape=jax.ShapeDtypeStruct((towers, rows, width), BF16),
        in_specs=[spec],
        out_specs=spec,
        compiler_params=pltpu.CompilerParams(vmem_limit_bytes=VMEM_LIMIT),
        name="regroup",
    )(mixing)


def adam_kernel(towers, scal_ref, *refs):
    pieces, (w_ref, first_ref, second_ref), outs = refs[:3], refs[3:6], refs[6:]
    factor = scal_ref[0]
    for tower, runs in enumerate(towers):

        @pl.when(pl.program_id(1) == tower)
        def _():
            for piece, at, begin, size in runs:
                new = adam_update(
                    w_ref[0, :, begin : begin + size],
                    first_ref[0, :, begin : begin + size],
                    second_ref[0, :, begin : begin + size],
                    pieces[piece][:, at : at + size] * factor,
                    RATES[0],
                )
                for out, value in zip(outs, new):
                    out[0, :, begin : begin + size] = value


def adam_mixing(factor, pieces, master, first, second, features):
    towers, rows, width = master.shape
    block = rows
    spec = pl.BlockSpec((1, block, width), lambda r, t: (t, r, 0))
    return pl.pallas_call(
        functools.partial(adam_kernel, gradient_runs(features, width)),
        grid=(rows // block, towers),
        out_shape=(jax.ShapeDtypeStruct(master.shape, F32),) * 3,
        in_specs=[pl.BlockSpec(memory_space=pltpu.SMEM)]
        + [pl.BlockSpec((block, piece.shape[1]), lambda r, t: (r, 0)) for piece in pieces]
        + [spec] * 3,
        out_specs=(spec,) * 3,
        compiler_params=pltpu.CompilerParams(vmem_limit_bytes=VMEM_LIMIT),
        name="adam_mixing",
    )(factor.reshape(1), *pieces, master, first, second)


def scale_kernel(first_ref, second_ref, slopes_ref, out_ref):
    width = first_ref.shape[1]
    for at, ref in enumerate((first_ref, second_ref)):
        part = ref[...].astype(F32) * slopes_ref[at : at + 1, :]
        out_ref[:, at * width : (at + 1) * width] = part.astype(BF16)


def scale_columns(first, second, slopes):
    rows, width = first.shape
    block = rows // 6
    spec = pl.BlockSpec((block, width), lambda j: (j, 0))
    return pl.pallas_call(
        scale_kernel,
        grid=(rows // block,),
        out_shape=jax.ShapeDtypeStruct((rows, 2 * width), BF16),
        in_specs=[spec, spec, pl.BlockSpec(slopes.shape, lambda j: (0, 0))],
        out_specs=pl.BlockSpec((block, 2 * width), lambda j: (j, 0)),
        compiler_params=pltpu.CompilerParams(vmem_limit_bytes=VMEM_LIMIT),
        name="scale_columns",
    )(first, second, slopes)


def patch_kernel(tile, video_ref, entry_ref, out_ref):
    patch = video_ref.shape[2]
    for at in range(0, patch, tile):
        out_ref[at : at + tile, :] = dot_tn(video_ref[0, :, at : at + tile], entry_ref[...]).astype(
            BF16
        )
    out_ref[patch:, :] = jnp.zeros((out_ref.shape[0] - patch, out_ref.shape[1]), BF16)


def patch_grads(video, entry, rows):
    return pl.pallas_call(
        functools.partial(patch_kernel, 512),
        out_shape=jax.ShapeDtypeStruct((rows, entry.shape[1]), BF16),
        in_specs=[pl.BlockSpec(memory_space=pltpu.VMEM)] * 2,
        out_specs=pl.BlockSpec(memory_space=pltpu.VMEM),
        compiler_params=pltpu.CompilerParams(vmem_limit_bytes=VMEM_LIMIT),
        name="patch_grads",
    )(video, entry)


def middle_kernel(
    scales, captions, sum_ref, base_ref, scale_ref, backs_ref, gains_ref, heads_ref, vt_ref,
    live_ref, pos_ref, count_ref,
    loss_ref, dv_ref, da_ref, dt_ref, gg_ref, z_ref, zt_ref, de_ref, dt_e_ref, ev_ref, dvt_ref,
    r1_ref, slope_ref,
    x1_ref, x2_ref, r2_ref, x3_ref, r3_ref, x4_ref, r4_ref, send, recv,
):
    group = lax.axis_size("fsdp")
    clips = lax.axis_size("dp") * group
    member = lax.axis_index("fsdp")
    replica = lax.axis_index("dp")
    me = replica * group + member
    part = backs_ref.shape[1]
    joint = vt_ref.shape[0]
    own_group = pl.ds(pl.multiple_of(replica * group, group), group)
    barrier = pltpu.get_barrier_semaphore()

    def place(step):
        peer = lax.rem(me + step, clips)
        return peer, (peer // group, lax.rem(peer, group))

    def near(step):
        peer = lax.rem(member + step, group)
        return peer, (replica, peer)

    def greet(step, carry):
        pl.semaphore_signal(barrier, inc=1, device_id=place(step)[1], device_id_type=MESH_ID)
        return carry

    def exchange(phase, count, where, source, target):
        def copy(step):
            peer, device = where(step)
            return pltpu.make_async_remote_copy(
                src_ref=source(peer),
                dst_ref=target,
                send_sem=send.at[phase, step],
                recv_sem=recv.at[phase, step],
                device_id=device,
                device_id_type=MESH_ID,
            )

        def begin(step, carry):
            copy(step).start()
            return carry

        def finish(step, carry):
            copy(step).wait()
            return carry

        lax.fori_loop(1, count, begin, 0)
        lax.fori_loop(1, count, finish, 0)

    def times(a, b, dims):
        return lax.dot_general(
            a, b, (dims, ((), ())), precision=FULL_PRECISION, preferred_element_type=F32
        )

    plain, right, left = ((1,), (0,)), ((1,), (1,)), ((0,), (0,))
    lax.fori_loop(1, clips, greet, 0)
    x1_ref[...] = jnp.zeros_like(x1_ref)
    x2_ref[...] = jnp.zeros_like(x2_ref)
    x4_ref[...] = jnp.zeros_like(x4_ref)
    for at in range(group):
        x1_ref[at, :, :part] = sum_ref[:, at * part : (at + 1) * part]
    pl.semaphore_wait(barrier, clips - 1)
    r1_ref[me] = x1_ref[member]
    exchange(0, clips, place, lambda peer: x1_ref.at[lax.rem(peer, group)], r1_ref.at[me])
    for k in range(2 + captions):
        x2_ref[:, k, :] = times(r1_ref[own_group, k, :part], backs_ref[min(k, 2)], plain)
    r2_ref[member] = x2_ref[member]
    exchange(1, group, near, lambda peer: x2_ref.at[peer], r2_ref.at[member])
    x3_ref[...] = (jnp.sum(r2_ref[...], 0) + base_ref[...]) * scale_ref[...]
    r3_ref[me] = x3_ref[...]
    exchange(2, clips, place, lambda peer: x3_ref, r3_ref.at[me])
    texts = jnp.concatenate([r3_ref[:, 2 + k, :] for k in range(captions)], 0)


    def normalise(values):
        centred = values - jnp.mean(values, -1, keepdims=True)
        inverse = lax.rsqrt(jnp.mean(centred * centred, -1, keepdims=True) + 1e-06)
        return centred * inverse, inverse

    def unit(values):
        scale = lax.rsqrt(jnp.sum(values * values, -1, keepdims=True) + 1e-06)
        return values * scale, scale

    def unit_back(values, scale, grads):
        along = jnp.sum(values * grads, -1, keepdims=True)
        return scale * grads - values * (scale * scale * scale * along)

    def soft(scores):
        highest = jnp.max(scores, -1, keepdims=True)
        exponent = jnp.exp(scores - highest)
        total = jnp.sum(exponent, -1, keepdims=True)
        return highest + jnp.log(total), exponent * (1.0 / total)

    hats, z = [], []
    for t, rows in enumerate((r3_ref[:, 0, :], r3_ref[:, 1, :], texts)):
        hat, inverse = normalise(rows)
        hats.append((hat, inverse))
        z.append(hat * gains_ref[2 * t : 2 * t + 1, :] + gains_ref[2 * t + 1 : 2 * t + 2, :])
    heads = heads_ref[...].astype(F32)
    parts = (heads[:, :joint], heads[:, joint : 2 * joint], heads[:, 2 * joint :])
    video_text = vt_ref[...].astype(F32)
    e_video = times(z[0], parts[0], plain)
    e_both = times(e_video, video_text, plain)
    e_audio = times(z[1], parts[1], plain)
    e_text = times(z[2], parts[2], plain)
    (n_video, s_video), (n_both, s_both) = unit(e_video), unit(e_both)
    (n_audio, s_audio), (n_text, s_text) = unit(e_audio), unit(e_text)
    scores = times(n_video, n_audio, right) / SOFTMAX_WARMTH
    own = lax.broadcasted_iota(jnp.int32, scores.shape, 0) == lax.broadcasted_iota(
        jnp.int32, scores.shape, 1
    )
    total, share = soft(scores)
    matched = total - jnp.sum(jnp.where(own, scores, 0.0), -1, keepdims=True)
    d_scores = (share - jnp.where(own, 1.0, 0.0)) * (1.0 / (clips * SOFTMAX_WARMTH))
    live = live_ref[...]
    positive = pos_ref[...]
    text_scores = times(n_both, n_text, right) / SOFTMAX_WARMTH
    every, every_share = soft(jnp.where(live > 0.5, text_scores, -1e30))
    chosen, chosen_share = soft(jnp.where(positive > 0.5, text_scores, -1e30))
    weight = jnp.sum(positive, -1, keepdims=True) / jnp.sum(live)
    loss = jnp.sum(matched) / clips + jnp.sum(weight * (every - chosen))
    loss_ref[...] = jnp.broadcast_to(loss, loss_ref.shape)
    d_text_scores = (every_share * live - chosen_share * positive) * (weight / SOFTMAX_WARMTH)
    d_video = unit_back(e_video, s_video, times(d_scores, n_audio, plain))
    d_audio = unit_back(e_audio, s_audio, times(d_scores, n_video, left))
    d_both = unit_back(e_both, s_both, times(d_text_scores, n_text, plain))
    d_text = unit_back(e_text, s_text, times(d_text_scores, n_both, left))
    d_video = d_video + times(d_both, video_text, right)
    for t, (grad, out) in enumerate(((d_video, dv_ref), (d_audio, da_ref), (d_text, dt_ref))):
        d_z = times(grad, parts[t], right)
        hat, inverse = hats[t]
        gg_ref[2 * t : 2 * t + 1, :] = jnp.sum(d_z * hat, 0, keepdims=True)
        gg_ref[2 * t + 1 : 2 * t + 2, :] = jnp.sum(d_z, 0, keepdims=True)
        d_hat = d_z * gains_ref[2 * t : 2 * t + 1, :]
        inner = d_hat - jnp.mean(d_hat, -1, keepdims=True)
        rows = inverse * (inner - hat * jnp.mean(d_hat * hat, -1, keepdims=True))
        out[...] = rows * scales[t] if t < 2 else rows / count_ref[...]
    z_ref[0] = z[0]
    z_ref[1] = z[1]
    zt_ref[...] = z[2]
    de_ref[0] = d_video
    de_ref[1] = d_audio
    dt_e_ref[...] = d_text
    ev_ref[...] = e_video
    dvt_ref[...] = d_both
    for k in range(2 + captions):
        if k < 2:
            rows = (dv_ref, da_ref)[k][own_group, :]
        else:
            begin = pl.multiple_of((k - 2) * clips + replica * group, group)
            rows = dt_ref[pl.ds(begin, group), :]
        x4_ref[:, k, :part] = times(rows.astype(BF16).astype(F32), backs_ref[min(k, 2)], right)
    r4_ref[member] = x4_ref[member]
    exchange(3, group, near, lambda peer: x4_ref.at[peer], r4_ref.at[member])
    for at in range(group):
        slope_ref[:, at * part : (at + 1) * part] = r4_ref[at, :, :part]


def contrast(scales, captions, sums, bases, token_scales, backs, gains, heads, video_text, *masks):
    group = lax.axis_size("fsdp")
    clips = lax.axis_size("dp") * group
    features = bases.shape[1]
    texts = captions * clips
    joint, width = video_text.shape
    part = backs.shape[1]
    padded = part + -part % 128
    shapes = [
        (8, 128),
        (clips, features),
        (clips, features),
        (texts, features),
        (8, features),
        (2, clips, features),
        (texts, features),
        (2, clips, joint),
        (texts, width),
        (clips, joint),
        (clips, width),
        (clips, 8, padded),
        (8, part * group),
    ]
    return pl.pallas_call(
        functools.partial(middle_kernel, scales, captions),
        out_shape=tuple(jax.ShapeDtypeStruct(shape, F32) for shape in shapes),
        in_specs=[pl.BlockSpec(memory_space=pltpu.VMEM)] * 10,
        out_specs=tuple(pl.BlockSpec(memory_space=pltpu.VMEM) for _ in shapes),
        scratch_shapes=[
            pltpu.VMEM((group, 8, padded), F32),
            pltpu.VMEM((group, 8, features), F32),
            pltpu.VMEM((group, 8, features), F32),
            pltpu.VMEM((8, features), F32),
            pltpu.VMEM((clips, 8, features), F32),
            pltpu.VMEM((group, 8, padded), F32),
            pltpu.VMEM((group, 8, padded), F32),
            pltpu.SemaphoreType.DMA((4, clips)),
            pltpu.SemaphoreType.DMA((4, clips)),
        ],
        compiler_params=pltpu.CompilerParams(
            vmem_limit_bytes=VMEM_LIMIT, collective_id=1, has_side_effects=True
        ),
        name="middle",
    )(sums, bases, token_scales, backs, gains, heads, video_text, *masks)


def feed_kernel(with_product, h_ref, w_ref, sel_ref, slope_ref, sums_ref, *rest):
    hidden = dot(h_ref[...], w_ref[...])
    root = 0.7978845608028654
    square = hidden * hidden
    tang = jnp.tanh(root * hidden * (1.0 + 0.044715 * square))
    half = 0.5 * (1.0 + tang)
    active = (hidden * half).astype(BF16)
    slope = half + (0.5 * root) * hidden * (1.0 - tang * tang) * (1.0 + (3 * 0.044715) * square)
    slope = slope.astype(BF16)
    slope_ref[...] = slope
    if with_product:
        sums_ref[...] = jnp.broadcast_to(
            jnp.sum(active.astype(F32), 0, keepdims=True), sums_ref.shape
        )
        rest[0][...] = dot_tn(h_ref[...], slope).astype(BF16)
    else:
        sums_ref[...] = dot(sel_ref[...], active)


def feed(normed, weight, column, select, tile, with_product):
    rows, features = normed.shape
    width = weight.shape[1] - column
    first = column // tile
    shapes = [
        jax.ShapeDtypeStruct((rows, width), BF16),
        jax.ShapeDtypeStruct((8, width), F32),
    ]
    outs = [
        pl.BlockSpec((rows, tile), lambda j: (0, j)),
        pl.BlockSpec((8, tile), lambda j: (0, j)),
    ]
    if with_product:
        shapes.append(jax.ShapeDtypeStruct((features, width), BF16))
        outs.append(pl.BlockSpec((features, tile), lambda j: (0, j)))
    return pl.pallas_call(
        functools.partial(feed_kernel, with_product),
        grid=(width // tile,),
        out_shape=tuple(shapes),
        in_specs=[
            pl.BlockSpec((rows, features), lambda j: (0, 0)),
            pl.BlockSpec((features, tile), lambda j: (0, first + j)),
            pl.BlockSpec(select.shape, lambda j: (0, 0)),
        ],
        out_specs=tuple(outs),
        compiler_params=pltpu.CompilerParams(vmem_limit_bytes=VMEM_LIMIT),
        cost_estimate=pl.CostEstimate(
            flops=rows * features * width // 8,
            bytes_accessed=rows * width,
            transcendentals=0,
        ),
        name=f"feed_{rows}",
    )(normed, weight, select)


def both_columns(own, other, core):
    first = jnp.where(core == 0, own, other)
    second = jnp.where(core == 0, other, own)
    return jnp.concatenate([first, second], -1)


def attention_forward(stream, bias, mixing, gains, block):
    features = stream.shape[1]
    normed = norm_rows(stream, gains[0], gains[1]).astype(BF16)
    joined = dot(normed, mixing[:, : 3 * features]).astype(BF16)
    return normed, joined, attend(joined, bias, block)


def feed_forward(stream, mixed, mixing, upper, column, gains, select, with_product):
    features = stream.shape[1]
    middle = stream + dot(mixed, mixing[:, 3 * features : 4 * features])
    normed = norm_rows(middle, gains[2], gains[3]).astype(BF16)
    return middle, normed, feed(normed, upper, column, select, 512, with_product)


def output_backward(grad_rows, grad_normed, mixed, middle, mixing, gains):
    features = middle.shape[1]
    grad_norm, grad_gain, grad_shift = jax.vjp(norm_rows, middle, gains[2], gains[3])[1](
        grad_normed
    )
    grad_middle = grad_rows + grad_norm
    grad_attention = grad_middle.astype(BF16)
    grad_mixed = dot_nt(grad_attention, mixing[:, 3 * features : 4 * features]).astype(BF16)
    grad_output = dot_tn(mixed, grad_attention).astype(BF16)
    return grad_middle, grad_output, grad_mixed, [grad_gain, grad_shift]


def input_backward(grad_middle, grad_joined, stream, mixing, gains):
    features = stream.shape[1]
    grad_normed = dot_nt(grad_joined, mixing[:, : 3 * features])
    grad_norm, grad_gain, grad_shift = jax.vjp(norm_rows, stream, gains[0], gains[1])[1](
        grad_normed
    )
    return (grad_middle + grad_norm).astype(BF16), [grad_gain, grad_shift]


def both_columns(own, other, core):
    first = jnp.where(core == 0, own, other)
    second = jnp.where(core == 0, other, own)
    return jnp.concatenate([first, second], -1)


class Links:
    def __init__(self):
        self.group = lax.axis_size("fsdp")
        self.replicas = lax.axis_size("dp")
        self.member = lax.axis_index("fsdp")
        self.replica = lax.axis_index("dp")
        self.core = self.member % 2
        self.paired = self.group == 16 and self.replicas == 2
        self.carried = []

    def swap(self, values, name):
        if name == "y":
            return lax.ppermute(values, "dp", [(0, 1), (1, 0)])
        if name == "corner":
            count = 2 * self.group
            pairs = [(f, (f + self.group) % count ^ 1) for f in range(count)]
            return lax.ppermute(values, ("dp", "fsdp"), pairs)
        bit = {"core": 1, "x": 2, "near": 4, "far": 8, "across": 12}[name]
        return lax.ppermute(values, "fsdp", [(f, f ^ bit) for f in range(self.group)])

    def bit(self, name):
        if name == "y":
            return self.replica
        return (self.member // {"core": 1, "x": 2, "near": 4, "far": 8}[name]) % 2

    def merge(self, values, other, names, name, order=("far", "near", "x", "core", "y")):
        names = sorted(names + [name], key=order.index)
        at = names.index(name)
        place = lax.broadcasted_iota(jnp.int32, (2,) + (1,) * (values.ndim - at), 0)
        joined = jnp.where(
            place == self.bit(name), jnp.expand_dims(values, at), jnp.expand_dims(other, at)
        )
        return joined, names

    def sides(self, values, names, name):
        at = names.index(name)
        bit = self.bit(name)
        give = lax.dynamic_index_in_dim(values, 1 - bit, at, keepdims=False)
        keep = lax.dynamic_index_in_dim(values, bit, at, keepdims=False)
        return keep, give, [n for n in names if n != name]

    def spread(self, values):
        for name in ("core", "x", "near", "far"):
            other = yield values, name
            values = jnp.where(self.bit(name) == 1, values, other)
        return values

    def gather_clips(self, values):
        if not self.paired:
            return lax.all_gather(values, ("dp", "fsdp"), axis=0, tiled=True)
        names = []
        order = ["y", "far", "near", "x", "core"]
        one, two, three = yield [(values, "near"), (values, "far"), (values, "across")]
        values, _ = self.merge(values, one, [], "near", order)
        others, names = self.merge(two, three, [], "near", order)
        values, names = self.merge(values, others, names, "far", order)
        for name in ("y", "x", "core"):
            other = yield values, name
            values, names = self.merge(values, other, names, name, order)
        return values.reshape(-1, values.shape[-1])

    def sum_replicas(self, part):
        if not self.paired:
            return lax.psum(part, "dp").astype(F32)
        other = yield part, "y"
        return part.astype(F32) + other.astype(F32)

    def gather_rows(self, shard, order):
        rows, width = shard.shape
        half = width // 2
        if not self.paired:
            return lax.all_gather(shard, "fsdp", axis=0, tiled=True)
        values = lax.dynamic_slice_in_dim(shard, self.replica * half, half, 1)
        names = []
        for name in order + ("core",):
            other = yield values, name
            if name == "y":
                values = both_columns(values, other, self.replica)
            else:
                values, names = self.merge(values, other, names, name)
        return values.reshape(self.group * rows, width)

    def reduce_line(self, values):
        far, near = self.bit("far"), self.bit("near")

        def part(at_far, at_near):
            begin = (at_far, at_near) + (0,) * (values.ndim - 2)
            return lax.dynamic_slice(values, begin, (1, 1) + values.shape[2:])[0, 0]

        others = yield [
            (part(far, 1 - near), "near"),
            (part(1 - far, near), "far"),
            (part(1 - far, 1 - near), "across"),
        ]
        total = part(far, near).astype(F32)
        for other in others:
            total = total + other.astype(F32)
        return total.astype(BF16)

    def reduce_columns(self, own, other, order):
        rows, half = own.shape
        part = rows // self.group
        if not self.paired:
            whole = both_columns(own, other, self.core)
            whole = lax.psum_scatter(whole, "fsdp", scatter_dimension=0, tiled=True)
            return lax.psum(whole, "dp")
        other = yield other, "core"
        values = add(own, other).reshape(2, 2, 2, 2, 2, part // 2, half)
        names = ["far", "near", "x", "core", "y"]
        for name in order:
            keep, give, names = self.sides(values, names, name)
            other = yield give, name
            values = add(keep, other)
        return (yield from self.reduce_line(values))

    def scatter_columns(self, own, other, order):
        values = yield from self.reduce_columns(own, other, order)
        if not self.paired:
            return values.astype(F32)
        mine, give, _ = self.sides(values, ["core"], "core")
        beside, across, corner = yield [(give, "core"), (mine, "y"), (give, "corner")]
        near = both_columns(mine, beside, self.core)
        far = both_columns(across, corner, self.core)
        values, _ = self.merge(near, far, [], "y")
        return values.reshape(2 * values.shape[1], values.shape[2]).astype(F32)

    def scatter_rows(self, values, order):
        rows, width = values.shape
        part = rows // self.group
        half = width // 2
        if not self.paired:
            part_sum = lax.psum_scatter(values, "fsdp", scatter_dimension=0, tiled=True)
            return lax.psum(part_sum, "dp").astype(F32)
        values = values.reshape(2, 2, 2, 2, part, width)
        names = ["far", "near", "x", "core"]
        for name in ("core",) + order:
            if name == "y":
                last = values.ndim - 1
                give = lax.dynamic_slice_in_dim(values, (1 - self.replica) * half, half, last)
                keep = lax.dynamic_slice_in_dim(values, self.replica * half, half, last)
            else:
                keep, give, names = self.sides(values, names, name)
            other = yield give, name
            values = add(keep, other)
        values = yield from self.reduce_line(values)
        other = yield values, "y"
        return both_columns(values, other, self.replica).astype(F32)

    def scatter_words(self, values):
        rows, width = values.shape
        if not self.paired:
            return lax.psum_scatter(values, "fsdp", scatter_dimension=0, tiled=True)
        values = values.reshape(2, 2, 2, 2, rows // self.group, width)
        names = ["far", "near", "x", "core"]
        for name in ("core", "x", "far", "near"):
            keep, give, names = self.sides(values, names, name)
            other = yield give, name
            values = add(keep, other)
        return values

    def stage(self, flows, work=None, inputs=(), slow=()):
        slow = [flow for flow in slow if flow.request is not None]
        active = [flow for flow in flows if flow.request is not None]
        every = active + slow
        asked = [flow.request if isinstance(flow.request, list) else [flow.request] for flow in every]
        held = [[values for values, _ in asks] for asks in asked]
        held, inputs = lax.optimization_barrier((held, inputs))
        sent = [
            [self.swap(values, name) for values, (_, name) in zip(group, asks)]
            for group, asks in zip(held, asked)
        ]
        ending = list(zip(active, sent)) + self.carried
        self.carried = list(zip(slow, sent[len(active) :]))
        made = work(*inputs) if work is not None else ()
        received, made = lax.optimization_barrier(([others for _, others in ending], made))
        for (flow, _), others in zip(ending, received):
            flow.push(others if isinstance(flow.request, list) else others[0])
        return made


class Flow:
    def __init__(self, steps):
        self.steps = steps
        self.value = None
        self.push(None)

    def push(self, other):
        try:
            self.request = self.steps.send(other)
        except StopIteration as end:
            self.request, self.value = None, end.value


def add(left, right):
    return (left.astype(F32) + right.astype(F32)).astype(BF16)


def body(
    video,
    audio,
    word_ids,
    word_counts,
    caption_counts,
    caption_clips,
    mixing_in,
    mixing_in_first,
    mixing_in_second,
    mixing_out,
    mixing_out_first,
    mixing_out_second,
    norm_params,
    norm_params_first,
    norm_params_second,
    input_embed,
    input_embed_first,
    input_embed_second,
    word_table,
    word_table_first,
    word_table_second,
    head_proj,
    head_proj_first,
    head_proj_second,
    video_text_proj,
    video_text_proj_first,
    video_text_proj_second,
):
    group = lax.axis_size("fsdp")
    replicas = lax.axis_size("dp")
    clips = group * replicas
    member = lax.axis_index("fsdp")
    replica = lax.axis_index("dp")
    clip = replica * group + member
    captions, slots = word_ids.shape[1:]
    words = captions * slots
    patch = video.shape[2]
    video_count, audio_count = video.shape[1], audio.shape[1]
    features = mixing_in.shape[1] * group
    pairs = features // 128
    shard = mixing_in.shape[1]
    qkv = 3 * features

    links = Links()
    core = links.core
    half = features // 2
    joint_part, text_width = video_text_proj.shape
    table_rows = word_table.shape[0]
    gain_part = norm_params.shape[2]
    wave = audio.shape[2]
    low = regroup(mixing_in, features)

    def gather(values):
        return lax.all_gather(values, "fsdp", axis=0, tiled=True)

    weights = [None] * 3
    weights[1] = gather(low[1])
    def exchange(*parts):
        packed = jnp.concatenate([part.reshape(-1).astype(F32) for part in parts])
        packed = jnp.pad(packed, (0, -packed.shape[0] % 1024)).reshape(-1, 128)
        return everyone(packed, 0).reshape(clips, -1)

    embed_low = input_embed.astype(BF16)
    embed_flow = Flow(links.gather_rows(embed_low, ("near", "far", "x", "y")))
    wave_flow = Flow(links.spread(embed_low[-wave:])) if links.paired else embed_flow
    every = links.stage(
        [embed_flow, wave_flow],
        exchange,
        (word_ids, word_counts, caption_counts, caption_clips, norm_params),
    )

    def owned_rows(ids):
        local_ids = ids - member * table_rows
        owned = (local_ids >= 0) & (local_ids < table_rows)
        return jnp.clip(local_ids, 0, table_rows - 1), owned

    def pick_words(every):
        ids = every[:, :words].astype(jnp.int32)
        group_ids = lax.dynamic_slice_in_dim(ids, replica * group, group, 0).reshape(-1)
        local_ids, owned = owned_rows(group_ids)
        return jnp.where(owned[:, None], word_table[local_ids], 0.0).astype(BF16)

    picked = links.stage([embed_flow, wave_flow], pick_words, (every,))
    words_flow = Flow(links.scatter_words(picked))

    def prepare(every):
        local_ids = owned_rows(every[:, :words].astype(jnp.int32).reshape(-1))
        at = words + captions
        live = jnp.arange(captions)[:, None] < every[:, at].astype(jnp.int32)[None, :]
        live = live.reshape(1, -1)
        counts = every[:, words : words + captions].T.reshape(-1, 1)
        owners = every[:, at + 1 : at + 1 + captions].astype(jnp.int32).T.reshape(1, -1)
        positive = live & (owners == jnp.arange(clips)[:, None])
        at = at + 1 + captions
        gains_all = (
            every[:group, at : at + 18 * gain_part]
            .reshape(group, 3, 6, gain_part)
            .transpose(1, 2, 0, 3)
            .reshape(3, 6, features)
            .astype(BF16)
            .astype(F32)
        )
        outer_rows = jnp.pad(gains_all[:, 4:].reshape(6, features), ((0, 2), (0, 0)))
        masks = (live.astype(F32), positive.astype(F32), counts)
        valid = (jnp.arange(slots)[None, :] < word_counts[0][:, None]).reshape(-1)
        caption_of = jnp.arange(words) // slots
        allowed = (caption_of[:, None] == caption_of[None, :]) & valid[None, :]
        word_bias = jnp.where(allowed, 0.0, -1000000000.0).astype(F32)
        select = ((jnp.arange(8)[:, None] == caption_of[None, :]) & valid[None, :]).astype(BF16)
        own_counts = word_counts[0].astype(F32)
        sizes = jnp.array([video_count, audio_count], F32)
        scales = 1.0 / jnp.concatenate([sizes, own_counts, jnp.ones(6 - captions, F32)])
        heads_low = jnp.concatenate(
            [head_proj, jnp.pad(video_text_proj, ((0, shard - joint_part), (0, 0)))], 1
        ).astype(BF16)
        backs = mixing_out.astype(BF16).astype(F32)
        return (
            gains_all,
            outer_rows,
            masks,
            (word_bias, word_bias.T, select),
            scales[:, None],
            heads_low,
            backs,
            local_ids,
        )

    (
        gains_all,
        outer_rows,
        masks,
        (word_bias, turned_bias, select),
        token_scales,
        heads_low,
        backs,
        (local_ids, owned),
    ) = links.stage([embed_flow, wave_flow], prepare, (every,))
    unused = jnp.zeros((8, 128), BF16)
    biases = (None, None, word_bias)
    turned_biases = (None, None, turned_bias)
    selects = (unused, unused, select)
    forward_block = (512, 512, words)
    backward_block = (512, 256, words)
    normed, joined, attended, fed, streams = ([None] * 3 for _ in range(5))
    links.stage([wave_flow])
    wave_rows = wave_flow.value
    if not links.paired:
        wave_rows = wave_rows[patch:]
    streams[1] = dot(audio[0], wave_rows)

    def attention(tower, stream, mixing):
        return attention_forward(
            stream, biases[tower], mixing, gains_all[tower], forward_block[tower]
        )

    def feeding(tower, stream, mixed, mixing, upper, column):
        return feed_forward(
            stream, mixed, mixing, upper, column, gains_all[tower], selects[tower], tower < 2
        )

    streams, weights[1], low_video, low_text = lax.optimization_barrier(
        (streams, weights[1], low[0], low[2, :, : 4 * features])
    )
    weights[0] = gather(low_video)
    weights[2] = gather(low_text)
    upper_flow = Flow(links.gather_rows(low[2, :, 4 * features :], ("near", "far", "x", "y")))
    normed[1], joined[1], attended[1] = links.stage(
        [embed_flow, words_flow, upper_flow],
        lambda stream, mixing: attention(1, stream, mixing),
        (streams[1], weights[1]),
    )
    fed[1] = links.stage(
        [embed_flow, words_flow, upper_flow],
        lambda mixed: feeding(1, streams[1], mixed, weights[1], weights[1], 4 * features),
        (attended[1][0],),
    )
    embed = embed_flow.value
    fed[1], weights[0], embed = lax.optimization_barrier((fed[1], weights[0], embed))

    def video_attention(rows, mixing):
        stream = dot(video[0], rows)
        return stream, attention(0, stream, mixing)

    streams[0], (normed[0], joined[0], attended[0]) = links.stage(
        [words_flow, upper_flow], video_attention, (embed[:patch], weights[0])
    )
    fed[0] = links.stage(
        [words_flow, upper_flow],
        lambda mixed: feeding(0, streams[0], mixed, weights[0], weights[0], 4 * features),
        (attended[0][0],),
    )
    links.stage([upper_flow])
    streams[2] = words_flow.value.astype(F32)
    text_upper = upper_flow.value
    text_upper, weights[2], heads_low = lax.optimization_barrier(
        (text_upper, weights[2], heads_low)
    )
    heads_all = gather(heads_low)
    normed[2], joined[2], attended[2] = attention(2, streams[2], weights[2])
    fed[2] = feeding(2, streams[2], attended[2][0], weights[2], text_upper, 0)
    uppers = (weights[0][:, 4 * features :], weights[1][:, 4 * features :], text_upper)

    heads = heads_all[:, : head_proj.shape[1]]
    video_text = heads_all[:, head_proj.shape[1] :].reshape(group, shard, text_width)
    video_text = video_text[:, :joint_part].reshape(group * joint_part, text_width)
    slopes = [fed[t][2][0] for t in range(3)]
    products = [fed[t][2][2] for t in range(2)]
    row_sums = [fed[t][2][1] for t in range(3)]
    token_count = 2 + captions
    summed = jnp.concatenate(
        [row_sums[0][:1], row_sums[1][:1], row_sums[2][: 8 - 2]], 0
    )
    bases = jnp.concatenate(
        [
            jnp.sum(fed[0][0], 0, keepdims=True),
            jnp.sum(fed[1][0], 0, keepdims=True),
            full(select[: 8 - 2].astype(F32), fed[2][0]),
        ],
        0,
    )
    (
        loss,
        *grad_rows_all,
        outer_grads,
        z_pair,
        z_text,
        d_pair,
        d_text,
        embed_video,
        d_video_text,
        every_sum,
        sloped,
    ) = contrast(
        (1.0 / video_count, 1.0 / audio_count),
        captions,
        summed,
        bases,
        token_scales,
        backs,
        outer_rows,
        heads,
        video_text,
        *masks,
    )
    loss = loss[0, 0]
    z = (z_pair[0], z_pair[1], z_text)
    d_heads = (d_pair[0], d_pair[1], d_text)

    def own_columns(values):
        return lax.dynamic_slice_in_dim(values, member * shard, shard, 1)

    def head_grads():
        heads_grad = jnp.concatenate([full(own_columns(z[t]).T, d_heads[t]) for t in range(3)], 1)
        own = lax.dynamic_slice_in_dim(embed_video, member * joint_part, joint_part, 1)
        return heads_grad, full(own.T, d_video_text)

    branch_all = [rows.astype(BF16) for rows in grad_rows_all]

    back_part = mixing_out.shape[1]

    def back_grads():
        own = every_sum[:, :, :back_part].transpose(1, 0, 2)
        own = (own[0], own[1], own[2:token_count].reshape(-1, back_part))
        return jnp.stack([full(own[t].T, branch_all[t].astype(F32)) for t in range(3)])

    own_grads = [
        lax.dynamic_slice_in_dim(grad_rows_all[0], clip, 1, 0),
        lax.dynamic_slice_in_dim(grad_rows_all[1], clip, 1, 0),
        lax.dynamic_slice_in_dim(
            grad_rows_all[2].reshape(captions, clips, features), clip, 1, 1
        ).reshape(captions, features),
    ]
    own_slopes = (sloped[:1], sloped[1:2], sloped[2:token_count])
    ups = scale_columns(products[1], products[0], jnp.concatenate(own_slopes[1::-1], 0))
    ups, own_slopes = lax.optimization_barrier((ups, own_slopes))
    up_part = lax.psum_scatter(ups, "fsdp", scatter_dimension=0, tiled=True)
    first, second = ("y", "x"), ("x", "y")

    def hidden_backward(tower, slope):
        upper = uppers[tower]
        if tower == 2:
            spread = select[:captions].astype(F32).T
            grad_hidden = (slopes[2].astype(F32) * full(spread, slope)).astype(BF16)
            up = dot_tn(fed[2][1], grad_hidden).astype(BF16)
            return full(spread, own_grads[2]), dot_nt(grad_hidden, upper), up
        scaled = (upper.astype(F32) * slope).astype(BF16)
        return own_grads[tower], dot_nt(slopes[tower], scaled), None

    def outward_backward(tower, slope):
        rows_grad, grads, up = hidden_backward(tower, slope)
        made = output_backward(
            rows_grad, grads, attended[tower][0], fed[tower][0], weights[tower], gains_all[tower]
        )
        return made, up

    def inner_backward(tower, grad_mixed):
        return attend_back(
            joined[tower],
            grad_mixed,
            attended[tower][0],
            attended[tower][1],
            turned_biases[tower],
            backward_block[tower],
        )

    def entry_backward(tower, grad_middle, grad_joined):
        return input_backward(
            grad_middle, grad_joined, streams[tower], weights[tower], gains_all[tower]
        )

    gains_grads = [None] * 3

    def text_backward(slope):
        made, up = outward_backward(2, slope)
        grad_joined = inner_backward(2, made[2])
        inward = dot_tn(normed[2], grad_joined).astype(BF16)
        entry, entry_gains = entry_backward(2, made[0], grad_joined)
        return (inward, made[1], up), entry, entry_gains + made[3]

    text_grad, entry, gains_grads[2] = links.stage([], text_backward, (own_slopes[2],))
    word_flow = Flow(links.gather_clips(entry))
    made_video, _ = links.stage(
        [word_flow], lambda slope: outward_backward(0, slope), (own_slopes[0],)
    )
    embed_rows = input_embed.shape[0] * group

    def video_inner(grad_mixed):
        grad_joined = inner_backward(0, grad_mixed)
        inward = dot_tn(normed[0], grad_joined).astype(BF16)
        entry, entry_gains = entry_backward(0, made_video[0], grad_joined)
        return jnp.concatenate([*text_grad, inward, made_video[1]], 1), entry, entry_gains

    pair_grad, entry, entry_gains = links.stage([word_flow], video_inner, (made_video[2],))
    gains_grads[0] = entry_gains + made_video[3]
    pair_part = lax.psum_scatter(pair_grad, "fsdp", scatter_dimension=0, tiled=True)

    def video_entry(entry, slope):
        made, _ = outward_backward(1, slope)
        return patch_grads(video, entry, embed_rows), made

    grad_embed, made_audio = links.stage(
        [], video_entry, (entry, own_slopes[1]), [word_flow]
    )
    embed_flow = Flow(links.scatter_rows(grad_embed, ("y", "x")))

    def audio_pairs(grad_mixed, *bounds):
        return attend_back(
            joined[1],
            grad_mixed,
            attended[1][0],
            attended[1][1],
            None,
            backward_block[1],
            *bounds,
        )

    first_pairs = links.stage(
        [embed_flow], lambda part: audio_pairs(part, 0, pairs // 2), (made_audio[2],)
    )

    def audio_inner(grad_mixed, first_pairs):
        grad_joined = audio_pairs(grad_mixed, pairs // 2, pairs, first_pairs)
        inward = dot_tn(normed[1], grad_joined).astype(BF16)
        sides = [
            jnp.concatenate(
                [
                    lax.dynamic_slice_in_dim(inward, at * 3 * half, 3 * half, 1),
                    lax.dynamic_slice_in_dim(made_audio[1], at * half, half, 1),
                ],
                1,
            )
            for at in (core, 1 - core)
        ]
        return grad_joined, sides

    joined_audio, audio_sides = links.stage(
        [embed_flow, word_flow], audio_inner, (made_audio[2], first_pairs)
    )
    audio_flow = Flow(links.scatter_columns(*audio_sides, ("y", "x")))

    def scatter_table(every_word):
        return jax.ops.segment_sum(
            jnp.where(owned[:, None], every_word.astype(F32), 0.0),
            local_ids,
            num_segments=table_rows,
        )

    def squared(*values):
        return sum(jnp.sum(value * value) for value in values)

    def audio_entry(grad_joined):
        entry, entry_gains = entry_backward(1, made_audio[0], grad_joined)
        wave_grad = dot_tn(entry, audio[0]).astype(BF16)
        every_gain = jnp.stack(gains_grads[0] + entry_gains + made_audio[3] + gains_grads[2])
        every_gain = jnp.pad(every_gain, ((0, wave - every_gain.shape[0]), (0, 0)))
        gain_columns = every_gain.T.astype(BF16)
        return (
            jnp.where(core == 0, wave_grad, gain_columns),
            jnp.where(core == 0, gain_columns, wave_grad),
        )

    up_flow = Flow(links.sum_replicas(up_part))
    beside = links.stage([audio_flow], audio_entry, (joined_audio,), [embed_flow, up_flow])
    beside_flow = Flow(links.reduce_columns(*beside, ("y", "x")))
    rest = [audio_flow, beside_flow]
    table_grad = links.stage(rest, scatter_table, (word_flow.value,))
    back_grad, (heads_grad, video_text_grad), table_square = links.stage(
        rest,
        lambda table, up: (back_grads(), head_grads(), squared(table, up)),
        (table_grad, up_flow.value),
        [embed_flow],
    )
    pair_flow = Flow(links.sum_replicas(pair_part))
    small_square = links.stage(
        rest + [pair_flow], squared, (back_grad, heads_grad, video_text_grad)
    )
    small_square = small_square + links.stage(rest + [embed_flow], squared, (pair_flow.value,))
    pieces = (up_flow.value, pair_flow.value, audio_flow.value)
    embed_grad = embed_flow.value

    outer = lax.dynamic_slice_in_dim(outer_grads[:6], member * gain_part, gain_part, 1)
    local_square = table_square + small_square + squared(pieces[2], embed_grad, outer)
    piece = beside_flow.value.reshape(-1, wave)
    piece_square = squared(piece.astype(F32))
    marks = jnp.where(jnp.arange(128) < 64, local_square, piece_square)
    mark_rows = []
    for _ in range(3):
        mark_rows.append(marks.astype(BF16))
        marks = marks - mark_rows[-1].astype(F32)
    mark_rows = jnp.pad(jnp.stack(mark_rows), ((0, 16 - 3 + -piece.shape[0] % 16), (0, 0)))
    sent = everyone(jnp.concatenate([piece, mark_rows], 0), 2).astype(F32)
    marks = jnp.sum(sent[:, piece.shape[0] : piece.shape[0] + 3], 1)
    sent = sent[:, : piece.shape[0]]
    if links.paired:
        square = jnp.sum(marks[:group, 0]) + jnp.sum(marks[:, 127])
        placed = sent.reshape(replicas, group // 2, 2, 2, gain_part // 2, wave)
        placed = placed.transpose(2, 1, 3, 0, 4, 5).reshape(2, features, wave)
    else:
        square = jnp.sum(marks[:group, 0]) + jnp.sum(marks[:group, 127])
        placed = sent[:group].reshape(group, gain_part, 2, wave)
        placed = placed.transpose(2, 0, 1, 3).reshape(2, features, wave)
    wave_rows, gain_rows = placed[0].T, placed[1].T
    embed_part = input_embed.shape[0]
    row = member * embed_part + jnp.arange(embed_part) - patch
    chosen = (row[:, None] == jnp.arange(wave)[None, :]).astype(F32)
    inner = lax.dynamic_slice_in_dim(gain_rows[:12], member * gain_part, gain_part, 1)
    gains_grad = jnp.concatenate(
        [inner.reshape(3, 4, gain_part), outer.reshape(3, 2, gain_part)], 1
    )
    grads = (
        None,
        back_grad,
        gains_grad,
        embed_grad + full(chosen, wave_rows),
        table_grad,
        heads_grad,
        video_text_grad,
    )
    grad_norm = jnp.sqrt(square)
    factor = CLIP_NORM / jnp.maximum(grad_norm, CLIP_NORM)
    clipped = [None] + [g * factor for g in grads[1:]]
    masters = (
        mixing_in,
        mixing_out,
        norm_params,
        input_embed,
        word_table,
        head_proj,
        video_text_proj,
    )
    firsts = (
        mixing_in_first,
        mixing_out_first,
        norm_params_first,
        input_embed_first,
        word_table_first,
        head_proj_first,
        video_text_proj_first,
    )
    seconds = (
        mixing_in_second,
        mixing_out_second,
        norm_params_second,
        input_embed_second,
        word_table_second,
        head_proj_second,
        video_text_proj_second,
    )
    new = [
        adam_mixing(
            factor,
            pieces,
            mixing_in,
            mixing_in_first,
            mixing_in_second,
            features,
        )
    ]
    for i in range(1, 7):
        new.append(adam_update(masters[i], firsts[i], seconds[i], clipped[i], RATES[i]))
    outputs = [loss, grad_norm]
    for i in range(7):
        outputs += [new[i][0], clipped[4] if i == 4 else new[i][1], new[i][2]]
    return tuple(outputs)


def solution(mesh):
    both = ("dp", "fsdp")
    weight_specs = (
        P(None, "fsdp", None),
        P(None, "fsdp", None),
        P(None, None, "fsdp"),
        P("fsdp", None),
        P("fsdp", None),
        P("fsdp", None),
        P("fsdp", None),
    )
    tripled = tuple(spec for spec in weight_specs for _ in range(3))
    return jax.shard_map(
        body,
        mesh=mesh,
        in_specs=(
            P(both, None, None),
            P(both, None, None),
            P(both, None, None),
            P(both, None),
            P(both),
            P(both, None),
        )
        + tripled,
        out_specs=(P(), P()) + tripled,
        check_vma=False,
    )
```
